128 devices in a mesh: pole: 8 (over x, y_lo), grid: 16 (over z, y_hi, core).
Axes of the slice: x: 4, y: 4 (y_hi: 2, y_lo: 2; y = y_hi * 2 + y_lo), z: 4, core: 2. Of those that a mesh axis runs over, the one named last changes fastest.
Arguments:
- hamiltonian: float32 [2048, 2048], P(('pole', 'grid')), may hold values from -6 to 6, as said below
- margin: float32 [2048, 2048], P(('pole', 'grid')), may hold values from -1 to 1.2, as said below
- pattern: int32 [4, 4], replicated, may hold values 0 or 1
- shift_real: float32 [8], P('pole'), may hold values from -0.5 to 0.5
- shift_imag: float32 [8], P('pole'), may hold values from 0.3 to 3
- residue: float32 [8, 2], P('pole'), may hold values from -4 to 4
Outputs:
- density: float32 [2048, 2048], P(('pole', 'grid'))
The draws below stay inside these ranges and needn't reach their ends.
Inputs may be any that keep to these rules, and one draw needn't show every extreme that they name: `hamiltonian`: symmetric. `margin`: symmetric.
All inputs are finite; a program needn't handle non-finite values.
Results may differ from the reference program's by a relative error of at most 0.0003.
Values sent between devices are 32-bit elements; how exact they have to be, the bound alone decides.
A program may use at most 320 MiB of HBM per device.

```python
import math
import jax
import jax.numpy as jnp
from jax import lax

SUPER = 256
NC = 2
NR = 4
C = 512
R = 1024
N = 2048
POLES = 8


def draw_hamiltonian(key, part):
    key_off, key_mag, key_sign = jax.random.split(jax.random.fold_in(key, 101), 3)
    spread = jax.random.normal(key_off, (N, N), jnp.float32)
    spread = (spread + spread.T) * (1.4 / math.sqrt(2.0 * N))
    magnitude = jax.random.uniform(key_mag, (N,), jnp.float32, 3.0, 6.0)
    signs = jnp.where(jax.random.bernoulli(key_sign, 0.5, (N,)), 1.0, -1.0)
    eye = jnp.eye(N, dtype=jnp.float32)
    return spread * (1.0 - eye) + jnp.diag(magnitude * signs)


def draw_margin(key, part):
    key_off, key_mag = jax.random.split(jax.random.fold_in(key, 202), 2)
    spread = jax.random.normal(key_off, (N, N), jnp.float32)
    spread = (spread + spread.T) * (0.3 / math.sqrt(2.0 * N))
    spread = jnp.clip(spread, -0.9, 0.9)
    magnitude = jax.random.uniform(key_mag, (N,), jnp.float32, 0.8, 1.2)
    eye = jnp.eye(N, dtype=jnp.float32)
    return spread * (1.0 - eye) + jnp.diag(magnitude)


def touch_ends(drawn, key, smallest, top_value):
    extent = drawn.shape
    spot = [jax.random.randint(jax.random.fold_in(key, axis), (), 0, extent[axis]) for axis in range(len(extent))]
    drawn = drawn.at[tuple(spot)].set(smallest)
    longest = extent.index(max(extent))
    spot[longest] = (spot[longest] + 1) % extent[longest]
    return drawn.at[tuple(spot)].set(top_value)


def block_scale(rng, shape, shards, low, largest):
    loudness = 1.0
    for axis_at, shards_of in shards:
        heights = jax.random.uniform(jax.random.fold_in(jax.random.fold_in(rng, 6), axis_at), (shards_of,), jnp.float32, low / len(shards), largest / len(shards))
        loudness = loudness * jnp.repeat(jnp.exp(heights), shape[axis_at] // shards_of).reshape((-1,) + (1,) * (len(shape) - 1 - axis_at))
    return loudness


def normal_values(rng, shape, scale, most, cuts=(), kind=jnp.bfloat16):
    entries = scale * jax.random.normal(rng, shape, jnp.float32)
    if cuts:
        entries = entries * block_scale(rng, shape, cuts, -0.22, 0.18)
    return jnp.clip(entries, -most, most).astype(kind)


def setup_inputs(seed: int = 0) -> dict:
    keys = jax.random.split(jax.random.key(seed), 7)
    return {
        "hamiltonian": draw_hamiltonian(jax.random.fold_in(keys[6], 71), 0),
        "margin": draw_margin(jax.random.fold_in(keys[6], 71), 0),
        "pattern": touch_ends((jax.random.randint(keys[2], (NR, 2 * NC), 0, 4) < 3).astype(jnp.int32), jax.random.fold_in(keys[2], 1), 0, 1),
        "shift_real": jnp.clip(jax.random.uniform(keys[3], (POLES,), jnp.float32, -0.5, 0.5) * block_scale(keys[3], (POLES,), ((0, 8),), -0.4, 0.0), -0.5, 0.5),
        "shift_imag": jnp.clip(jnp.exp(math.log(3.0) - 2.3025851 * jax.random.uniform(keys[4], (POLES,), jnp.float32) ** block_scale(keys[4], (POLES,), ((0, 8),), -0.2, 0.2)), 0.3, 3.0),
        "residue": normal_values(keys[5], (POLES, 2), 1.0, 4.0, ((0, 8),), jnp.float32),
    }


HIGH = lax.Precision.HIGHEST


def cdot(left, right):
    def mult(a, b):
        return jnp.dot(a, b, precision=HIGH, preferred_element_type=jnp.float32)
    return mult(left[0], right[0]) - mult(left[1], right[1]), mult(left[0], right[1]) + mult(left[1], right[0])


def cmul(left, right):
    return left[0] * right[0] - left[1] * right[1], left[0] * right[1] + left[1] * right[0]


def newton(matrix):
    size = matrix[0].shape[0]
    diag_real = jnp.diagonal(matrix[0])
    diag_imag = jnp.diagonal(matrix[1])
    denom = diag_real * diag_real + diag_imag * diag_imag
    inv_real = diag_real / denom
    inv_imag = -diag_imag / denom
    scaled = cmul((inv_real[:, None], inv_imag[:, None]), matrix)
    scaled = cmul(scaled, (inv_real[None, :], inv_imag[None, :]))
    eye = jnp.eye(size, dtype=jnp.float32)
    start = (2.0 * eye * inv_real[None, :] - scaled[0], 2.0 * eye * inv_imag[None, :] - scaled[1])
    product = cdot(start, matrix)
    product = cdot(product, start)
    return (2.0 * start[0] - product[0], 2.0 * start[1] - product[1])


def build_mask(pattern):
    blocks = jnp.repeat(jnp.repeat(pattern.astype(jnp.float32), SUPER, axis=0), SUPER, axis=1)
    ones_child = jnp.ones((C, C), jnp.float32)
    zero_child = jnp.zeros((C, C), jnp.float32)
    top = jnp.concatenate([ones_child, zero_child, blocks[:, :C].T], axis=1)
    middle = jnp.concatenate([zero_child, ones_child, blocks[:, C:].T], axis=1)
    bottom = jnp.concatenate([blocks, jnp.ones((R, R), jnp.float32)], axis=1)
    return jnp.concatenate([top, middle, bottom], axis=0)


def reference(hamiltonian, margin, pattern, shift_real, shift_imag, residue):
    mask = build_mask(pattern)

    def one_pole(total, inputs):
        real_shift, imag_shift, weight = inputs
        real = (hamiltonian - real_shift * margin) * mask
        imag = (-imag_shift * margin) * mask

        def block(row_lo, row_hi, col_lo, col_hi):
            return real[row_lo:row_hi, col_lo:col_hi], imag[row_lo:row_hi, col_lo:col_hi]

        schur = block(2 * C, N, 2 * C, N)
        inverses, factors = [], []
        for child in range(2):
            low = child * C
            high = low + C
            inverse = newton(block(low, high, low, high))
            factor = cdot(block(2 * C, N, low, high), inverse)
            term = cdot(factor, block(low, high, 2 * C, N))
            schur = (schur[0] - term[0], schur[1] - term[1])
            inverses.append(inverse)
            factors.append(factor)
        root_inv = newton(schur)
        sides, panels, diags = [], [], []
        for child in range(2):
            panel = cdot(root_inv, factors[child])
            panel = (-panel[0], -panel[1])
            side = (panel[0].T, panel[1].T)
            corr = cdot(side, factors[child])
            diag_block = (inverses[child][0] - corr[0], inverses[child][1] - corr[1])
            sides.append(side)
            panels.append(panel)
            diags.append(diag_block)

        def weigh(pair):
            return weight[0] * pair[0] - weight[1] * pair[1]

        empty = jnp.zeros((C, C), jnp.float32)
        first = jnp.concatenate([weigh(diags[0]), empty, weigh(sides[0])], axis=1)
        second = jnp.concatenate([empty, weigh(diags[1]), weigh(sides[1])], axis=1)
        third = jnp.concatenate([weigh(panels[0]), weigh(panels[1]), weigh(root_inv)], axis=1)
        return total + jnp.concatenate([first, second, third], axis=0), None

    start = jnp.zeros((N, N), jnp.float32)
    total, unused = lax.scan(one_pole, start, (shift_real, shift_imag, residue))
    return total * mask
```

```python
import jax
import jax.numpy as jnp
from jax import lax
from jax.experimental import pallas as pl
from jax.experimental.pallas import tpu as pltpu
from jax.sharding import PartitionSpec as P

C = 512
R = 1024
F32 = jnp.float32
BF16 = jnp.bfloat16
MESH = pl.DeviceIdType.MESH
ANY = pl.BlockSpec(memory_space=pl.ANY)
VM = pl.BlockSpec(memory_space=pltpu.VMEM)
SM = pl.BlockSpec(memory_space=pltpu.SMEM)
BLOCKS = ((0, 0), (0, 1), (0, 2), (1, 1), (1, 2), (1, 3), (2, 2), (2, 3), (3, 3), (3, 0))
NB = len(BLOCKS)


def mod4(v):
    return lax.rem(v + 4, 4)


def half(v):
    return lax.div(v, 2)


def place():
    p = lax.axis_index("pole")
    g = lax.axis_index("grid")
    x, yl = half(p), lax.rem(p, 2)
    z, q, c = lax.div(g, 4), half(g), lax.rem(g, 2)
    return p, g, x, yl, z, lax.rem(q, 2), q, c


def spot(x, y, z, c):
    return (2 * x + lax.rem(y, 2), 4 * z + 2 * half(y) + c)


def greet(devices):
    barrier = pltpu.get_barrier_semaphore()
    for device in devices:
        pl.semaphore_signal(barrier, inc=1, device_id=device, device_id_type=MESH)
    pl.semaphore_wait(barrier, len(devices))


def remote(src, dst, send, recv, device):
    return pltpu.make_async_remote_copy(
        src_ref=src, dst_ref=dst, send_sem=send, recv_sem=recv, device_id=device, device_id_type=MESH
    )


def gather_kernel(
    h_ref, s_ref, ab_ref, a0_ref,
    loc_sem, sib_s, sib_r, x_s, x_r, f_s, f_r, fo_s, fo_r, g_s, g_r, go_s, go_r,
    y0_s, y0_r, x0_s, x0_r,
):
    p, g, x, yl, z, yh, q, c = place()
    y = 2 * yh + yl
    sibling = (p, g + 1 - 2 * c)
    partner = (p + 1 - 2 * yl, g)
    xs = [spot(mod4(x + d), y, z, c) for d in (1, 2, 3)]
    ys = [spot(x, mod4(y + d), z, c) for d in (1, -1)]
    zs = [spot(x, y, mod4(z + d), c) for d in (1, -1)]
    greet([sibling] + xs + ys + zs)
    first = c == 0

    def pick(a, b):
        return tuple(jnp.where(first, u, v) for u, v in zip(a, b))

    fs = [pick(ys[i], zs[i]) for i in (0, 1)]
    gs = [pick(zs[i], ys[i]) for i in (0, 1)]
    f0 = jnp.where(first, y, z)
    g0 = jnp.where(first, z, y)

    def row(slot, f, s):
        yy, zz = jnp.where(first, f, s), jnp.where(first, s, f)
        return pl.multiple_of(slot * 512 + lax.rem(yy, 2) * 256 + (2 * zz + half(yy)) * 32, 32)

    def slab(slot, f, s):
        return ab_ref.at[:, pl.ds(row(slot, f, s), 32), :]

    def part(slot, f, s, k):
        return ab_ref.at[k, pl.ds(row(slot, f, s), 32), :]

    root = x >= 2
    mine = jnp.logical_or(root, x == c)
    his = jnp.logical_or(root, x == 1 - c)
    slot0 = jnp.maximum(x - 1, 0)
    row0 = pl.multiple_of(slot0 * 512 + yl * 256 + q * 32 + c * 16, 16)
    inputs = (h_ref, s_ref)
    own_cols = pl.ds(pl.multiple_of(c * 512, 128), 512)
    sib_cols = pl.ds(pl.multiple_of((1 - c) * 512, 128), 512)
    dst_rows = pl.ds(row0, 16)
    sib_rows = pl.ds(pl.multiple_of(row0 + (1 - 2 * c) * 16, 16), 16)
    own = [pltpu.make_async_copy(inputs[k].at[:, own_cols], ab_ref.at[k, dst_rows, :], loc_sem.at[k]) for k in (0, 1)]
    to_sib = [
        remote(inputs[k].at[:, sib_cols], ab_ref.at[k, dst_rows, :], sib_s.at[k], sib_r.at[k], sibling)
        for k in (0, 1)
    ]
    from_sib = [
        remote(inputs[k].at[:, own_cols], ab_ref.at[k, sib_rows, :], sib_s.at[k], sib_r.at[k], sibling)
        for k in (0, 1)
    ]
    j0 = 2 * jnp.maximum(x - 2, 0) + yl
    j1 = 2 * jnp.maximum(x - 2, 0) + 1 - yl

    def top(k, j):
        return a0_ref.at[k, pl.ds(pl.multiple_of(j * 16, 16), 16), :]

    top_src = [inputs[k].at[:, pl.ds(1024, 1024)] for k in (0, 1)]
    top_own = [pltpu.make_async_copy(top_src[k], top(k, j0), loc_sem.at[2 + k]) for k in (0, 1)]
    top_y = [remote(top_src[k], top(k, j0), y0_s.at[k], y0_r.at[k], partner) for k in (0, 1)]
    top_y_in = [remote(top_src[k], top(k, j1), y0_s.at[k], y0_r.at[k], partner) for k in (0, 1)]
    sx = jnp.maximum(x - 2, 0)
    top_x = [
        remote(top_src[k], top(k, j0), x0_s.at[n, 0, k], x0_r.at[sx, 0, k], xs[n]) for n in range(3) for k in (0, 1)
    ]
    top_x2 = [
        remote(top(k, j1), top(k, j1), x0_s.at[n, 1, k], x0_r.at[sx, 1, k], xs[n]) for n in range(3) for k in (0, 1)
    ]

    @pl.when(mine)
    def _():
        for copy in own:
            copy.start()

    @pl.when(his)
    def _():
        for copy in to_sib:
            copy.start()

    @pl.when(root)
    def _():
        for copy in top_y:
            copy.start()

    @pl.when(mine)
    def _():
        for copy in own:
            copy.wait()
        for copy in from_sib:
            copy.wait_recv()

    to_x = [remote(slab(slot0, f0, g0), slab(slot0, f0, g0), x_s.at[n], x_r.at[slot0], xs[n]) for n in range(3)]

    @pl.when(mine)
    def _():
        for copy in to_x:
            copy.start()

    @pl.when(root)
    def _():
        for copy in top_own:
            copy.start()
        for copy in top_x:
            copy.start()

    for slot in range(3):
        not_mine = jnp.logical_or(jnp.logical_not(mine), slot0 != slot)

        @pl.when(not_mine)
        def _():
            remote(slab(slot, f0, g0), slab(slot, f0, g0), x_s.at[0], x_r.at[slot], xs[0]).wait_recv()

    pending = []

    def go(copy):
        copy.start()
        pending.append(copy)

    f_at = (mod4(f0 - 1), mod4(f0 + 1), mod4(f0 + 2))
    g_at = (mod4(g0 - 1), mod4(g0 + 1), mod4(g0 + 2))
    for slot in range(3):
        for d in (0, 1):
            ref = slab(slot, f0, g0)
            go(remote(ref, ref, f_s.at[d, slot], f_r.at[d, slot], fs[d]))

    def spread(slot, n, f):
        ref = slab(slot, f, g0)
        for d in (0, 1):
            go(remote(ref, ref, g_s.at[d, slot, n], g_r.at[d, slot, n], gs[d]))

    for slot in range(3):
        spread(slot, 0, f0)
    for slot in range(3):
        for d in (0, 1):
            ref = slab(slot, f_at[d], g0)
            remote(ref, ref, f_s.at[d, slot], f_r.at[d, slot], fs[d]).wait_recv()
            ref = part(slot, f_at[d], g0, d)
            go(remote(ref, ref, fo_s.at[slot, d], fo_r.at[slot, d], fs[d]))
            spread(slot, 1 + d, f_at[d])

    @pl.when(root)
    def _():
        for k in (0, 1):
            top_y_in[k].wait_recv()
        for copy in top_x2:
            copy.start()

    def relay(slot, n, f):
        for d in (0, 1):
            ref = slab(slot, f, g_at[d])
            remote(ref, ref, g_s.at[d, slot, n], g_r.at[d, slot, n], gs[d]).wait_recv()
            ref = part(slot, f, g_at[d], d)
            go(remote(ref, ref, go_s.at[slot, n, d], go_r.at[slot, n, d], gs[d]))

    for slot in range(3):
        relay(slot, 0, f0)
    for slot in range(3):
        for d in (0, 1):
            ref = part(slot, f_at[2], g0, d)
            remote(ref, ref, fo_s.at[slot, d], fo_r.at[slot, d], fs[d]).wait_recv()
        spread(slot, 3, f_at[2])
    for n in (1, 2, 3):
        for slot in range(3):
            relay(slot, n, f_at[n - 1])
    for n in range(4):
        f = (f0,) + f_at
        for slot in range(3):
            for d in (0, 1):
                ref = part(slot, f[n], g_at[2], d)
                remote(ref, ref, go_s.at[slot, n, d], go_r.at[slot, n, d], gs[d]).wait_recv()

    for sx_in in (0, 1):
        jx = (2 * sx_in + yl, 2 * sx_in + 1 - yl)

        @pl.when(x != 2 + sx_in)
        def _():
            for o in (0, 1):
                for k in (0, 1):
                    ref = top(k, jx[o])
                    remote(ref, ref, x0_s.at[0, o, k], x0_r.at[sx_in, o, k], xs[0]).wait_recv()

    for copy in pending:
        copy.wait_send()

    @pl.when(his)
    def _():
        for copy in to_sib:
            copy.wait_send()

    @pl.when(mine)
    def _():
        for copy in to_x:
            copy.wait_send()

    @pl.when(root)
    def _():
        for copy in top_own:
            copy.wait()
        for copy in top_y + top_x + top_x2:
            copy.wait_send()


def gather_inputs(ham, margin):
    dma = pltpu.SemaphoreType.DMA
    return pl.pallas_call(
        gather_kernel,
        name="gather_inputs",
        out_shape=(
            jax.ShapeDtypeStruct((2, 1536, 512), F32),
            jax.ShapeDtypeStruct((2, 64, 1024), F32),
        ),
        in_specs=[ANY, ANY],
        out_specs=(ANY, ANY),
        scratch_shapes=[
            dma((4,)), dma((2,)), dma((2,)), dma((3,)), dma((3,)),
            dma((2, 3)), dma((2, 3)), dma((3, 2)), dma((3, 2)),
            dma((2, 3, 4)), dma((2, 3, 4)), dma((3, 4, 2)), dma((3, 4, 2)),
            dma((2,)), dma((2,)), dma((3, 2, 2)), dma((2, 2, 2)),
        ],
        compiler_params=pltpu.CompilerParams(collective_id=0, has_side_effects=True),
        cost_estimate=pl.CostEstimate(flops=0, bytes_accessed=16 << 20, transcendentals=0),
    )(ham, margin)


def split(v):
    high = v.astype(BF16)
    return high, (v - high.astype(F32)).astype(BF16)


def put_pair(lhs_ref, vr, vi):
    m, k = vr.shape
    rh, rl = split(vr)
    ih, il = split(vi)
    for at, (re, im) in enumerate(((rh, ih), (rl, il))):
        base = at * 2 * m
        lhs_ref[base : base + m, 0:k] = re
        lhs_ref[base : base + m, k : 2 * k] = -im
        lhs_ref[base + m : base + 2 * m, 0:k] = im
        lhs_ref[base + m : base + 2 * m, k : 2 * k] = re


def fold(wide, narrow, m):
    total = wide[0 : 2 * m] + wide[2 * m : 4 * m] + narrow
    return total[0:m], total[m : 2 * m]


def dot(a, b):
    return jnp.dot(a, b, preferred_element_type=F32)


def dot_t(a, b):
    return lax.dot_general(a, b, (((1,), (1,)), ((), ())), preferred_element_type=F32)


def times(lhs_ref, rhs_ref, out_ref, vr, vi, width):
    m, k = vr.shape
    put_pair(lhs_ref, vr, vi)
    for n in range(width // 256):
        cols = slice(n * 256, n * 256 + 256)
        wide = dot(lhs_ref[0 : 4 * m, 0 : 2 * k], rhs_ref[0, :, cols])
        narrow = dot(lhs_ref[0 : 2 * m, 0 : 2 * k], rhs_ref[1, :, cols])
        re, im = fold(wide, narrow, m)
        out_ref[0, 0:m, cols] = re
        out_ref[1, 0:m, cols] = im


def rotate(vr, vi, dr, di):
    return vr * dr - vi * di, vr * di + vi * dr


def recip(dr, di):
    den = dr * dr + di * di
    return dr / den, -di / den


def child_kernel(
    sc_ref, id_ref, ab_ref, mb_ref, ehl_ref, dinv_ref, bhl_ref, tb_ref, w_ref, xc_ref,
    lhs_e, lhs_t, u_ref, t_ref,
):
    sr, si = sc_ref[0], sc_ref[1]
    q = id_ref[0]
    dinv_ref[...] = jnp.zeros_like(dinv_ref)

    def scale_rows(n, _):
        r0 = pl.multiple_of(n * 64, 64)
        rows = pl.ds(r0, 64)
        low = pl.ds(pl.multiple_of(n * 64 + C, 64), 64)
        s = ab_ref[1, rows, :]
        re = ab_ref[0, rows, :] - sr * s
        im = -si * s
        eye = lax.broadcasted_iota(jnp.int32, (64, C), 1) == lax.broadcasted_iota(jnp.int32, (64, C), 0) + r0
        ir, ii = recip(
            jnp.sum(jnp.where(eye, re, 0.0), axis=1, keepdims=True),
            jnp.sum(jnp.where(eye, im, 0.0), axis=1, keepdims=True),
        )
        dinv_ref[0:1, :] += jnp.sum(jnp.where(eye, ir, 0.0), axis=0, keepdims=True)
        dinv_ref[1:2, :] += jnp.sum(jnp.where(eye, ii, 0.0), axis=0, keepdims=True)
        er, ei = rotate(re, im, -ir, -ii)
        for part, value in ((rows, er), (low, ei)):
            high, rest = split(jnp.where(eye, 0.0, value))
            ehl_ref[0, part, :] = high
            ehl_ref[1, part, :] = rest
        return 0

    lax.fori_loop(0, 8, scale_rows, 0)

    def couple(rows, j):
        m = mb_ref[pl.ds(j, 1), :]
        s = ab_ref[1, rows, :] * m
        return ab_ref[0, rows, :] * m - sr * s, -si * s

    def split_rows(n, _):
        re, im = couple(pl.ds(pl.multiple_of(C + n * 64, 64), 64), lax.div(n, 4))
        rows = pl.ds(pl.multiple_of(n * 64, 64), 64)
        for at, value in ((0, re), (C, im)):
            high, rest = split(value)
            bhl_ref[0, rows, at : at + C] = high
            bhl_ref[1, rows, at : at + C] = rest
        return 0

    lax.fori_loop(0, 16, split_rows, 0)

    for j in range(4):
        re, im = couple(pl.ds(pl.multiple_of(C + j * 256 + q * 32, 32), 32), j)
        t_ref[0, j * 32 : j * 32 + 32, :] = re
        t_ref[1, j * 32 : j * 32 + 32, :] = im
    vr, vi = t_ref[0, 0:128, :], t_ref[1, 0:128, :]
    times(lhs_e, ehl_ref, u_ref, vr, vi, C)
    u_ref[0, 0:128, :] += t_ref[0, 0:128, :]
    u_ref[1, 0:128, :] += t_ref[1, 0:128, :]
    for jj in range(2):
        at = pl.multiple_of(jj * 256 + q * 32, 32)
        low = pl.multiple_of(jj * 256 + q * 32 + C, 32)
        eye = lax.broadcasted_iota(jnp.int32, (32, C), 1) == lax.broadcasted_iota(jnp.int32, (32, C), 0) + at
        rows = slice(128 + jj * 32, 160 + jj * 32)
        er = ehl_ref[0, pl.ds(at, 32), :].astype(F32) + ehl_ref[1, pl.ds(at, 32), :].astype(F32)
        ei = ehl_ref[0, pl.ds(low, 32), :].astype(F32) + ehl_ref[1, pl.ds(low, 32), :].astype(F32)
        u_ref[0, rows, :] = jnp.where(eye, 1.0, er)
        u_ref[1, rows, :] = ei
    times(lhs_e, ehl_ref, t_ref, u_ref[0], u_ref[1], C)
    times(lhs_e, ehl_ref, t_ref, t_ref[0], t_ref[1], C)
    lr, li = rotate(u_ref[0] + t_ref[0], u_ref[1] + t_ref[1], dinv_ref[0:1, :], dinv_ref[1:2, :])
    xc_ref[0] = lr[128:192]
    xc_ref[1] = li[128:192]
    put_pair(lhs_t, lr, li)
    for n in range(4):
        rows = slice(n * 256, n * 256 + 256)
        wide = dot_t(lhs_t[...], bhl_ref[0, rows, :])
        narrow = dot_t(lhs_t[0:384, :], bhl_ref[1, rows, :])
        pair = fold(wide, narrow, 192)
        for k in (0, 1):
            w_ref[k, :, rows] = pair[k][128:192]
            for b, (j, other) in enumerate(BLOCKS):
                if other == n:
                    for cc in (0, 1):
                        tb_ref[cc, b, k] = pair[k][j * 32 + cc * 16 : j * 32 + cc * 16 + 16]


def child_part(scalars, ids, ab, mask_b):
    return pl.pallas_call(
        child_kernel,
        name="child_part",
        out_shape=(
            jax.ShapeDtypeStruct((2, 1024, C), BF16),
            jax.ShapeDtypeStruct((8, C), F32),
            jax.ShapeDtypeStruct((2, R, 2 * C), BF16),
            jax.ShapeDtypeStruct((2, NB, 2, 16, 256), F32),
            jax.ShapeDtypeStruct((2, 64, R), F32),
            jax.ShapeDtypeStruct((2, 64, C), F32),
        ),
        in_specs=[SM, SM, VM, VM],
        out_specs=(VM,) * 6,
        scratch_shapes=[
            pltpu.VMEM((768, 1024), BF16), pltpu.VMEM((768, 1024), BF16),
            pltpu.VMEM((2, 192, C), F32), pltpu.VMEM((2, 192, C), F32),
        ],
        compiler_params=pltpu.CompilerParams(vmem_limit_bytes=52 << 20),
        cost_estimate=pl.CostEstimate(flops=4 << 30, bytes_accessed=16 << 20, transcendentals=0),
    )(scalars, ids, ab, mask_b)


def schur_kernel(
    sc_ref, tb_ref, a0_ref, sg_ref,
    tin_ref, own_ref, t_s, t_r, loc_sem, y_s, y_r, z_s, z_r, o_s, o_r, b_s, b_r,
):
    p, g, x, yl, z, yh, q, c = place()
    y = 2 * yh + yl
    sibling = (p, g + 1 - 2 * c)
    over = (p, g + 2 - 4 * yh)
    zs = [spot(x, y, mod4(z + d), c) for d in (1, -1)]
    greet([sibling, over] + zs)
    swap = remote(tb_ref.at[1 - c], tin_ref, t_s, t_r, sibling)
    swap.start()
    sr, si = sc_ref[0], sc_ref[1]
    for b, (j, other) in enumerate(BLOCKS):
        s = a0_ref[1, j * 16 : j * 16 + 16, other * 256 : other * 256 + 256]
        own_ref[b, 0] = a0_ref[0, j * 16 : j * 16 + 16, other * 256 : other * 256 + 256] - sr * s - tb_ref[c, b, 0]
        own_ref[b, 1] = -si * s - tb_ref[c, b, 1]
    swap.wait()
    own_ref[...] = own_ref[...] - tin_ref[...]

    pending = []

    def go(copy):
        copy.start()
        pending.append(copy)

    def whole(gg):
        return sg_ref.at[:, :, gg]

    def part(gg, k):
        return sg_ref.at[:, k, gg]

    go(remote(own_ref, whole(g), y_s, y_r, over))
    for d in (0, 1):
        go(remote(own_ref, whole(g), z_s.at[d, 0], z_r.at[d, 0], zs[d]))
    mine = pltpu.make_async_copy(own_ref, whole(g), loc_sem)
    mine.start()
    for k in (0, 1):
        go(remote(own_ref.at[:, k], part(g, k), b_s.at[0, 0, k], b_r.at[0, 0, k], sibling))
    base = (g, g + 2 - 4 * yh)
    z_at = [4 * (mod4(z + d) - z) for d in (-1, 1, 2)]

    def hand_over(n, o, gg):
        for k in (0, 1):
            go(remote(part(gg, k), part(gg, k), b_s.at[n, o, k], b_r.at[n, o, k], sibling))

    remote(whole(base[1]), whole(base[1]), y_s, y_r, over).wait_recv()
    for d in (0, 1):
        go(remote(whole(base[1]), whole(base[1]), z_s.at[d, 1], z_r.at[d, 1], zs[d]))
    hand_over(0, 1, base[1])
    for o in (0, 1):
        for d in (0, 1):
            gg = base[o] + z_at[d]
            remote(whole(gg), whole(gg), z_s.at[d, o], z_r.at[d, o], zs[d]).wait_recv()
            go(remote(part(gg, d), part(gg, d), o_s.at[o, d], o_r.at[o, d], zs[d]))
            hand_over(1 + d, o, gg)
    for o in (0, 1):
        gg = base[o] + z_at[2]
        for d in (0, 1):
            remote(part(gg, d), part(gg, d), o_s.at[o, d], o_r.at[o, d], zs[d]).wait_recv()
            go(remote(part(gg, d), part(gg, d), b_s.at[3, o, d], b_r.at[3, o, d], sibling))
    for n in range(4):
        for o in (0, 1):
            gg = base[o] + ((0,) + tuple(z_at))[n] + 1 - 2 * c
            for k in (0, 1):
                remote(part(gg, k), part(gg, k), b_s.at[n, o, k], b_r.at[n, o, k], sibling).wait_recv()
    mine.wait()
    for copy in pending:
        copy.wait_send()


def share_schur(scalars, tb, a0):
    dma = pltpu.SemaphoreType.DMA
    return pl.pallas_call(
        schur_kernel,
        name="share_schur",
        out_shape=jax.ShapeDtypeStruct((NB, 2, 16, 16, 256), F32),
        in_specs=[SM, VM, VM],
        out_specs=ANY,
        scratch_shapes=[
            pltpu.VMEM((NB, 2, 16, 256), F32), pltpu.VMEM((NB, 2, 16, 256), F32),
            dma, dma, dma, dma, dma, dma((2, 2)), dma((2, 2)), dma((2, 2)), dma((2, 2)),
            dma((4, 2, 2)), dma((4, 2, 2)),
        ],
        compiler_params=pltpu.CompilerParams(collective_id=1, has_side_effects=True),
        cost_estimate=pl.CostEstimate(flops=0, bytes_accessed=16 << 20, transcendentals=0),
    )(scalars, tb, a0)


def root_kernel(
    sc_ref, id_ref, sg_ref, ehl_ref, dinv_ref, bhl_ref, w_ref, xc_ref, mf_ref,
    dw_ref, fw_ref, ft_ref, gw_ref,
    shl_ref, d0_ref, lhs, u_ref, t_ref, k_ref, ku_ref,
):
    g = id_ref[1]
    wr, wi = sc_ref[2], sc_ref[3]
    where = {pair: b for b, pair in enumerate(BLOCKS)}
    eye = lax.broadcasted_iota(jnp.int32, (256, 256), 1) == lax.broadcasted_iota(jnp.int32, (256, 256), 0)
    for j in range(4):
        rows = slice(j * 256, j * 256 + 256)
        low = slice(R + j * 256, R + j * 256 + 256)
        b = where[(j, j)]
        ir, ii = recip(
            jnp.sum(jnp.where(eye, sg_ref[b, 0], 0.0), axis=1, keepdims=True),
            jnp.sum(jnp.where(eye, sg_ref[b, 1], 0.0), axis=1, keepdims=True),
        )
        d0_ref[0:1, rows] = jnp.sum(jnp.where(eye, ir, 0.0), axis=0, keepdims=True)
        d0_ref[1:2, rows] = jnp.sum(jnp.where(eye, ii, 0.0), axis=0, keepdims=True)
        for other in range(4):
            cols = slice(other * 256, other * 256 + 256)
            if (j, other) in where:
                b = where[(j, other)]
                re, im = sg_ref[b, 0], sg_ref[b, 1]
            else:
                b = where[(other, j)]
                re, im = sg_ref[b, 0].T, sg_ref[b, 1].T
            er, ei = rotate(re, im, -ir, -ii)
            for part, value in ((rows, er), (low, ei)):
                if j == other:
                    value = jnp.where(eye, 0.0, value)
                high, rest = split(value)
                shl_ref[0, part, cols] = high
                shl_ref[1, part, cols] = rest
    times(lhs, shl_ref, u_ref, w_ref[0], w_ref[1], R)
    u_ref[0, 0:64, :] += w_ref[0]
    u_ref[1, 0:64, :] += w_ref[1]
    for j in range(4):
        at = pl.multiple_of(j * 256 + g * 16, 16)
        low = pl.multiple_of(j * 256 + g * 16 + R, 16)
        on = lax.broadcasted_iota(jnp.int32, (16, R), 1) == lax.broadcasted_iota(jnp.int32, (16, R), 0) + at
        rows = slice(64 + j * 16, 80 + j * 16)
        er = shl_ref[0, pl.ds(at, 16), :].astype(F32) + shl_ref[1, pl.ds(at, 16), :].astype(F32)
        ei = shl_ref[0, pl.ds(low, 16), :].astype(F32) + shl_ref[1, pl.ds(low, 16), :].astype(F32)
        u_ref[0, rows, :] = jnp.where(on, 1.0, er)
        u_ref[1, rows, :] = ei
    times(lhs, shl_ref, t_ref, u_ref[0], u_ref[1], R)
    times(lhs, shl_ref, t_ref, t_ref[0], t_ref[1], R)
    yr, yi = rotate(u_ref[0] + t_ref[0], u_ref[1] + t_ref[1], d0_ref[0:1, :], d0_ref[1:2, :])
    gw_ref[...] = wr * yr[64:128] - wi * yi[64:128]
    yr, yi = yr[0:64], yi[0:64]
    side = -(wr * yr - wi * yi) * mf_ref[...]
    fw_ref[...] = side
    ft_ref[...] = side.T
    rh, rl = split(yr)
    ih, il = split(yi)
    for at, (re, im) in enumerate(((rh, ih), (rl, il))):
        lhs[at * 128 : at * 128 + 64, 0:R] = re
        lhs[at * 128 + 64 : at * 128 + 128, 0:R] = im
        lhs[at * 128 : at * 128 + 64, R : 2 * R] = -im
        lhs[at * 128 + 64 : at * 128 + 128, R : 2 * R] = re
    wide = dot(lhs[0:256, 0:R], bhl_ref[0, :, 0:C]) + dot(lhs[0:256, R : 2 * R], bhl_ref[0, :, C : 2 * C])
    narrow = dot(lhs[0:128, 0:R], bhl_ref[1, :, 0:C]) + dot(lhs[0:128, R : 2 * R], bhl_ref[1, :, C : 2 * C])
    pr, pi = fold(wide, narrow, 64)
    times(lhs, ehl_ref, k_ref, pr, pi, C)
    ku_ref[0] = k_ref[0] + pr
    ku_ref[1] = k_ref[1] + pi
    times(lhs, ehl_ref, k_ref, ku_ref[0], ku_ref[1], C)
    times(lhs, ehl_ref, k_ref, k_ref[0], k_ref[1], C)
    zr, zi = rotate(ku_ref[0] + k_ref[0], ku_ref[1] + k_ref[1], dinv_ref[0:1, :], dinv_ref[1:2, :])
    dw_ref[...] = wr * (xc_ref[0] + zr) - wi * (xc_ref[1] + zi)


def root_part(scalars, ids, sg, ehl, dinv, bhl, w, xc, mask_f):
    return pl.pallas_call(
        root_kernel,
        name="root_part",
        out_shape=(
            jax.ShapeDtypeStruct((64, C), F32),
            jax.ShapeDtypeStruct((64, R), F32),
            jax.ShapeDtypeStruct((R, 64), F32),
            jax.ShapeDtypeStruct((64, R), F32),
        ),
        in_specs=[SM, SM] + [VM] * 7,
        out_specs=(VM,) * 4,
        scratch_shapes=[
            pltpu.VMEM((2, 2 * R, R), BF16), pltpu.VMEM((8, R), F32), pltpu.VMEM((512, 2 * R), BF16),
            pltpu.VMEM((2, 128, R), F32), pltpu.VMEM((2, 128, R), F32),
            pltpu.VMEM((2, 64, C), F32), pltpu.VMEM((2, 64, C), F32),
        ],
        compiler_params=pltpu.CompilerParams(vmem_limit_bytes=52 << 20),
        cost_estimate=pl.CostEstimate(flops=8 << 30, bytes_accessed=16 << 20, transcendentals=0),
    )(scalars, ids, sg, ehl, dinv, bhl, w, xc, mask_f)


def sum_kernel(
    dw_ref, fw_ref, ft_ref, gw_ref, main_ref, d_ref, e_ref,
    rf_ref, rd_ref, re_ref, ea_ref,
    loc_sem, a_s, a_r, f_s, f_r, d_s, d_r, g_s, e_s, e_r,
):
    p, g, x, yl, z, yh, q, c = place()
    poles = [lax.rem(p + d, 8) for d in range(8)]
    sib = g + 1 - 2 * c
    grids = [lax.rem(g + d, 16) for d in range(1, 16)]
    greet([(pp, g) for pp in poles[1:]] + [(pp, sib) for pp in poles[1:]] + [(p, gg) for gg in grids])
    top = p >= 4
    pending = []

    def go(copy):
        copy.start()
        pending.append(copy)

    for d, gg in enumerate(grids):
        go(remote(ft_ref.at[:, gg], ea_ref.at[g], a_s.at[d], a_r.at[d], (p, gg)))
    keep = pltpu.make_async_copy(ft_ref.at[:, g], ea_ref.at[g], loc_sem.at[0])
    keep.start()
    later = []
    for j in range(4):
        src = gw_ref.at[pl.ds(j * 16, 16), :]
        away = remote(src, rf_ref.at[p], g_s.at[j], f_r.at[p], (4 + j, g))
        stay = pltpu.make_async_copy(src, rf_ref.at[p], g_s.at[j])
        later.append((p == 4 + j, away, stay))
    for jj in (0, 1):
        for cc in (0, 1):
            rows = pl.ds(jj * 32 + cc * 16, 16)
            target = (2 * c + jj, 2 * q + cc)
            here = jnp.logical_and(p == 2 * c + jj, c == cc)
            for src, dst, ss, rs in ((fw_ref, rf_ref, f_s, f_r), (dw_ref, rd_ref, d_s, d_r)):
                away = remote(src.at[rows, :], dst.at[p], ss.at[jj, cc], rs.at[p], target)
                stay = pltpu.make_async_copy(src.at[rows, :], dst.at[p], ss.at[jj, cc])
                later.append((here, away, stay))
    for here, away, stay in later:

        @pl.when(jnp.logical_not(here))
        def _():
            away.start()

        @pl.when(here)
        def _():
            stay.start()

    keep.wait()
    for d in range(15):
        gg = lax.rem(g + 15 - d, 16)
        remote(ea_ref.at[gg], ea_ref.at[gg], a_s.at[d], a_r.at[d], (p, grids[0])).wait_recv()
    last = []
    for j in range(4):
        src = ea_ref.at[:, j]
        away = remote(src, re_ref.at[p], e_s.at[j], e_r.at[p], (4 + j, g))
        stay = pltpu.make_async_copy(src, re_ref.at[p], e_s.at[j])
        last.append((p == 4 + j, away, stay))
    for here, away, stay in last:

        @pl.when(jnp.logical_not(here))
        def _():
            away.start()

        @pl.when(here)
        def _():
            stay.start()

    for here, away, stay in later + last:

        @pl.when(jnp.logical_not(here))
        def _():
            away.wait_send()

        @pl.when(here)
        def _():
            stay.wait()

    other = (lax.rem(p + 1, 8), g)
    same = jnp.logical_or(top, c == half(p))
    for d in range(8):
        pp = poles[d]

        @pl.when(jnp.logical_or(jnp.logical_not(same), d > 0))
        def _():
            remote(rf_ref.at[pp], rf_ref.at[pp], f_s.at[0, 0], f_r.at[pp], other).wait_recv()

        @pl.when(jnp.logical_and(jnp.logical_not(top), jnp.logical_or(jnp.logical_not(same), d > 0)))
        def _():
            remote(rd_ref.at[pp], rd_ref.at[pp], d_s.at[0, 0], d_r.at[pp], other).wait_recv()

    main = rf_ref[0]
    for n in range(1, 8):
        main = main + rf_ref[n]
    main_ref[...] = main

    @pl.when(top)
    def _():
        for d in range(1, 8):
            pp = poles[d]
            remote(re_ref.at[pp], re_ref.at[pp], e_s.at[0], e_r.at[pp], other).wait_recv()
        total = re_ref[0]
        for n in range(1, 8):
            total = total + re_ref[n]
        e_ref[...] = total
        d_ref[...] = jnp.zeros_like(d_ref)

    @pl.when(jnp.logical_not(top))
    def _():
        total = rd_ref[0]
        for n in range(1, 8):
            total = total + rd_ref[n]
        d_ref[...] = total
        e_ref[...] = jnp.zeros_like(e_ref)

    for copy in pending:
        copy.wait_send()


def sum_poles(dw, fw, ft, gw):
    dma = pltpu.SemaphoreType.DMA
    return pl.pallas_call(
        sum_kernel,
        name="sum_poles",
        out_shape=(
            jax.ShapeDtypeStruct((16, R), F32),
            jax.ShapeDtypeStruct((16, C), F32),
            jax.ShapeDtypeStruct((16, 16, 64), F32),
        ),
        in_specs=[VM] * 4,
        out_specs=(VM,) * 3,
        scratch_shapes=[
            pltpu.VMEM((8, 16, R), F32), pltpu.VMEM((8, 16, C), F32), pltpu.VMEM((8, 16, 16, 64), F32),
            pltpu.VMEM((16, 4, 16, 64), F32),
            dma((1,)), dma((15,)), dma((15,)), dma((2, 2)), dma((8,)), dma((2, 2)), dma((8,)),
            dma((4,)), dma((4,)), dma((8,)),
        ],
        compiler_params=pltpu.CompilerParams(
            collective_id=2, has_side_effects=True, vmem_limit_bytes=40 << 20
        ),
        cost_estimate=pl.CostEstimate(flops=0, bytes_accessed=4 << 20, transcendentals=0),
    )(dw, fw, ft.reshape(4, 16, 16, 64), gw)


def local(hamiltonian, margin, pattern, shift_real, shift_imag, residue):
    p = lax.axis_index("pole")
    g = lax.axis_index("grid")
    q, c = g // 2, g % 2
    scalars = jnp.stack([shift_real[0], shift_imag[0], residue[0, 0], residue[0, 1]])
    ids = jnp.stack([q, g]).astype(jnp.int32)
    own = lax.dynamic_slice_in_dim(pattern.astype(F32), 2 * c, 2, 1)
    mask_b = jnp.repeat(own, 256, axis=1)
    mask_f = jnp.repeat(jnp.repeat(own.T, 32, axis=0), 256, axis=1)
    ab, a0 = gather_inputs(hamiltonian, margin)
    ehl, dinv, bhl, tb, w, xc = child_part(scalars, ids, ab, mask_b)
    sg = share_schur(scalars, tb, a0).reshape(NB, 2, 256, 256)
    dw, fw, ft, gw = root_part(scalars, ids, sg, ehl, dinv, bhl, w, xc, mask_f)
    main, diag, side = sum_poles(dw, fw, ft, gw)
    side = side.reshape(8, 2, 16, 2, 32).transpose(2, 1, 3, 0, 4).reshape(16, R)
    zero = jnp.zeros_like(diag)
    left = jnp.where(
        p < 4,
        jnp.concatenate([jnp.where(p < 2, diag, zero), jnp.where(p < 2, zero, diag)], axis=1),
        side,
    )
    return jnp.concatenate([left, main], axis=1)


def solution(mesh):
    return jax.shard_map(
        local,
        mesh=mesh,
        in_specs=(
            P(("pole", "grid"), None),
            P(("pole", "grid"), None),
            P(),
            P("pole"),
            P("pole"),
            P("pole", None),
        ),
        out_specs=P(("pole", "grid"), None),
        check_vma=False,
    )
```

```python
import jax
import jax.numpy as jnp
from jax import lax
from jax.experimental import pallas as pl
from jax.experimental.pallas import tpu as pltpu
from jax.sharding import PartitionSpec as P

C = 512
R = 1024
F32 = jnp.float32
BF16 = jnp.bfloat16
MESH = pl.DeviceIdType.MESH
VM = pl.BlockSpec(memory_space=pltpu.VMEM)
SM = pl.BlockSpec(memory_space=pltpu.SMEM)
BLOCKS = ((0, 0), (3, 0), (0, 1), (1, 1), (0, 2), (1, 2), (2, 2), (1, 3), (2, 3), (3, 3))
WHERE = {pair: b for b, pair in enumerate(BLOCKS)}
NB = len(BLOCKS)
GROUPS = (slice(0, 4), slice(4, 10))


def mod4(v):
    return lax.rem(v + 4, 4)


def half(v):
    return lax.div(v, 2)


def place():
    p = lax.axis_index("pole")
    g = lax.axis_index("grid")
    x, yl = half(p), lax.rem(p, 2)
    z, q, c = lax.div(g, 4), half(g), lax.rem(g, 2)
    return p, g, x, yl, z, lax.rem(q, 2), q, c


def spot(x, y, z, c):
    return (2 * x + lax.rem(y, 2), 4 * z + 2 * half(y) + c)


def greet(devices):
    barrier = pltpu.get_barrier_semaphore()
    for device in devices:
        pl.semaphore_signal(barrier, inc=1, device_id=device, device_id_type=MESH)
    pl.semaphore_wait(barrier, len(devices))


def remote(src, dst, send, recv, device):
    return pltpu.make_async_remote_copy(
        src_ref=src, dst_ref=dst, send_sem=send, recv_sem=recv, device_id=device, device_id_type=MESH
    )


def split(v):
    high = v.astype(BF16)
    return high, (v - high.astype(F32)).astype(BF16)


def put_pair(lhs_ref, vr, vi):
    m, k = vr.shape
    rh, rl = split(vr)
    ih, il = split(vi)
    for at, (re, im) in enumerate(((rh, ih), (rl, il))):
        base = at * 2 * m
        lhs_ref[base : base + m, 0:k] = re
        lhs_ref[base : base + m, k : 2 * k] = -im
        lhs_ref[base + m : base + 2 * m, 0:k] = im
        lhs_ref[base + m : base + 2 * m, k : 2 * k] = re


def fold(wide, narrow, m):
    total = wide[0 : 2 * m] + wide[2 * m : 4 * m] + narrow
    return total[0:m], total[m : 2 * m]


def dot(a, b):
    return jnp.dot(a, b, preferred_element_type=F32)


def dot_t(a, b):
    return lax.dot_general(a, b, (((1,), (1,)), ((), ())), preferred_element_type=F32)


def times(lhs_ref, rhs_ref, out_ref, vr, vi, width):
    m, k = vr.shape
    put_pair(lhs_ref, vr, vi)
    for n in range(width // 256):
        cols = slice(n * 256, n * 256 + 256)
        wide = dot(lhs_ref[0 : 4 * m, 0 : 2 * k], rhs_ref[0, :, cols])
        narrow = dot(lhs_ref[0 : 2 * m, 0 : 2 * k], rhs_ref[1, :, cols])
        re, im = fold(wide, narrow, m)
        out_ref[0, 0:m, cols] = re
        out_ref[1, 0:m, cols] = im


def rotate(vr, vi, dr, di):
    return vr * dr - vi * di, vr * di + vi * dr


def recip(dr, di):
    den = dr * dr + di * di
    return dr / den, -di / den


def iota(shape, dim):
    return lax.broadcasted_iota(jnp.int32, shape, dim)


def kernel(
    h_ref, s_ref, pat_ref, sr_ref, si_ref, res_ref, out_ref,
    ab_ref, a0_ref, ehl_ref, bhl_ref, dinv_ref, lhs, cu_ref, ct_ref, xc_ref, w_ref, tb_ref,
    tin_ref, own_ref, sg_ref, shl_ref, d0_ref, u_ref, t_ref,
    k_ref, ku_ref, fw_ref, ft_ref, gw_ref, dw_ref, rf_ref, rd_ref, re_ref, ea_ref,
    loc_sem, sib_s, sib_r, x_s, x_r, f_s, f_r, fo_s, fo_r, g_s, g_r, go_s, go_r,
    y0_s, y0_r, x0_s, x0_r,
    tt_s, tt_r, own_sem, y_s, y_r, yo_s, yo_r, z_s, z_r, o_s, o_r, b_s, b_r,
    keep_sem, a_s, a_r, sf_s, sf_r, sd_s, sd_r, sg_s, se_s, se_r,
):
    p, g, x, yl, z, yh, q, c = place()
    y = 2 * yh + yl
    sr, si = sr_ref[0], si_ref[0]
    wr, wi = res_ref[0, 0], res_ref[0, 1]
    sib = g + 1 - 2 * c
    sibling = (p, sib)
    partner = (p + 1 - 2 * yl, g)
    over = (p, g + 2 - 4 * yh)
    xs = [spot(mod4(x + d), y, z, c) for d in (1, 2, 3)]
    ys = [spot(x, mod4(y + d), z, c) for d in (1, -1)]
    zs = [spot(x, y, mod4(z + d), c) for d in (1, -1)]
    poles = [lax.rem(p + d, 8) for d in range(8)]
    grids = [lax.rem(g + d, 16) for d in range(1, 16)]
    beyond = (partner[0], over[1])
    greet(
        [(pp, g) for pp in poles[1:]] + [(pp, sib) for pp in poles[1:]] + [(p, gg) for gg in grids] + [beyond]
    )

    pending = []

    def go(copy):
        copy.start()
        pending.append(copy)

    first = c == 0

    def pick(a, b):
        return tuple(jnp.where(first, u, v) for u, v in zip(a, b))

    fs = [pick(ys[i], zs[i]) for i in (0, 1)]
    gs = [pick(zs[i], ys[i]) for i in (0, 1)]
    f0 = jnp.where(first, y, z)
    g0 = jnp.where(first, z, y)

    def row(slot, f, s):
        yy, zz = jnp.where(first, f, s), jnp.where(first, s, f)
        return pl.multiple_of(slot * 512 + lax.rem(yy, 2) * 256 + (2 * zz + half(yy)) * 32, 32)

    def slab(slot, f, s):
        return ab_ref.at[:, pl.ds(row(slot, f, s), 32), :]

    def part(slot, f, s, k):
        return ab_ref.at[k, pl.ds(row(slot, f, s), 32), :]

    root = x >= 2
    mine = jnp.logical_or(root, x == c)
    his = jnp.logical_or(root, x == 1 - c)
    slot0 = jnp.maximum(x - 1, 0)
    row0 = pl.multiple_of(slot0 * 512 + yl * 256 + q * 32 + c * 16, 16)
    inputs = (h_ref, s_ref)
    own_cols = pl.ds(pl.multiple_of(c * 512, 128), 512)
    sib_cols = pl.ds(pl.multiple_of((1 - c) * 512, 128), 512)
    dst_rows = pl.ds(row0, 16)
    sib_rows = pl.ds(pl.multiple_of(row0 + (1 - 2 * c) * 16, 16), 16)
    own = [pltpu.make_async_copy(inputs[k].at[:, own_cols], ab_ref.at[k, dst_rows, :], loc_sem.at[k]) for k in (0, 1)]
    to_sib = [
        remote(inputs[k].at[:, sib_cols], ab_ref.at[k, dst_rows, :], sib_s.at[k], sib_r.at[k], sibling)
        for k in (0, 1)
    ]
    from_sib = [
        remote(inputs[k].at[:, own_cols], ab_ref.at[k, sib_rows, :], sib_s.at[k], sib_r.at[k], sibling)
        for k in (0, 1)
    ]
    sx = jnp.maximum(x - 2, 0)
    j0 = 2 * sx + yl
    j1 = 2 * sx + 1 - yl

    def top(k, j):
        return a0_ref.at[k, pl.ds(pl.multiple_of(j * 16, 16), 16), :]

    top_src = [inputs[k].at[:, pl.ds(1024, 1024)] for k in (0, 1)]
    top_own = [pltpu.make_async_copy(top_src[k], top(k, j0), loc_sem.at[2 + k]) for k in (0, 1)]
    top_y = [remote(top_src[k], top(k, j0), y0_s.at[k], y0_r.at[k], partner) for k in (0, 1)]
    top_y_in = [remote(top_src[k], top(k, j1), y0_s.at[k], y0_r.at[k], partner) for k in (0, 1)]
    top_x = [
        remote(top_src[k], top(k, j0), x0_s.at[n, 0, k], x0_r.at[sx, 0, k], xs[n]) for n in range(3) for k in (0, 1)
    ]
    top_x2 = [
        remote(top(k, j1), top(k, j1), x0_s.at[n, 1, k], x0_r.at[sx, 1, k], xs[n]) for n in range(3) for k in (0, 1)
    ]

    @pl.when(his)
    def _():
        for copy in to_sib:
            copy.start()

    @pl.when(mine)
    def _():
        for copy in own:
            copy.start()
        for copy in own:
            copy.wait()
        for copy in from_sib:
            copy.wait_recv()

    to_x = [remote(slab(slot0, f0, g0), slab(slot0, f0, g0), x_s.at[n], x_r.at[slot0], xs[n]) for n in range(3)]

    @pl.when(mine)
    def _():
        for copy in to_x:
            copy.start()

    for slot in range(3):
        not_mine = jnp.logical_or(jnp.logical_not(mine), slot0 != slot)

        @pl.when(not_mine)
        def _():
            remote(slab(slot, f0, g0), slab(slot, f0, g0), x_s.at[0], x_r.at[slot], xs[0]).wait_recv()

    f_at = (f0, mod4(f0 - 1), mod4(f0 + 1), mod4(f0 + 2))
    g_at = (mod4(g0 - 1), mod4(g0 + 1), mod4(g0 + 2))

    def spread(slot, n):
        ref = slab(slot, f_at[n], g0)
        for d in (0, 1):
            go(remote(ref, ref, g_s.at[d, slot, n], g_r.at[d, slot, n], gs[d]))

    def open_slot(slot):
        ref = slab(slot, f0, g0)
        for d in (0, 1):
            go(remote(ref, ref, f_s.at[d, slot], f_r.at[d, slot], fs[d]))
        spread(slot, 0)

    def near(slot):
        for d in (0, 1):
            ref = slab(slot, f_at[1 + d], g0)
            remote(ref, ref, f_s.at[d, slot], f_r.at[d, slot], fs[d]).wait_recv()
            ref = part(slot, f_at[1 + d], g0, d)
            go(remote(ref, ref, fo_s.at[slot, d], fo_r.at[slot, d], fs[d]))
            spread(slot, 1 + d)

    def far(slot):
        for d in (0, 1):
            ref = part(slot, f_at[3], g0, d)
            remote(ref, ref, fo_s.at[slot, d], fo_r.at[slot, d], fs[d]).wait_recv()
        spread(slot, 3)

    def relay(slot, n):
        for d in (0, 1):
            ref = slab(slot, f_at[n], g_at[d])
            remote(ref, ref, g_s.at[d, slot, n], g_r.at[d, slot, n], gs[d]).wait_recv()
            ref = part(slot, f_at[n], g_at[d], d)
            go(remote(ref, ref, go_s.at[slot, n, d], go_r.at[slot, n, d], gs[d]))

    def close_slot(slot):
        for n in range(4):
            for d in (0, 1):
                ref = part(slot, f_at[n], g_at[2], d)
                remote(ref, ref, go_s.at[slot, n, d], go_r.at[slot, n, d], gs[d]).wait_recv()

    def top_start():
        @pl.when(root)
        def _():
            for copy in top_y + top_own + top_x:
                copy.start()

    def top_more():
        @pl.when(root)
        def _():
            for k in (0, 1):
                top_y_in[k].wait_recv()
            for copy in top_x2:
                copy.start()

    dinv_ref[...] = jnp.zeros_like(dinv_ref)

    def scale_rows(n):
        rows = slice(n * 64, n * 64 + 64)
        low = slice(n * 64 + C, n * 64 + C + 64)
        s = ab_ref[1, rows, :]
        re = ab_ref[0, rows, :] - sr * s
        im = -si * s
        eye = iota((64, C), 1) == iota((64, C), 0) + n * 64
        ir, ii = recip(
            jnp.sum(jnp.where(eye, re, 0.0), axis=1, keepdims=True),
            jnp.sum(jnp.where(eye, im, 0.0), axis=1, keepdims=True),
        )
        dinv_ref[0:1, :] += jnp.sum(jnp.where(eye, ir, 0.0), axis=0, keepdims=True)
        dinv_ref[1:2, :] += jnp.sum(jnp.where(eye, ii, 0.0), axis=0, keepdims=True)
        er, ei = rotate(re, im, -ir, -ii)
        for where, value in ((rows, er), (low, ei)):
            high, rest = split(jnp.where(eye, 0.0, value))
            ehl_ref[0, where, :] = high
            ehl_ref[1, where, :] = rest

    def pattern_at(j, half_at):
        return jnp.where(first, pat_ref[j, half_at], pat_ref[j, 2 + half_at]).astype(F32)

    def couple(rows, j):
        m = jnp.where(iota((1, C), 1) < 256, pattern_at(j, 0), pattern_at(j, 1))
        s = ab_ref[1, rows, :] * m
        return ab_ref[0, rows, :] * m - sr * s, -si * s

    def split_rows(n):
        re, im = couple(slice(C + n * 64, C + n * 64 + 64), n // 4)
        rows = slice(n * 64, n * 64 + 64)
        for at, value in ((0, re), (C, im)):
            high, rest = split(value)
            bhl_ref[0, rows, at : at + C] = high
            bhl_ref[1, rows, at : at + C] = rest

    def chain_start():
        for j in range(4):
            re, im = couple(pl.ds(pl.multiple_of(C + j * 256 + q * 32, 32), 32), j)
            ct_ref[0, j * 32 : j * 32 + 32, :] = re
            ct_ref[1, j * 32 : j * 32 + 32, :] = im
        times(lhs, ehl_ref, cu_ref, ct_ref[0, 0:128, :], ct_ref[1, 0:128, :], C)
        cu_ref[0, 0:128, :] += ct_ref[0, 0:128, :]
        cu_ref[1, 0:128, :] += ct_ref[1, 0:128, :]
        for jj in range(2):
            at = pl.multiple_of(jj * 256 + q * 32, 32)
            low = pl.multiple_of(jj * 256 + q * 32 + C, 32)
            eye = iota((32, C), 1) == iota((32, C), 0) + at
            rows = slice(128 + jj * 32, 160 + jj * 32)
            er = ehl_ref[0, pl.ds(at, 32), :].astype(F32) + ehl_ref[1, pl.ds(at, 32), :].astype(F32)
            ei = ehl_ref[0, pl.ds(low, 32), :].astype(F32) + ehl_ref[1, pl.ds(low, 32), :].astype(F32)
            cu_ref[0, rows, :] = jnp.where(eye, 1.0, er)
            cu_ref[1, rows, :] = ei

    def chain_two():
        times(lhs, ehl_ref, ct_ref, cu_ref[0], cu_ref[1], C)

    def chain_three():
        times(lhs, ehl_ref, ct_ref, ct_ref[0], ct_ref[1], C)
        lr, li = rotate(cu_ref[0] + ct_ref[0], cu_ref[1] + ct_ref[1], dinv_ref[0:1, :], dinv_ref[1:2, :])
        xc_ref[0] = lr[128:192]
        xc_ref[1] = li[128:192]
        put_pair(lhs, lr, li)

    def product(n):
        rows = slice(n * 256, n * 256 + 256)
        wide = dot_t(lhs[0:768, 0 : 2 * C], bhl_ref[0, rows, :])
        narrow = dot_t(lhs[0:384, 0 : 2 * C], bhl_ref[1, rows, :])
        pair = fold(wide, narrow, 192)
        for k in (0, 1):
            w_ref[k, :, rows] = pair[k][128:192]
            for b, (j, other) in enumerate(BLOCKS):
                if other == n:
                    for cc in (0, 1):
                        tb_ref[cc, b, k] = pair[k][j * 32 + cc * 16 : j * 32 + cc * 16 + 16]

    for slot in range(3):
        open_slot(slot)
    near(0)
    relay(0, 0)
    near(1)
    far(0)
    top_start()
    relay(1, 0)
    near(2)
    for n in (1, 2):
        relay(0, n)
    relay(2, 0)
    relay(0, 3)
    far(1)
    relay(1, 1)
    far(2)
    relay(1, 2)
    close_slot(0)
    mixed = [
        lambda: scale_rows(0), lambda: scale_rows(1), lambda: relay(2, 1),
        lambda: scale_rows(2), lambda: scale_rows(3), lambda: relay(2, 2),
        lambda: scale_rows(4), lambda: scale_rows(5), lambda: relay(1, 3),
        lambda: scale_rows(6), lambda: scale_rows(7), lambda: relay(2, 3), top_more,
        chain_start, chain_two, chain_three,
        lambda: close_slot(1),
    ] + [lambda n=n: split_rows(n) for n in range(8)] + [
        lambda: close_slot(2),
    ] + [lambda n=n: split_rows(n) for n in range(8, 16)]
    for step in mixed:
        step()

    for sx_in in (0, 1):
        jx = (2 * sx_in + yl, 2 * sx_in + 1 - yl)

        @pl.when(x != 2 + sx_in)
        def _():
            for o in (0, 1):
                for k in (0, 1):
                    ref = top(k, jx[o])
                    remote(ref, ref, x0_s.at[0, o, k], x0_r.at[sx_in, o, k], xs[0]).wait_recv()

    @pl.when(root)
    def _():
        for copy in top_own:
            copy.wait()

    swaps = [
        remote(tb_ref.at[1 - c, blocks], tin_ref.at[blocks], tt_s.at[n], tt_r.at[n], sibling)
        for n, blocks in enumerate(GROUPS_DS)
    ]
    product(0)
    product(1)
    go(swaps[0])
    product(2)
    product(3)
    go(swaps[1])

    def finish(n):
        for b in range(GROUPS[n].start, GROUPS[n].stop):
            j, other = BLOCKS[b]
            s = a0_ref[1, j * 16 : j * 16 + 16, other * 256 : other * 256 + 256]
            h = a0_ref[0, j * 16 : j * 16 + 16, other * 256 : other * 256 + 256]
            own_ref[b, 0] = h - sr * s - tb_ref[c, b, 0]
            own_ref[b, 1] = -si * s - tb_ref[c, b, 1]
        swaps[n].wait_recv()
        rows = GROUPS[n]
        own_ref[rows] = own_ref[rows] - tin_ref[rows]

    def whole(n, gg):
        return sg_ref.at[GROUPS_DS[n], :, gg]

    def piece(n, gg, k):
        return sg_ref.at[GROUPS_DS[n], k, gg]

    base = (g, g + 2 - 4 * yh)
    hop = [0] + [4 * (mod4(z + d) - z) for d in (-1, 1, 2)]

    def hand(n, m, o, ref_of):
        for k in (0, 1):
            ref = piece(n, base[o] + hop[m], k)
            go(remote(ref_of(k), ref, b_s.at[n, m, o, k], b_r.at[n, m, o, k], sibling))

    def along_z(n, o, src):
        dst = whole(n, base[o])
        for d in (0, 1):
            go(remote(dst if src is None else src, dst, z_s.at[d, n, o], z_r.at[d, n, o], zs[d]))

    keeps = []
    for n in (0, 1):
        finish(n)
        src = own_ref.at[GROUPS_DS[n]]
        along_z(n, 0, src)
        go(remote(src, whole(n, g), y_s.at[n], y_r.at[n], over))
        keep = pltpu.make_async_copy(src, whole(n, g), own_sem.at[n])
        keep.start()
        keeps.append(keep)
        hand(n, 0, 0, lambda k, n=n: own_ref.at[GROUPS_DS[n], k])

    def from_over(n):
        ref = whole(n, base[1])
        remote(ref, ref, y_s.at[n], y_r.at[n], over).wait_recv()
        hand(n, 0, 1, lambda k: piece(n, base[1], k))

    def from_z(n, o):
        for d in (0, 1):
            gg = base[o] + hop[1 + d]
            ref = whole(n, gg)
            remote(ref, ref, z_s.at[d, n, o], z_r.at[d, n, o], zs[d]).wait_recv()
            ref = piece(n, gg, d)
            go(remote(ref, ref, o_s.at[n, o, d], o_r.at[n, o, d], zs[d]))
            if n == 0:
                for k in (0, 1):
                    ref = piece(n, gg, k)
                    go(remote(ref, ref, yo_s.at[1 + d, k], yo_r.at[1 + d, k], over))
            hand(n, 1 + d, o, lambda k, gg=gg: piece(n, gg, k))

    def from_far(n, o):
        gg = base[o] + hop[3]
        for k in (0, 1):
            ref = piece(n, gg, k)
            remote(ref, ref, o_s.at[n, o, k], o_r.at[n, o, k], zs[k]).wait_recv()
            if n == 0:
                go(remote(ref, ref, yo_s.at[3, k], yo_r.at[3, k], over))
            go(remote(ref, ref, b_s.at[n, 3, o, k], b_r.at[n, 3, o, k], sibling))

    def over_far(m):
        gg = base[1] + hop[m]
        for k in (0, 1):
            ref = piece(0, gg, k)
            remote(ref, ref, yo_s.at[m, k], yo_r.at[m, k], over).wait_recv()
            go(remote(ref, ref, b_s.at[0, m, 1, k], b_r.at[0, m, 1, k], sibling))

    from_z(0, 0)
    from_over(1)
    along_z(1, 1, None)
    from_over(0)
    from_far(0, 0)
    from_z(1, 0)
    over_far(1)
    over_far(2)
    from_z(1, 1)
    from_far(1, 0)
    over_far(3)
    from_far(1, 1)
    for n in (0, 1):
        for m in range(4):
            for o in (0, 1):
                gg = base[o] + hop[m] + 1 - 2 * c
                for k in (0, 1):
                    ref = piece(n, gg, k)
                    remote(ref, ref, b_s.at[n, m, o, k], b_r.at[n, m, o, k], sibling).wait_recv()
    for keep in keeps:
        keep.wait()

    def block(b, k):
        return sg_ref[b, k].reshape(256, 256)

    eye = iota((256, 256), 1) == iota((256, 256), 0)
    for j in range(4):
        rows = slice(j * 256, j * 256 + 256)
        low = slice(R + j * 256, R + j * 256 + 256)
        b = WHERE[(j, j)]
        ir, ii = recip(
            jnp.sum(jnp.where(eye, block(b, 0), 0.0), axis=1, keepdims=True),
            jnp.sum(jnp.where(eye, block(b, 1), 0.0), axis=1, keepdims=True),
        )
        d0_ref[0:1, rows] = jnp.sum(jnp.where(eye, ir, 0.0), axis=0, keepdims=True)
        d0_ref[1:2, rows] = jnp.sum(jnp.where(eye, ii, 0.0), axis=0, keepdims=True)
        for other in range(4):
            cols = slice(other * 256, other * 256 + 256)
            if (j, other) in WHERE:
                b = WHERE[(j, other)]
                re, im = block(b, 0), block(b, 1)
            else:
                b = WHERE[(other, j)]
                re, im = block(b, 0).T, block(b, 1).T
            er, ei = rotate(re, im, -ir, -ii)
            for where, value in ((rows, er), (low, ei)):
                if j == other:
                    value = jnp.where(eye, 0.0, value)
                high, rest = split(value)
                shl_ref[0, where, cols] = high
                shl_ref[1, where, cols] = rest
    times(lhs, shl_ref, u_ref, w_ref[0], w_ref[1], R)
    u_ref[0, 0:64, :] += w_ref[0]
    u_ref[1, 0:64, :] += w_ref[1]
    for j in range(4):
        at = pl.multiple_of(j * 256 + g * 16, 16)
        low = pl.multiple_of(j * 256 + g * 16 + R, 16)
        on = iota((16, R), 1) == iota((16, R), 0) + at
        rows = slice(64 + j * 16, 80 + j * 16)
        er = shl_ref[0, pl.ds(at, 16), :].astype(F32) + shl_ref[1, pl.ds(at, 16), :].astype(F32)
        ei = shl_ref[0, pl.ds(low, 16), :].astype(F32) + shl_ref[1, pl.ds(low, 16), :].astype(F32)
        u_ref[0, rows, :] = jnp.where(on, 1.0, er)
        u_ref[1, rows, :] = ei
    times(lhs, shl_ref, t_ref, u_ref[0], u_ref[1], R)
    times(lhs, shl_ref, t_ref, t_ref[0], t_ref[1], R)
    yr, yi = rotate(u_ref[0] + t_ref[0], u_ref[1] + t_ref[1], d0_ref[0:1, :], d0_ref[1:2, :])
    gw_ref[...] = wr * yr[64:128] - wi * yi[64:128]
    yr, yi = yr[0:64], yi[0:64]
    weighted = -(wr * yr - wi * yi)
    for j in range(4):
        cols = slice(j * 256, j * 256 + 256)
        m = jnp.where(iota((64, 1), 0) < 32, pattern_at(j, 0), pattern_at(j, 1))
        side = weighted[:, cols] * m
        fw_ref[:, cols] = side
        ft_ref[j] = side.T.reshape(16, 16, 64)

    for d, gg in enumerate(grids):
        go(remote(ft_ref.at[:, gg], ea_ref.at[g], a_s.at[d], a_r.at[d], (p, gg)))
    keep = pltpu.make_async_copy(ft_ref.at[:, g], ea_ref.at[g], keep_sem)
    keep.start()
    sent = []

    def send_or_keep(src, dst, ss, rs, target, here):
        away = remote(src, dst, ss, rs, target)
        stay = pltpu.make_async_copy(src, dst, ss)

        @pl.when(jnp.logical_not(here))
        def _():
            away.start()

        @pl.when(here)
        def _():
            stay.start()

        sent.append((here, away, stay))

    def child_rows(src, dst, ss, rs):
        for jj in (0, 1):
            for cc in (0, 1):
                here = jnp.logical_and(p == 2 * c + jj, c == cc)
                rows = pl.ds(jj * 32 + cc * 16, 16)
                send_or_keep(src.at[rows, :], dst.at[p], ss.at[jj, cc], rs.at[p], (2 * c + jj, 2 * q + cc), here)

    for j in range(4):
        send_or_keep(gw_ref.at[pl.ds(j * 16, 16), :], rf_ref.at[p], sg_s.at[j], sf_r.at[p], (4 + j, g), p == 4 + j)
    child_rows(fw_ref, rf_ref, sf_s, sf_r)

    rh, rl = split(yr)
    ih, il = split(yi)
    for at, (re, im) in enumerate(((rh, ih), (rl, il))):
        lhs[at * 128 : at * 128 + 64, 0:R] = re
        lhs[at * 128 + 64 : at * 128 + 128, 0:R] = im
        lhs[at * 128 : at * 128 + 64, R : 2 * R] = -im
        lhs[at * 128 + 64 : at * 128 + 128, R : 2 * R] = re
    wide = dot(lhs[0:256, 0:R], bhl_ref[0, :, 0:C]) + dot(lhs[0:256, R : 2 * R], bhl_ref[0, :, C : 2 * C])
    narrow = dot(lhs[0:128, 0:R], bhl_ref[1, :, 0:C]) + dot(lhs[0:128, R : 2 * R], bhl_ref[1, :, C : 2 * C])
    pr, pi = fold(wide, narrow, 64)

    keep.wait()
    for d in range(15):
        gg = lax.rem(g + 15 - d, 16)
        remote(ea_ref.at[gg], ea_ref.at[gg], a_s.at[d], a_r.at[d], (p, grids[0])).wait_recv()
    for j in range(4):
        send_or_keep(ea_ref.at[:, j], re_ref.at[p], se_s.at[j], se_r.at[p], (4 + j, g), p == 4 + j)

    times(lhs, ehl_ref, k_ref, pr, pi, C)
    ku_ref[0] = k_ref[0] + pr
    ku_ref[1] = k_ref[1] + pi
    times(lhs, ehl_ref, k_ref, ku_ref[0], ku_ref[1], C)
    times(lhs, ehl_ref, k_ref, k_ref[0], k_ref[1], C)
    zr, zi = rotate(ku_ref[0] + k_ref[0], ku_ref[1] + k_ref[1], dinv_ref[0:1, :], dinv_ref[1:2, :])
    dw_ref[...] = wr * (xc_ref[0] + zr) - wi * (xc_ref[1] + zi)
    child_rows(dw_ref, rd_ref, sd_s, sd_r)

    for here, away, stay in sent:

        @pl.when(jnp.logical_not(here))
        def _():
            away.wait_send()

        @pl.when(here)
        def _():
            stay.wait()

    lead = p >= 4
    same = jnp.logical_or(lead, c == half(p))
    for d in range(8):
        pp = poles[d]

        @pl.when(jnp.logical_or(jnp.logical_not(same), d > 0))
        def _():
            remote(rf_ref.at[pp], rf_ref.at[pp], sf_s.at[0, 0], sf_r.at[pp], partner).wait_recv()

        @pl.when(jnp.logical_and(jnp.logical_not(lead), jnp.logical_or(jnp.logical_not(same), d > 0)))
        def _():
            remote(rd_ref.at[pp], rd_ref.at[pp], sd_s.at[0, 0], sd_r.at[pp], partner).wait_recv()

    def total(ref):
        value = ref[0]
        for n in range(1, 8):
            value = value + ref[n]
        return value

    out_ref[:, R : 2 * R] = total(rf_ref)

    @pl.when(lead)
    def _():
        for d in range(1, 8):
            pp = poles[d]
            remote(re_ref.at[pp], re_ref.at[pp], se_s.at[0], se_r.at[pp], partner).wait_recv()
        side = total(re_ref)
        for k in (0, 1):
            for jj in (0, 1):
                cols = [side[2 * qq + k][:, jj * 32 : jj * 32 + 32] for qq in range(8)]
                at = k * 512 + jj * 256
                out_ref[:, at : at + 256] = jnp.concatenate(cols, axis=1)

    @pl.when(jnp.logical_not(lead))
    def _():
        diag = total(rd_ref)
        upper = p < 2
        out_ref[:, 0:C] = jnp.where(upper, diag, 0.0)
        out_ref[:, C : 2 * C] = jnp.where(upper, 0.0, diag)

    for copy in pending:
        copy.wait_send()

    @pl.when(his)
    def _():
        for copy in to_sib:
            copy.wait_send()

    @pl.when(mine)
    def _():
        for copy in to_x:
            copy.wait_send()

    @pl.when(root)
    def _():
        for copy in top_y + top_x + top_x2:
            copy.wait_send()


GROUPS_DS = tuple(pl.ds(blocks.start, blocks.stop - blocks.start) for blocks in GROUPS)


def local(hamiltonian, margin, pattern, shift_real, shift_imag, residue):
    dma = pltpu.SemaphoreType.DMA
    vm = pltpu.VMEM
    return pl.pallas_call(
        kernel,
        name="selected_inversion",
        out_shape=jax.ShapeDtypeStruct((16, 2 * R), F32),
        in_specs=[VM, VM, SM, SM, SM, SM],
        out_specs=VM,
        scratch_shapes=[
            vm((2, 1536, 512), F32), vm((2, 64, 1024), F32), vm((2, 1024, C), BF16), vm((2, R, 2 * C), BF16),
            vm((8, C), F32), vm((768, 2 * R), BF16), vm((2, 192, C), F32), vm((2, 192, C), F32),
            vm((2, 64, C), F32), vm((2, 64, R), F32), vm((2, NB, 2, 16, 256), F32),
            vm((NB, 2, 16, 256), F32), vm((NB, 2, 16, 256), F32), vm((NB, 2, 16, 16, 256), F32),
            vm((2, 2 * R, R), BF16), vm((8, R), F32), vm((2, 128, R), F32), vm((2, 128, R), F32),
            vm((2, 64, C), F32), vm((2, 64, C), F32), vm((64, R), F32), vm((4, 16, 16, 64), F32),
            vm((64, R), F32), vm((64, C), F32),
            vm((8, 16, R), F32), vm((8, 16, C), F32), vm((8, 16, 16, 64), F32), vm((16, 4, 16, 64), F32),
            dma((4,)), dma((2,)), dma((2,)), dma((3,)), dma((3,)),
            dma((2, 3)), dma((2, 3)), dma((3, 2)), dma((3, 2)),
            dma((2, 3, 4)), dma((2, 3, 4)), dma((3, 4, 2)), dma((3, 4, 2)),
            dma((2,)), dma((2,)), dma((3, 2, 2)), dma((2, 2, 2)),
            dma((2,)), dma((2,)), dma((2,)), dma((2,)), dma((2,)), dma((4, 2)), dma((4, 2)),
            dma((2, 2, 2)), dma((2, 2, 2)), dma((2, 2, 2)), dma((2, 2, 2)),
            dma((2, 4, 2, 2)), dma((2, 4, 2, 2)),
            dma, dma((15,)), dma((15,)), dma((2, 2)), dma((8,)), dma((2, 2)), dma((8,)),
            dma((4,)), dma((4,)), dma((8,)),
        ],
        compiler_params=pltpu.CompilerParams(
            collective_id=0, has_side_effects=True, vmem_limit_bytes=56 << 20
        ),
        cost_estimate=pl.CostEstimate(flops=12 << 30, bytes_accessed=1 << 20, transcendentals=0),
    )(hamiltonian, margin, pattern, shift_real, shift_imag, residue)


def solution(mesh):
    return jax.shard_map(
        local,
        mesh=mesh,
        in_specs=(
            P(("pole", "grid"), None),
            P(("pole", "grid"), None),
            P(),
            P("pole"),
            P("pole"),
            P("pole", None),
        ),
        out_specs=P(("pole", "grid"), None),
        check_vma=False,
    )
```

```python
import jax
import jax.numpy as jnp
from jax import lax
from jax.experimental import pallas as pl
from jax.experimental.pallas import tpu as pltpu
from jax.sharding import PartitionSpec as P

C = 512
R = 1024
F32 = jnp.float32
BF16 = jnp.bfloat16
MESH = pl.DeviceIdType.MESH
VM = pl.BlockSpec(memory_space=pltpu.VMEM)
SM = pl.BlockSpec(memory_space=pltpu.SMEM)
BLOCKS = ((0, 0), (3, 0), (0, 1), (1, 1), (0, 2), (1, 2), (2, 2), (1, 3), (2, 3), (3, 3))
WHERE = {pair: b for b, pair in enumerate(BLOCKS)}
NB = len(BLOCKS)
GROUPS = (slice(0, 4), slice(4, 10))


def mod4(v):
    return lax.rem(v + 4, 4)


def half(v):
    return lax.div(v, 2)


def place():
    p = lax.axis_index("pole")
    g = lax.axis_index("grid")
    x, yl = half(p), lax.rem(p, 2)
    z, q, c = lax.div(g, 4), half(g), lax.rem(g, 2)
    return p, g, x, yl, z, lax.rem(q, 2), q, c


def spot(x, y, z, c):
    return (2 * x + lax.rem(y, 2), 4 * z + 2 * half(y) + c)


def greet(devices):
    barrier = pltpu.get_barrier_semaphore()
    for device in devices:
        pl.semaphore_signal(barrier, inc=1, device_id=device, device_id_type=MESH)
    pl.semaphore_wait(barrier, len(devices))


def remote(src, dst, send, recv, device):
    return pltpu.make_async_remote_copy(
        src_ref=src, dst_ref=dst, send_sem=send, recv_sem=recv, device_id=device, device_id_type=MESH
    )


def split(v):
    high = v.astype(BF16)
    return high, (v - high.astype(F32)).astype(BF16)


def put_pair(lhs_ref, vr, vi):
    m, k = vr.shape
    rh, rl = split(vr)
    ih, il = split(vi)
    for at, (re, im) in enumerate(((rh, ih), (rl, il))):
        base = at * 2 * m
        lhs_ref[base : base + m, 0:k] = re
        lhs_ref[base : base + m, k : 2 * k] = -im
        lhs_ref[base + m : base + 2 * m, 0:k] = im
        lhs_ref[base + m : base + 2 * m, k : 2 * k] = re


def fold(wide, narrow, m):
    total = wide[0 : 2 * m] + wide[2 * m : 4 * m] + narrow
    return total[0:m], total[m : 2 * m]


def dot(a, b):
    return jnp.dot(a, b, preferred_element_type=F32)


def dot_t(a, b):
    return lax.dot_general(a, b, (((1,), (1,)), ((), ())), preferred_element_type=F32)


def times(lhs_ref, rhs_ref, out_ref, vr, vi, width):
    m, k = vr.shape
    put_pair(lhs_ref, vr, vi)
    for n in range(width // 256):
        cols = slice(n * 256, n * 256 + 256)
        wide = dot(lhs_ref[0 : 4 * m, 0 : 2 * k], rhs_ref[0, :, cols])
        narrow = dot(lhs_ref[0 : 2 * m, 0 : 2 * k], rhs_ref[1, :, cols])
        re, im = fold(wide, narrow, m)
        out_ref[0, 0:m, cols] = re
        out_ref[1, 0:m, cols] = im


def rotate(vr, vi, dr, di):
    return vr * dr - vi * di, vr * di + vi * dr


def recip(dr, di):
    den = dr * dr + di * di
    return dr / den, -di / den


def iota(shape, dim):
    return lax.broadcasted_iota(jnp.int32, shape, dim)


def kernel(
    h_ref, s_ref, pat_ref, sr_ref, si_ref, res_ref, out_ref,
    hs_ref, ab_ref, lb_ref, a0_ref, ehl_ref, bhl_ref, dinv_ref, lhs, cu_ref, ct_ref, xc_ref, w_ref, tb_ref,
    tin_ref, own_ref, sg_ref, shl_ref, d0_ref, u_ref, t_ref,
    k_ref, ku_ref, fw_ref, ft_ref, gw_ref, dw_ref, rf_ref, rd_ref, re_ref, ea_ref,
    loc_sem, x_s, x_r, f_s, f_r, fo_s, fo_r, g_s, g_r, go_s, go_r,
    lb_s, lb_r, xl_s, xl_r, xo_s, xo_r, y0_s, y0_r, x0_s, x0_r,
    tt_s, tt_r, own_sem, y_s, y_r, yo_s, yo_r, z_s, z_r, o_s, o_r, b_s, b_r,
    keep_sem, a_s, a_r, sf_s, sf_r, sd_s, sd_r, sg_s, se_s, se_r,
):
    p, g, x, yl, z, yh, q, c = place()
    y = 2 * yh + yl
    sr, si = sr_ref[0], si_ref[0]
    wr, wi = res_ref[0, 0], res_ref[0, 1]
    sib = g + 1 - 2 * c
    sibling = (p, sib)
    partner = (p + 1 - 2 * yl, g)
    over = (p, g + 2 - 4 * yh)
    xs = [spot(mod4(x + d), y, z, c) for d in (1, 2, 3)]
    ys = [spot(x, mod4(y + d), z, c) for d in (1, -1)]
    zs = [spot(x, y, mod4(z + d), c) for d in (1, -1)]
    poles = [lax.rem(p + d, 8) for d in range(8)]
    grids = [lax.rem(g + d, 16) for d in range(1, 16)]
    beyond = (partner[0], over[1])
    hs_ref[0] = h_ref[...]
    hs_ref[1] = s_ref[...]
    greet(
        [(pp, g) for pp in poles[1:]] + [(pp, sib) for pp in poles[1:]] + [(p, gg) for gg in grids] + [beyond]
    )

    pending = []

    def go(copy):
        copy.start()
        pending.append(copy)

    first = c == 0

    def pick(a, b):
        return tuple(jnp.where(first, u, v) for u, v in zip(a, b))

    fs = [pick(ys[i], zs[i]) for i in (0, 1)]
    gs = [pick(zs[i], ys[i]) for i in (0, 1)]
    f0 = jnp.where(first, y, z)
    g0 = jnp.where(first, z, y)

    def row(slot, f, s):
        yy, zz = jnp.where(first, f, s), jnp.where(first, s, f)
        return pl.multiple_of(slot * 512 + lax.rem(yy, 2) * 256 + (2 * zz + half(yy)) * 32, 32)

    def quarter(xx):
        return pl.ds(pl.multiple_of(xx * 128, 128), 128)

    def slab(slot, f, s):
        rows = pl.ds(row(slot, f, s), 32)
        return ab_ref.at[:, rows, :] if slot < 2 else ab_ref.at[:, rows, quarter(x)]

    def part(slot, f, s, k):
        rows = pl.ds(row(slot, f, s), 32)
        return ab_ref.at[k, rows, :] if slot < 2 else ab_ref.at[k, rows, quarter(x)]

    def own_slab(slot):
        return slab(slot, f0, g0) if slot < 2 else lb_ref.at[:, yl, :, quarter(x)]

    root = x >= 2
    peers = [[spot(mod4(x + d), y, z, cc) for cc in (c, 1 - c)] for d in range(4)]

    def land(slot, cc):
        if slot == 2:
            return lb_ref.at[:, yl, pl.ds(pl.multiple_of(cc * 16, 16), 16), :]
        return ab_ref.at[:, pl.ds(pl.multiple_of(slot * 512 + yl * 256 + q * 32 + cc * 16, 16), 16), :]

    def child_cols(k):
        return hs_ref.at[:, :, pl.ds(pl.multiple_of(k * 512, 128), 512)]

    def stay_put(slot):
        return pltpu.make_async_copy(child_cols(c), land(slot, c), loc_sem.at[slot])

    def give(slot, d, e):
        return remote(
            child_cols(c if e == 0 else 1 - c), land(slot, c), x_s.at[d, e], x_r.at[slot, e], peers[d][e]
        )

    def givers(slot):
        if slot > 0:
            away = [give(slot, d, e) for d in range(4) for e in (0, 1) if d + e > 0]
            return [(x == slot + 1, [stay_put(slot)], away)]
        return [
            (jnp.logical_and(x < 2, x == c), [stay_put(0)], [give(0, d, 0) for d in (1, 2, 3)]),
            (jnp.logical_and(x < 2, x != c), [], [give(0, d, 1) for d in range(4)]),
        ]

    gifts = givers(2) + givers(0) + givers(1)
    for when, here, away in gifts:

        @pl.when(when)
        def _():
            for copy in away + here:
                copy.start()

    def taken(slot):
        source = c if slot == 0 else slot + 1
        remote(land(slot, 1 - c), land(slot, 1 - c), x_s.at[1, 1], x_r.at[slot, 1], peers[1][1]).wait_recv()

        @pl.when(x != source)
        def _():
            remote(land(slot, c), land(slot, c), x_s.at[1, 0], x_r.at[slot, 0], peers[1][0]).wait_recv()

        @pl.when(x == source)
        def _():
            stay_put(slot).wait()

    sx = jnp.maximum(x - 2, 0)
    j0 = 2 * sx + yl
    j1 = 2 * sx + 1 - yl

    def top(k, j):
        return a0_ref.at[k, pl.ds(pl.multiple_of(j * 16, 16), 16), :]

    top_src = [hs_ref.at[k, :, pl.ds(1024, 1024)] for k in (0, 1)]
    top_own = [pltpu.make_async_copy(top_src[k], top(k, j0), loc_sem.at[3 + k]) for k in (0, 1)]
    top_y = [remote(top_src[k], top(k, j0), y0_s.at[k], y0_r.at[k], partner) for k in (0, 1)]
    top_y_in = [remote(top_src[k], top(k, j1), y0_s.at[k], y0_r.at[k], partner) for k in (0, 1)]
    top_x = [
        remote(top_src[k], top(k, j0), x0_s.at[n, 0, k], x0_r.at[sx, 0, k], xs[n]) for n in range(3) for k in (0, 1)
    ]
    top_x2 = [
        remote(top(k, j1), top(k, j1), x0_s.at[n, 1, k], x0_r.at[sx, 1, k], xs[n]) for n in range(3) for k in (0, 1)
    ]

    f_at = (f0, mod4(f0 - 1), mod4(f0 + 1), mod4(f0 + 2))
    g_at = (mod4(g0 - 1), mod4(g0 + 1), mod4(g0 + 2))

    def spread(slot, n):
        dst = slab(slot, f_at[n], g0)
        ref = own_slab(slot) if n == 0 else dst
        for d in (0, 1):
            go(remote(ref, dst, g_s.at[d, slot, n], g_r.at[d, slot, n], gs[d]))

    def open_slot(slot):
        taken(slot)
        for d in (0, 1):
            go(remote(own_slab(slot), slab(slot, f0, g0), f_s.at[d, slot], f_r.at[d, slot], fs[d]))
        spread(slot, 0)

    def near(slot):
        for d in (0, 1):
            ref = slab(slot, f_at[1 + d], g0)
            remote(ref, ref, f_s.at[d, slot], f_r.at[d, slot], fs[d]).wait_recv()
            ref = part(slot, f_at[1 + d], g0, d)
            go(remote(ref, ref, fo_s.at[slot, d], fo_r.at[slot, d], fs[d]))
            spread(slot, 1 + d)

    def far(slot):
        for d in (0, 1):
            ref = part(slot, f_at[3], g0, d)
            remote(ref, ref, fo_s.at[slot, d], fo_r.at[slot, d], fs[d]).wait_recv()
        spread(slot, 3)

    def relay(slot, n):
        for d in (0, 1):
            ref = slab(slot, f_at[n], g_at[d])
            remote(ref, ref, g_s.at[d, slot, n], g_r.at[d, slot, n], gs[d]).wait_recv()
            ref = part(slot, f_at[n], g_at[d], d)
            go(remote(ref, ref, go_s.at[slot, n, d], go_r.at[slot, n, d], gs[d]))

    def close_slot(slot):
        for n in range(4):
            for d in (0, 1):
                ref = part(slot, f_at[n], g_at[2], d)
                remote(ref, ref, go_s.at[slot, n, d], go_r.at[slot, n, d], gs[d]).wait_recv()

    def last_rows():
        ref = lb_ref.at[:, yl]
        go(remote(ref, ref, lb_s, lb_r, partner))
        pltpu.make_async_copy(own_slab(2), slab(2, f0, g0), loc_sem.at[5]).start()

    def last_rows_in():
        ref = lb_ref.at[:, 1 - yl]
        remote(ref, ref, lb_s, lb_r, partner).wait_recv()

    xx_at = (mod4(x - 1), mod4(x + 1), mod4(x + 2))
    along = (peers[1][0], peers[3][0])

    def column(xx):
        return ab_ref.at[:, pl.ds(1024, 512), quarter(xx)]

    def column_part(xx, k):
        return ab_ref.at[k, pl.ds(1024, 512), quarter(xx)]

    def join():
        pltpu.make_async_copy(own_slab(2), slab(2, f0, g0), loc_sem.at[5]).wait()
        for d in (0, 1):
            go(remote(column(x), column(x), xl_s.at[d], xl_r.at[d], along[d]))

    def join_more():
        for d in (0, 1):
            ref = column(xx_at[d])
            remote(ref, ref, xl_s.at[d], xl_r.at[d], along[d]).wait_recv()
            ref = column_part(xx_at[d], d)
            go(remote(ref, ref, xo_s.at[d], xo_r.at[d], along[d]))

    def join_end():
        for d in (0, 1):
            ref = column_part(xx_at[2], d)
            remote(ref, ref, xo_s.at[d], xo_r.at[d], along[d]).wait_recv()

    def top_start():
        @pl.when(root)
        def _():
            for copy in top_y + top_own + top_x:
                copy.start()

    def top_more():
        @pl.when(root)
        def _():
            for k in (0, 1):
                top_y_in[k].wait_recv()
            for copy in top_x2:
                copy.start()

    dinv_ref[...] = jnp.zeros_like(dinv_ref)

    def scale_rows(n):
        rows = slice(n * 64, n * 64 + 64)
        low = slice(n * 64 + C, n * 64 + C + 64)
        s = ab_ref[1, rows, :]
        re = ab_ref[0, rows, :] - sr * s
        im = -si * s
        eye = iota((64, C), 1) == iota((64, C), 0) + n * 64
        ir, ii = recip(
            jnp.sum(jnp.where(eye, re, 0.0), axis=1, keepdims=True),
            jnp.sum(jnp.where(eye, im, 0.0), axis=1, keepdims=True),
        )
        dinv_ref[0:1, :] += jnp.sum(jnp.where(eye, ir, 0.0), axis=0, keepdims=True)
        dinv_ref[1:2, :] += jnp.sum(jnp.where(eye, ii, 0.0), axis=0, keepdims=True)
        er, ei = rotate(re, im, -ir, -ii)
        for where, value in ((rows, er), (low, ei)):
            high, rest = split(jnp.where(eye, 0.0, value))
            ehl_ref[0, where, :] = high
            ehl_ref[1, where, :] = rest

    def pattern_at(j, half_at):
        return jnp.where(first, pat_ref[j, half_at], pat_ref[j, 2 + half_at]).astype(F32)

    def couple(h, s, j):
        m = jnp.where(iota((1, C), 1) < 256, pattern_at(j, 0), pattern_at(j, 1))
        s = s * m
        return h * m - sr * s, -si * s

    def split_rows(n):
        rows = slice(C + n * 64, C + n * 64 + 64)
        re, im = couple(ab_ref[0, rows, :], ab_ref[1, rows, :], n // 4)
        rows = slice(n * 64, n * 64 + 64)
        for at, value in ((0, re), (C, im)):
            high, rest = split(value)
            bhl_ref[0, rows, at : at + C] = high
            bhl_ref[1, rows, at : at + C] = rest

    def chain_start():
        for j in range(4):
            if j < 2:
                rows = pl.ds(pl.multiple_of(C + j * 256 + q * 32, 32), 32)
                re, im = couple(ab_ref[0, rows, :], ab_ref[1, rows, :], j)
            else:
                re, im = couple(lb_ref[0, j - 2], lb_ref[1, j - 2], j)
            ct_ref[0, j * 32 : j * 32 + 32, :] = re
            ct_ref[1, j * 32 : j * 32 + 32, :] = im
        times(lhs, ehl_ref, cu_ref, ct_ref[0, 0:128, :], ct_ref[1, 0:128, :], C)
        cu_ref[0, 0:128, :] += ct_ref[0, 0:128, :]
        cu_ref[1, 0:128, :] += ct_ref[1, 0:128, :]
        for jj in range(2):
            at = pl.multiple_of(jj * 256 + q * 32, 32)
            low = pl.multiple_of(jj * 256 + q * 32 + C, 32)
            eye = iota((32, C), 1) == iota((32, C), 0) + at
            rows = slice(128 + jj * 32, 160 + jj * 32)
            er = ehl_ref[0, pl.ds(at, 32), :].astype(F32) + ehl_ref[1, pl.ds(at, 32), :].astype(F32)
            ei = ehl_ref[0, pl.ds(low, 32), :].astype(F32) + ehl_ref[1, pl.ds(low, 32), :].astype(F32)
            cu_ref[0, rows, :] = jnp.where(eye, 1.0, er)
            cu_ref[1, rows, :] = ei

    def chain_two():
        times(lhs, ehl_ref, ct_ref, cu_ref[0], cu_ref[1], C)

    def chain_three():
        times(lhs, ehl_ref, ct_ref, ct_ref[0], ct_ref[1], C)
        lr, li = rotate(cu_ref[0] + ct_ref[0], cu_ref[1] + ct_ref[1], dinv_ref[0:1, :], dinv_ref[1:2, :])
        xc_ref[0] = lr[128:192]
        xc_ref[1] = li[128:192]
        put_pair(lhs, lr, li)

    def product(n):
        rows = slice(n * 256, n * 256 + 256)
        wide = dot_t(lhs[0:768, 0 : 2 * C], bhl_ref[0, rows, :])
        narrow = dot_t(lhs[0:384, 0 : 2 * C], bhl_ref[1, rows, :])
        pair = fold(wide, narrow, 192)
        for k in (0, 1):
            w_ref[k, :, rows] = pair[k][128:192]
            for b, (j, other) in enumerate(BLOCKS):
                if other == n:
                    for cc in (0, 1):
                        tb_ref[cc, b, k] = pair[k][j * 32 + cc * 16 : j * 32 + cc * 16 + 16]

    steps = [
        lambda: open_slot(2), last_rows, lambda: open_slot(0), lambda: open_slot(1), top_start,
        lambda: near(2), lambda: relay(2, 0), lambda: near(0), lambda: far(2),
        lambda: relay(2, 1), lambda: relay(2, 2), lambda: near(1), lambda: relay(0, 0),
        lambda: relay(2, 3), lambda: far(0), lambda: close_slot(2), join, top_more,
        lambda: relay(1, 0), lambda: relay(0, 1), lambda: relay(0, 2), lambda: far(1),
        lambda: relay(0, 3), lambda: relay(1, 1), last_rows_in, lambda: close_slot(0),
        lambda: scale_rows(0), lambda: scale_rows(1), lambda: relay(1, 2),
        lambda: scale_rows(2), lambda: scale_rows(3), lambda: scale_rows(4), join_more,
        lambda: scale_rows(5), lambda: scale_rows(6), lambda: scale_rows(7), lambda: relay(1, 3),
        chain_start, chain_two, chain_three, lambda: close_slot(1),
    ] + [lambda n=n: split_rows(n) for n in range(8)] + [
        lambda: product(0), lambda: product(1), join_end,
    ] + [lambda n=n: split_rows(n) for n in range(8, 16)]
    for step in steps:
        step()

    for sx_in in (0, 1):
        jx = (2 * sx_in + yl, 2 * sx_in + 1 - yl)

        @pl.when(x != 2 + sx_in)
        def _():
            for o in (0, 1):
                for k in (0, 1):
                    ref = top(k, jx[o])
                    remote(ref, ref, x0_s.at[0, o, k], x0_r.at[sx_in, o, k], xs[0]).wait_recv()

    @pl.when(root)
    def _():
        for copy in top_own:
            copy.wait()

    swaps = [
        remote(tb_ref.at[1 - c, blocks], tin_ref.at[blocks], tt_s.at[n], tt_r.at[n], sibling)
        for n, blocks in enumerate(GROUPS_DS)
    ]
    go(swaps[0])
    product(2)
    product(3)
    go(swaps[1])

    def finish(n):
        for b in range(GROUPS[n].start, GROUPS[n].stop):
            j, other = BLOCKS[b]
            s = a0_ref[1, j * 16 : j * 16 + 16, other * 256 : other * 256 + 256]
            h = a0_ref[0, j * 16 : j * 16 + 16, other * 256 : other * 256 + 256]
            own_ref[b, 0] = h - sr * s - tb_ref[c, b, 0]
            own_ref[b, 1] = -si * s - tb_ref[c, b, 1]
        swaps[n].wait_recv()
        rows = GROUPS[n]
        own_ref[rows] = own_ref[rows] - tin_ref[rows]

    def whole(n, gg):
        return sg_ref.at[GROUPS_DS[n], :, gg]

    def piece(n, gg, k):
        return sg_ref.at[GROUPS_DS[n], k, gg]

    base = (g, g + 2 - 4 * yh)
    hop = [0] + [4 * (mod4(z + d) - z) for d in (-1, 1, 2)]

    def hand(n, m, o, ref_of):
        for k in (0, 1):
            ref = piece(n, base[o] + hop[m], k)
            go(remote(ref_of(k), ref, b_s.at[n, m, o, k], b_r.at[n, m, o, k], sibling))

    def along_z(n, o, src):
        dst = whole(n, base[o])
        for d in (0, 1):
            go(remote(dst if src is None else src, dst, z_s.at[d, n, o], z_r.at[d, n, o], zs[d]))

    keeps = []
    for n in (0, 1):
        finish(n)
        src = own_ref.at[GROUPS_DS[n]]
        along_z(n, 0, src)
        go(remote(src, whole(n, g), y_s.at[n], y_r.at[n], over))
        keep = pltpu.make_async_copy(src, whole(n, g), own_sem.at[n])
        keep.start()
        keeps.append(keep)
        hand(n, 0, 0, lambda k, n=n: own_ref.at[GROUPS_DS[n], k])

    def from_over(n):
        ref = whole(n, base[1])
        remote(ref, ref, y_s.at[n], y_r.at[n], over).wait_recv()
        hand(n, 0, 1, lambda k: piece(n, base[1], k))

    def from_z(n, o):
        for d in (0, 1):
            gg = base[o] + hop[1 + d]
            ref = whole(n, gg)
            remote(ref, ref, z_s.at[d, n, o], z_r.at[d, n, o], zs[d]).wait_recv()
            ref = piece(n, gg, d)
            go(remote(ref, ref, o_s.at[n, o, d], o_r.at[n, o, d], zs[d]))
            if n == 0:
                for k in (0, 1):
                    ref = piece(n, gg, k)
                    go(remote(ref, ref, yo_s.at[1 + d, k], yo_r.at[1 + d, k], over))
            hand(n, 1 + d, o, lambda k, gg=gg: piece(n, gg, k))

    def from_far(n, o):
        gg = base[o] + hop[3]
        for k in (0, 1):
            ref = piece(n, gg, k)
            remote(ref, ref, o_s.at[n, o, k], o_r.at[n, o, k], zs[k]).wait_recv()
            if n == 0:
                go(remote(ref, ref, yo_s.at[3, k], yo_r.at[3, k], over))
            go(remote(ref, ref, b_s.at[n, 3, o, k], b_r.at[n, 3, o, k], sibling))

    def over_far(m):
        gg = base[1] + hop[m]
        for k in (0, 1):
            ref = piece(0, gg, k)
            remote(ref, ref, yo_s.at[m, k], yo_r.at[m, k], over).wait_recv()
            go(remote(ref, ref, b_s.at[0, m, 1, k], b_r.at[0, m, 1, k], sibling))

    from_z(0, 0)
    from_over(1)
    along_z(1, 1, None)
    from_over(0)
    from_far(0, 0)
    from_z(1, 0)
    over_far(1)
    over_far(2)
    from_z(1, 1)
    from_far(1, 0)
    over_far(3)
    from_far(1, 1)
    for n in (0, 1):
        for m in range(4):
            for o in (0, 1):
                gg = base[o] + hop[m] + 1 - 2 * c
                for k in (0, 1):
                    ref = piece(n, gg, k)
                    remote(ref, ref, b_s.at[n, m, o, k], b_r.at[n, m, o, k], sibling).wait_recv()
    for keep in keeps:
        keep.wait()

    def block(b, k):
        return sg_ref[b, k].reshape(256, 256)

    eye = iota((256, 256), 1) == iota((256, 256), 0)
    for j in range(4):
        rows = slice(j * 256, j * 256 + 256)
        low = slice(R + j * 256, R + j * 256 + 256)
        b = WHERE[(j, j)]
        ir, ii = recip(
            jnp.sum(jnp.where(eye, block(b, 0), 0.0), axis=1, keepdims=True),
            jnp.sum(jnp.where(eye, block(b, 1), 0.0), axis=1, keepdims=True),
        )
        d0_ref[0:1, rows] = jnp.sum(jnp.where(eye, ir, 0.0), axis=0, keepdims=True)
        d0_ref[1:2, rows] = jnp.sum(jnp.where(eye, ii, 0.0), axis=0, keepdims=True)
        for other in range(4):
            cols = slice(other * 256, other * 256 + 256)
            if (j, other) in WHERE:
                b = WHERE[(j, other)]
                re, im = block(b, 0), block(b, 1)
            else:
                b = WHERE[(other, j)]
                re, im = block(b, 0).T, block(b, 1).T
            er, ei = rotate(re, im, -ir, -ii)
            for where, value in ((rows, er), (low, ei)):
                if j == other:
                    value = jnp.where(eye, 0.0, value)
                high, rest = split(value)
                shl_ref[0, where, cols] = high
                shl_ref[1, where, cols] = rest
    times(lhs, shl_ref, u_ref, w_ref[0], w_ref[1], R)
    u_ref[0, 0:64, :] += w_ref[0]
    u_ref[1, 0:64, :] += w_ref[1]
    for j in range(4):
        at = pl.multiple_of(j * 256 + g * 16, 16)
        low = pl.multiple_of(j * 256 + g * 16 + R, 16)
        on = iota((16, R), 1) == iota((16, R), 0) + at
        rows = slice(64 + j * 16, 80 + j * 16)
        er = shl_ref[0, pl.ds(at, 16), :].astype(F32) + shl_ref[1, pl.ds(at, 16), :].astype(F32)
        ei = shl_ref[0, pl.ds(low, 16), :].astype(F32) + shl_ref[1, pl.ds(low, 16), :].astype(F32)
        u_ref[0, rows, :] = jnp.where(on, 1.0, er)
        u_ref[1, rows, :] = ei
    times(lhs, shl_ref, t_ref, u_ref[0], u_ref[1], R)
    times(lhs, shl_ref, t_ref, t_ref[0], t_ref[1], R)
    yr, yi = rotate(u_ref[0] + t_ref[0], u_ref[1] + t_ref[1], d0_ref[0:1, :], d0_ref[1:2, :])
    gw_ref[...] = wr * yr[64:128] - wi * yi[64:128]
    yr, yi = yr[0:64], yi[0:64]
    weighted = -(wr * yr - wi * yi)
    for j in range(4):
        cols = slice(j * 256, j * 256 + 256)
        m = jnp.where(iota((64, 1), 0) < 32, pattern_at(j, 0), pattern_at(j, 1))
        side = weighted[:, cols] * m
        fw_ref[:, cols] = side
        ft_ref[j] = side.T.reshape(16, 16, 64)

    for d, gg in enumerate(grids):
        go(remote(ft_ref.at[:, gg], ea_ref.at[g], a_s.at[d], a_r.at[d], (p, gg)))
    keep = pltpu.make_async_copy(ft_ref.at[:, g], ea_ref.at[g], keep_sem)
    keep.start()
    sent = []

    def send_or_keep(src, dst, ss, rs, target, here):
        away = remote(src, dst, ss, rs, target)
        stay = pltpu.make_async_copy(src, dst, ss)

        @pl.when(jnp.logical_not(here))
        def _():
            away.start()

        @pl.when(here)
        def _():
            stay.start()

        sent.append((here, away, stay))

    def child_rows(src, dst, ss, rs):
        for jj in (0, 1):
            for cc in (0, 1):
                here = jnp.logical_and(p == 2 * c + jj, c == cc)
                rows = pl.ds(jj * 32 + cc * 16, 16)
                send_or_keep(src.at[rows, :], dst.at[p], ss.at[jj, cc], rs.at[p], (2 * c + jj, 2 * q + cc), here)

    for j in range(4):
        send_or_keep(gw_ref.at[pl.ds(j * 16, 16), :], rf_ref.at[p], sg_s.at[j], sf_r.at[p], (4 + j, g), p == 4 + j)
    child_rows(fw_ref, rf_ref, sf_s, sf_r)

    rh, rl = split(yr)
    ih, il = split(yi)
    for at, (re, im) in enumerate(((rh, ih), (rl, il))):
        lhs[at * 128 : at * 128 + 64, 0:R] = re
        lhs[at * 128 + 64 : at * 128 + 128, 0:R] = im
        lhs[at * 128 : at * 128 + 64, R : 2 * R] = -im
        lhs[at * 128 + 64 : at * 128 + 128, R : 2 * R] = re
    wide = dot(lhs[0:256, 0:R], bhl_ref[0, :, 0:C]) + dot(lhs[0:256, R : 2 * R], bhl_ref[0, :, C : 2 * C])
    narrow = dot(lhs[0:128, 0:R], bhl_ref[1, :, 0:C]) + dot(lhs[0:128, R : 2 * R], bhl_ref[1, :, C : 2 * C])
    pr, pi = fold(wide, narrow, 64)

    keep.wait()
    for d in range(15):
        gg = lax.rem(g + 15 - d, 16)
        remote(ea_ref.at[gg], ea_ref.at[gg], a_s.at[d], a_r.at[d], (p, grids[0])).wait_recv()
    for j in range(4):
        send_or_keep(ea_ref.at[:, j], re_ref.at[p], se_s.at[j], se_r.at[p], (4 + j, g), p == 4 + j)

    times(lhs, ehl_ref, k_ref, pr, pi, C)
    ku_ref[0] = k_ref[0] + pr
    ku_ref[1] = k_ref[1] + pi
    times(lhs, ehl_ref, k_ref, ku_ref[0], ku_ref[1], C)
    times(lhs, ehl_ref, k_ref, k_ref[0], k_ref[1], C)
    zr, zi = rotate(ku_ref[0] + k_ref[0], ku_ref[1] + k_ref[1], dinv_ref[0:1, :], dinv_ref[1:2, :])
    dw_ref[...] = wr * (xc_ref[0] + zr) - wi * (xc_ref[1] + zi)
    child_rows(dw_ref, rd_ref, sd_s, sd_r)

    for here, away, stay in sent:

        @pl.when(jnp.logical_not(here))
        def _():
            away.wait_send()

        @pl.when(here)
        def _():
            stay.wait()

    lead = p >= 4
    same = jnp.logical_or(lead, c == half(p))
    for d in range(8):
        pp = poles[d]

        @pl.when(jnp.logical_or(jnp.logical_not(same), d > 0))
        def _():
            remote(rf_ref.at[pp], rf_ref.at[pp], sf_s.at[0, 0], sf_r.at[pp], partner).wait_recv()

        @pl.when(jnp.logical_and(jnp.logical_not(lead), jnp.logical_or(jnp.logical_not(same), d > 0)))
        def _():
            remote(rd_ref.at[pp], rd_ref.at[pp], sd_s.at[0, 0], sd_r.at[pp], partner).wait_recv()

    def total(ref):
        value = ref[0]
        for n in range(1, 8):
            value = value + ref[n]
        return value

    out_ref[:, R : 2 * R] = total(rf_ref)

    @pl.when(lead)
    def _():
        for d in range(1, 8):
            pp = poles[d]
            remote(re_ref.at[pp], re_ref.at[pp], se_s.at[0], se_r.at[pp], partner).wait_recv()
        side = total(re_ref)
        for k in (0, 1):
            for jj in (0, 1):
                cols = [side[2 * qq + k][:, jj * 32 : jj * 32 + 32] for qq in range(8)]
                at = k * 512 + jj * 256
                out_ref[:, at : at + 256] = jnp.concatenate(cols, axis=1)

    @pl.when(jnp.logical_not(lead))
    def _():
        diag = total(rd_ref)
        upper = p < 2
        out_ref[:, 0:C] = jnp.where(upper, diag, 0.0)
        out_ref[:, C : 2 * C] = jnp.where(upper, 0.0, diag)

    for copy in pending:
        copy.wait_send()

    for when, here, away in gifts:

        @pl.when(when)
        def _():
            for copy in away:
                copy.wait_send()

    @pl.when(root)
    def _():
        for copy in top_y + top_x + top_x2:
            copy.wait_send()


GROUPS_DS = tuple(pl.ds(blocks.start, blocks.stop - blocks.start) for blocks in GROUPS)


def local(hamiltonian, margin, pattern, shift_real, shift_imag, residue):
    dma = pltpu.SemaphoreType.DMA
    vm = pltpu.VMEM
    return pl.pallas_call(
        kernel,
        name="selected_inversion",
        out_shape=jax.ShapeDtypeStruct((16, 2 * R), F32),
        in_specs=[VM, VM, SM, SM, SM, SM],
        out_specs=VM,
        scratch_shapes=[
            vm((2, 16, 2 * R), F32), vm((2, 1536, 512), F32), vm((2, 2, 32, 512), F32), vm((2, 64, 1024), F32), vm((2, 1024, C), BF16), vm((2, R, 2 * C), BF16),
            vm((8, C), F32), vm((768, 2 * R), BF16), vm((2, 192, C), F32), vm((2, 192, C), F32),
            vm((2, 64, C), F32), vm((2, 64, R), F32), vm((2, NB, 2, 16, 256), F32),
            vm((NB, 2, 16, 256), F32), vm((NB, 2, 16, 256), F32), vm((NB, 2, 16, 16, 256), F32),
            vm((2, 2 * R, R), BF16), vm((8, R), F32), vm((2, 128, R), F32), vm((2, 128, R), F32),
            vm((2, 64, C), F32), vm((2, 64, C), F32), vm((64, R), F32), vm((4, 16, 16, 64), F32),
            vm((64, R), F32), vm((64, C), F32),
            vm((8, 16, R), F32), vm((8, 16, C), F32), vm((8, 16, 16, 64), F32), vm((16, 4, 16, 64), F32),
            dma((6,)), dma((4, 2)), dma((3, 2)),
            dma((2, 3)), dma((2, 3)), dma((3, 2)), dma((3, 2)),
            dma((2, 3, 4)), dma((2, 3, 4)), dma((3, 4, 2)), dma((3, 4, 2)),
            dma, dma, dma((2,)), dma((2,)), dma((2,)), dma((2,)),
            dma((2,)), dma((2,)), dma((3, 2, 2)), dma((2, 2, 2)),
            dma((2,)), dma((2,)), dma((2,)), dma((2,)), dma((2,)), dma((4, 2)), dma((4, 2)),
            dma((2, 2, 2)), dma((2, 2, 2)), dma((2, 2, 2)), dma((2, 2, 2)),
            dma((2, 4, 2, 2)), dma((2, 4, 2, 2)),
            dma, dma((15,)), dma((15,)), dma((2, 2)), dma((8,)), dma((2, 2)), dma((8,)),
            dma((4,)), dma((4,)), dma((8,)),
        ],
        compiler_params=pltpu.CompilerParams(
            collective_id=0, has_side_effects=True, vmem_limit_bytes=56 << 20
        ),
        cost_estimate=pl.CostEstimate(flops=12 << 30, bytes_accessed=1 << 20, transcendentals=0),
    )(hamiltonian, margin, pattern, shift_real, shift_imag, residue)


def solution(mesh):
    return jax.shard_map(
        local,
        mesh=mesh,
        in_specs=(
            P(("pole", "grid"), None),
            P(("pole", "grid"), None),
            P(),
            P("pole"),
            P("pole"),
            P("pole", None),
        ),
        out_specs=P(("pole", "grid"), None),
        check_vma=False,
    )
```

```python
import jax
import jax.numpy as jnp
from jax import lax
from jax.experimental import pallas as pl
from jax.experimental.pallas import tpu as pltpu
from jax.sharding import PartitionSpec as P

C = 512
R = 1024
F32 = jnp.float32
BF16 = jnp.bfloat16
MESH = pl.DeviceIdType.MESH
VM = pl.BlockSpec(memory_space=pltpu.VMEM)
SM = pl.BlockSpec(memory_space=pltpu.SMEM)
BLOCKS = ((0, 0), (3, 0), (0, 1), (1, 1), (0, 2), (1, 2), (2, 2), (1, 3), (2, 3), (3, 3))
WHERE = {pair: b for b, pair in enumerate(BLOCKS)}
NB = len(BLOCKS)
GROUPS = (slice(0, 4), slice(4, 10))


def mod4(v):
    return lax.rem(v + 4, 4)


def half(v):
    return lax.div(v, 2)


def place():
    p = lax.axis_index("pole")
    g = lax.axis_index("grid")
    x, yl = half(p), lax.rem(p, 2)
    z, q, c = lax.div(g, 4), half(g), lax.rem(g, 2)
    return p, g, x, yl, z, lax.rem(q, 2), q, c


def spot(x, y, z, c):
    return (2 * x + lax.rem(y, 2), 4 * z + 2 * half(y) + c)


def greet(devices):
    barrier = pltpu.get_barrier_semaphore()
    for device in devices:
        pl.semaphore_signal(barrier, inc=1, device_id=device, device_id_type=MESH)
    pl.semaphore_wait(barrier, len(devices))


def remote(src, dst, send, recv, device):
    return pltpu.make_async_remote_copy(
        src_ref=src, dst_ref=dst, send_sem=send, recv_sem=recv, device_id=device, device_id_type=MESH
    )


def split(v):
    high = v.astype(BF16)
    return high, (v - high.astype(F32)).astype(BF16)


def put_pair(lhs_ref, vr, vi, start=0):
    m, k = vr.shape
    rh, rl = split(vr)
    ih, il = split(vi)
    for at, (re, im) in enumerate(((rh, ih), (rl, il))):
        base = start + at * 2 * m
        lhs_ref[base : base + m, 0:k] = re
        lhs_ref[base : base + m, k : 2 * k] = -im
        lhs_ref[base + m : base + 2 * m, 0:k] = im
        lhs_ref[base + m : base + 2 * m, k : 2 * k] = re


def fold(wide, narrow, m):
    total = wide[0 : 2 * m] + wide[2 * m : 4 * m] + narrow
    return total[0:m], total[m : 2 * m]


def dot(a, b):
    return jnp.dot(a, b, preferred_element_type=F32)


def dot_t(a, b):
    return lax.dot_general(a, b, (((1,), (1,)), ((), ())), preferred_element_type=F32)


def times(lhs_ref, rhs_ref, out_ref, vr, vi, width):
    m, k = vr.shape
    put_pair(lhs_ref, vr, vi)
    for n in range(width // 256):
        cols = slice(n * 256, n * 256 + 256)
        wide = dot(lhs_ref[0 : 4 * m, 0 : 2 * k], rhs_ref[0, :, cols])
        narrow = dot(lhs_ref[0 : 2 * m, 0 : 2 * k], rhs_ref[1, :, cols])
        re, im = fold(wide, narrow, m)
        out_ref[0, 0:m, cols] = re
        out_ref[1, 0:m, cols] = im


def rotate(vr, vi, dr, di):
    return vr * dr - vi * di, vr * di + vi * dr


def recip(dr, di):
    den = dr * dr + di * di
    return dr / den, -di / den


def iota(shape, dim):
    return lax.broadcasted_iota(jnp.int32, shape, dim)


def kernel(
    h_ref, s_ref, pat_ref, sr_ref, si_ref, res_ref, left_ref, right_ref,
    hs_ref, ab_ref, a0_ref, ehl_ref, bhl_ref, dinv_ref, lhs, cu_ref, ct_ref, xc_ref, w_ref, tb_ref,
    tin_ref, own_ref, sg_ref, shl_ref, d0_ref, u_ref, t_ref,
    k_ref, ku_ref, fw_ref, ft_ref, gw_ref, dw_ref, rf_ref, rd_ref, re_ref, ea_ref,
    loc_sem, x_s, x_r, f_s, f_r, fo_s, fo_r, g_s, g_r, go_s, go_r,
    y0_s, y0_r, x0_s, x0_r,
    tt_s, tt_r, own_sem, y_s, y_r, yo_s, yo_r, z_s, z_r, o_s, o_r, b_s, b_r,
    keep_sem, a_s, a_r, sf_s, sf_r, sd_s, sd_r, sg_s, se_s, se_r,
):
    p, g, x, yl, z, yh, q, c = place()
    y = 2 * yh + yl
    sr, si = sr_ref[0], si_ref[0]
    wr, wi = res_ref[0, 0], res_ref[0, 1]
    sib = g + 1 - 2 * c
    sibling = (p, sib)
    partner = (p + 1 - 2 * yl, g)
    over = (p, g + 2 - 4 * yh)
    xs = [spot(mod4(x + d), y, z, c) for d in (1, 2, 3)]
    ys = [spot(x, mod4(y + d), z, c) for d in (1, -1)]
    zs = [spot(x, y, mod4(z + d), c) for d in (1, -1)]
    poles = [lax.rem(p + d, 8) for d in range(8)]
    grids = [lax.rem(g + d, 16) for d in range(1, 16)]
    peers = [[spot(mod4(x + d), y, z, cc) for cc in (c, 1 - c)] for d in range(4)]
    hs_ref[0] = h_ref[...]
    hs_ref[1] = s_ref[...]
    greet([peers[d][e] for d in range(4) for e in (0, 1) if d + e > 0] + ys + zs)

    pending = []

    def go(copy):
        copy.start()
        pending.append(copy)

    first = c == 0

    def pick(a, b):
        return tuple(jnp.where(first, u, v) for u, v in zip(a, b))

    fs = [pick(ys[i], zs[i]) for i in (0, 1)]
    gs = [pick(zs[i], ys[i]) for i in (0, 1)]
    f0 = jnp.where(first, y, z)
    g0 = jnp.where(first, z, y)

    def row(slot, f, s):
        yy, zz = jnp.where(first, f, s), jnp.where(first, s, f)
        return pl.multiple_of(slot * 512 + lax.rem(yy, 2) * 256 + (2 * zz + half(yy)) * 32, 32)

    def slab(slot, f, s):
        return ab_ref.at[:, pl.ds(row(slot, f, s), 32), :]

    def part(slot, f, s, k):
        return ab_ref.at[k, pl.ds(row(slot, f, s), 32), :]

    root = x >= 2

    def land(slot, cc):
        return ab_ref.at[:, pl.ds(pl.multiple_of(slot * 512 + yl * 256 + q * 32 + cc * 16, 16), 16), :]

    def child_cols(k):
        return hs_ref.at[:, :, pl.ds(pl.multiple_of(k * 512, 128), 512)]

    def stay_put(slot):
        return pltpu.make_async_copy(child_cols(c), land(slot, c), loc_sem.at[slot])

    def give(slot, d, e):
        return remote(
            child_cols(c if e == 0 else 1 - c), land(slot, c), x_s.at[d, e], x_r.at[slot, e], peers[d][e]
        )

    def givers(slot):
        if slot > 0:
            away = [give(slot, d, e) for d in range(4) for e in (0, 1) if d + e > 0]
            return [(x == slot + 1, [stay_put(slot)], away)]
        return [
            (jnp.logical_and(x < 2, x == c), [stay_put(0)], [give(0, d, 0) for d in (1, 2, 3)]),
            (jnp.logical_and(x < 2, x != c), [], [give(0, d, 1) for d in range(4)]),
        ]

    gifts = givers(0) + givers(1) + givers(2)
    for when, here, away in gifts:

        @pl.when(when)
        def _():
            for copy in away + here:
                copy.start()

    def taken(slot):
        source = jnp.where(slot == 0, c, slot + 1)
        remote(land(slot, 1 - c), land(slot, 1 - c), x_s.at[1, 1], x_r.at[slot, 1], peers[1][1]).wait_recv()

        @pl.when(x != source)
        def _():
            remote(land(slot, c), land(slot, c), x_s.at[1, 0], x_r.at[slot, 0], peers[1][0]).wait_recv()

        @pl.when(x == source)
        def _():
            stay_put(slot).wait()

    sx = jnp.maximum(x - 2, 0)
    j0 = 2 * sx + yl
    j1 = 2 * sx + 1 - yl

    def top(k, j):
        return a0_ref.at[k, pl.ds(pl.multiple_of(j * 16, 16), 16), :]

    top_src = [hs_ref.at[k, :, pl.ds(1024, 1024)] for k in (0, 1)]
    top_own = [pltpu.make_async_copy(top_src[k], top(k, j0), loc_sem.at[3 + k]) for k in (0, 1)]
    top_y = [remote(top_src[k], top(k, j0), y0_s.at[k], y0_r.at[k], partner) for k in (0, 1)]
    top_y_in = [remote(top_src[k], top(k, j1), y0_s.at[k], y0_r.at[k], partner) for k in (0, 1)]
    top_x = [
        remote(top_src[k], top(k, j0), x0_s.at[n, 0, k], x0_r.at[sx, 0, k], xs[n]) for n in range(3) for k in (0, 1)
    ]
    top_x2 = [
        remote(top(k, j1), top(k, j1), x0_s.at[n, 1, k], x0_r.at[sx, 1, k], xs[n]) for n in range(3) for k in (0, 1)
    ]

    f_at = (f0, mod4(f0 - 1), mod4(f0 + 1), mod4(f0 + 2))
    g_at = (mod4(g0 - 1), mod4(g0 + 1), mod4(g0 + 2))

    def spread(slot, n):
        ref = slab(slot, f_at[n], g0)
        for d in (0, 1):
            go(remote(ref, ref, g_s.at[d, slot, n], g_r.at[d, slot, n], gs[d]))

    def open_slot(slot):
        taken(slot)
        for d in (0, 1):
            ref = slab(slot, f0, g0)
            go(remote(ref, ref, f_s.at[d, slot], f_r.at[d, slot], fs[d]))
        spread(slot, 0)

    def near(slot):
        for d in (0, 1):
            ref = slab(slot, f_at[1 + d], g0)
            remote(ref, ref, f_s.at[d, slot], f_r.at[d, slot], fs[d]).wait_recv()
            ref = part(slot, f_at[1 + d], g0, d)
            go(remote(ref, ref, fo_s.at[slot, d], fo_r.at[slot, d], fs[d]))
            spread(slot, 1 + d)

    def far(slot):
        for d in (0, 1):
            ref = part(slot, f_at[3], g0, d)
            remote(ref, ref, fo_s.at[slot, d], fo_r.at[slot, d], fs[d]).wait_recv()
        spread(slot, 3)

    def relay(slot, n):
        for d in (0, 1):
            ref = slab(slot, f_at[n], g_at[d])
            remote(ref, ref, g_s.at[d, slot, n], g_r.at[d, slot, n], gs[d]).wait_recv()
            ref = part(slot, f_at[n], g_at[d], d)
            go(remote(ref, ref, go_s.at[slot, n, d], go_r.at[slot, n, d], gs[d]))

    def close_slot(slot):
        for n in range(4):
            for d in (0, 1):
                ref = part(slot, f_at[n], g_at[2], d)
                remote(ref, ref, go_s.at[slot, n, d], go_r.at[slot, n, d], gs[d]).wait_recv()

    def top_start():
        @pl.when(root)
        def _():
            for copy in top_y + top_own + top_x:
                copy.start()

    def top_more():
        @pl.when(root)
        def _():
            for k in (0, 1):
                top_y_in[k].wait_recv()
            for copy in top_x2:
                copy.start()

    dinv_ref[...] = jnp.zeros_like(dinv_ref)

    def scale_rows(n):
        rows = slice(n * 64, n * 64 + 64)
        low = slice(n * 64 + C, n * 64 + C + 64)
        s = ab_ref[1, rows, :]
        re = ab_ref[0, rows, :] - sr * s
        im = -si * s
        eye = iota((64, C), 1) == iota((64, C), 0) + n * 64
        ir, ii = recip(
            jnp.sum(jnp.where(eye, re, 0.0), axis=1, keepdims=True),
            jnp.sum(jnp.where(eye, im, 0.0), axis=1, keepdims=True),
        )
        dinv_ref[0:1, :] += jnp.sum(jnp.where(eye, ir, 0.0), axis=0, keepdims=True)
        dinv_ref[1:2, :] += jnp.sum(jnp.where(eye, ii, 0.0), axis=0, keepdims=True)
        er, ei = rotate(re, im, -ir, -ii)
        for where, value in ((rows, er), (low, ei)):
            high, rest = split(jnp.where(eye, 0.0, value))
            ehl_ref[0, where, :] = high
            ehl_ref[1, where, :] = rest

    def pattern_at(j, half_at):
        return jnp.where(first, pat_ref[j, half_at], pat_ref[j, 2 + half_at]).astype(F32)

    def couple(h, s, j):
        m = jnp.where(iota((1, C), 1) < 256, pattern_at(j, 0), pattern_at(j, 1))
        s = s * m
        return h * m - sr * s, -si * s

    def split_rows(n):
        rows = slice(C + n * 64, C + n * 64 + 64)
        re, im = couple(ab_ref[0, rows, :], ab_ref[1, rows, :], n // 4)
        rows = slice(n * 64, n * 64 + 64)
        for at, value in ((0, re), (C, im)):
            high, rest = split(value)
            bhl_ref[0, rows, at : at + C] = high
            bhl_ref[1, rows, at : at + C] = rest

    def chain_start():
        for j in range(4):
            rows = pl.ds(pl.multiple_of(C + j * 256 + q * 32, 32), 32)
            re, im = couple(ab_ref[0, rows, :], ab_ref[1, rows, :], j)
            ct_ref[0, j * 32 : j * 32 + 32, :] = re
            ct_ref[1, j * 32 : j * 32 + 32, :] = im
        times(lhs, ehl_ref, cu_ref, ct_ref[0, 0:128, :], ct_ref[1, 0:128, :], C)
        cu_ref[0, 0:128, :] += ct_ref[0, 0:128, :]
        cu_ref[1, 0:128, :] += ct_ref[1, 0:128, :]
        for jj in range(2):
            at = pl.multiple_of(jj * 256 + q * 32, 32)
            low = pl.multiple_of(jj * 256 + q * 32 + C, 32)
            eye = iota((32, C), 1) == iota((32, C), 0) + at
            rows = slice(128 + jj * 32, 160 + jj * 32)
            er = ehl_ref[0, pl.ds(at, 32), :].astype(F32) + ehl_ref[1, pl.ds(at, 32), :].astype(F32)
            ei = ehl_ref[0, pl.ds(low, 32), :].astype(F32) + ehl_ref[1, pl.ds(low, 32), :].astype(F32)
            cu_ref[0, rows, :] = jnp.where(eye, 1.0, er)
            cu_ref[1, rows, :] = ei

    def chain_two():
        times(lhs, ehl_ref, ct_ref, cu_ref[0], cu_ref[1], C)

    def chain_three():
        times(lhs, ehl_ref, ct_ref, ct_ref[0], ct_ref[1], C)
        lr, li = rotate(cu_ref[0] + ct_ref[0], cu_ref[1] + ct_ref[1], dinv_ref[0:1, :], dinv_ref[1:2, :])
        xc_ref[0] = lr[128:192]
        xc_ref[1] = li[128:192]
        put_pair(lhs, lr[0:128], li[0:128])
        put_pair(lhs, lr[128:192], li[128:192], 512)

    def product(n):
        rows = slice(n * 256, n * 256 + 256)
        wide = dot_t(lhs[0:512, 0 : 2 * C], bhl_ref[0, rows, :])
        narrow = dot_t(lhs[0:256, 0 : 2 * C], bhl_ref[1, rows, :])
        pair = fold(wide, narrow, 128)
        for k in (0, 1):
            for b, (j, other) in enumerate(BLOCKS):
                if other == n:
                    for cc in (0, 1):
                        tb_ref[cc, b, k] = pair[k][j * 32 + cc * 16 : j * 32 + cc * 16 + 16]

    def product_w(n):
        rows = slice(n * 256, n * 256 + 256)
        wide = dot_t(lhs[512:768, 0 : 2 * C], bhl_ref[0, rows, :])
        narrow = dot_t(lhs[512:640, 0 : 2 * C], bhl_ref[1, rows, :])
        w_ref[0, :, rows], w_ref[1, :, rows] = fold(wide, narrow, 64)

    order = (jnp.maximum(x - 1, 0), jnp.where(x < 2, 1, 0), jnp.where(x == 3, 1, 2))

    def turn(stage, o, *more):
        return lambda: stage(order[o], *more)

    steps = [
        turn(open_slot, 0), turn(near, 0), turn(relay, 0, 0), turn(far, 0),
        turn(open_slot, 1), turn(open_slot, 2), top_start,
        turn(relay, 0, 1), turn(relay, 0, 2), turn(near, 1), turn(relay, 0, 3), turn(relay, 1, 0),
        turn(near, 2), turn(far, 1), turn(relay, 2, 0), turn(relay, 1, 1), turn(relay, 1, 2), top_more,
        turn(far, 2), turn(relay, 1, 3), turn(close_slot, 0), turn(close_slot, 1),
        lambda: scale_rows(0), lambda: scale_rows(1), turn(relay, 2, 1),
        lambda: scale_rows(2), lambda: scale_rows(3), turn(relay, 2, 2),
        lambda: scale_rows(4), lambda: scale_rows(5), lambda: scale_rows(6), turn(relay, 2, 3),
        lambda: scale_rows(7), chain_start, chain_two, chain_three, turn(close_slot, 2),
    ] + [lambda n=n: split_rows(n) for n in range(16)]
    for step in steps:
        step()

    for sx_in in (0, 1):
        jx = (2 * sx_in + yl, 2 * sx_in + 1 - yl)

        @pl.when(x != 2 + sx_in)
        def _():
            for o in (0, 1):
                for k in (0, 1):
                    ref = top(k, jx[o])
                    remote(ref, ref, x0_s.at[0, o, k], x0_r.at[sx_in, o, k], xs[0]).wait_recv()

    @pl.when(root)
    def _():
        for copy in top_own:
            copy.wait()

    swaps = [
        remote(tb_ref.at[1 - c, blocks], tin_ref.at[blocks], tt_s.at[n], tt_r.at[n], sibling)
        for n, blocks in enumerate(GROUPS_DS)
    ]
    def finish(n):
        for b in range(GROUPS[n].start, GROUPS[n].stop):
            j, other = BLOCKS[b]
            s = a0_ref[1, j * 16 : j * 16 + 16, other * 256 : other * 256 + 256]
            h = a0_ref[0, j * 16 : j * 16 + 16, other * 256 : other * 256 + 256]
            own_ref[b, 0] = h - sr * s - tb_ref[c, b, 0]
            own_ref[b, 1] = -si * s - tb_ref[c, b, 1]
        swaps[n].wait_recv()
        rows = GROUPS[n]
        own_ref[rows] = own_ref[rows] - tin_ref[rows]

    def whole(n, gg):
        return sg_ref.at[GROUPS_DS[n], :, gg]

    def piece(n, gg, k):
        return sg_ref.at[GROUPS_DS[n], k, gg]

    base = (g, g + 2 - 4 * yh)
    hop = [0] + [4 * (mod4(z + d) - z) for d in (-1, 1, 2)]

    def hand(n, m, o, ref_of):
        for k in (0, 1):
            ref = piece(n, base[o] + hop[m], k)
            go(remote(ref_of(k), ref, b_s.at[n, m, o, k], b_r.at[n, m, o, k], sibling))

    def along_z(n, o, src):
        dst = whole(n, base[o])
        for d in (0, 1):
            go(remote(dst if src is None else src, dst, z_s.at[d, n, o], z_r.at[d, n, o], zs[d]))

    keeps = []

    def launch(n):
        finish(n)
        src = own_ref.at[GROUPS_DS[n]]
        if n == 0:
            along_z(n, 0, src)
        go(remote(src, whole(n, g), y_s.at[n], y_r.at[n], over))
        if n == 1:
            along_z(n, 0, src)
        keep = pltpu.make_async_copy(src, whole(n, g), own_sem.at[n])
        keep.start()
        keeps.append(keep)
        hand(n, 0, 0, lambda k: own_ref.at[GROUPS_DS[n], k])

    def from_over(n):
        ref = whole(n, base[1])
        remote(ref, ref, y_s.at[n], y_r.at[n], over).wait_recv()
        hand(n, 0, 1, lambda k: piece(n, base[1], k))

    def from_z(n, o):
        for d in (0, 1):
            gg = base[o] + hop[1 + d]
            ref = whole(n, gg)
            remote(ref, ref, z_s.at[d, n, o], z_r.at[d, n, o], zs[d]).wait_recv()
            ref = piece(n, gg, d)
            go(remote(ref, ref, o_s.at[n, o, d], o_r.at[n, o, d], zs[d]))
            if n == 0:
                for k in (0, 1):
                    ref = piece(n, gg, k)
                    go(remote(ref, ref, yo_s.at[1 + d, k], yo_r.at[1 + d, k], over))
            hand(n, 1 + d, o, lambda k, gg=gg: piece(n, gg, k))

    def from_far(n, o):
        gg = base[o] + hop[3]
        for k in (0, 1):
            ref = piece(n, gg, k)
            remote(ref, ref, o_s.at[n, o, k], o_r.at[n, o, k], zs[k]).wait_recv()
            if n == 0:
                go(remote(ref, ref, yo_s.at[3, k], yo_r.at[3, k], over))
            go(remote(ref, ref, b_s.at[n, 3, o, k], b_r.at[n, 3, o, k], sibling))

    def over_far(m):
        gg = base[1] + hop[m]
        for k in (0, 1):
            ref = piece(0, gg, k)
            remote(ref, ref, yo_s.at[m, k], yo_r.at[m, k], over).wait_recv()
            go(remote(ref, ref, b_s.at[0, m, 1, k], b_r.at[0, m, 1, k], sibling))

    product(0)
    product(1)
    go(swaps[0])
    product(2)
    launch(0)
    product(3)
    go(swaps[1])
    product_w(0)
    launch(1)
    from_z(0, 0)
    product_w(1)
    from_over(1)
    along_z(1, 1, None)
    from_over(0)
    product_w(2)
    product_w(3)
    from_far(0, 0)
    from_z(1, 0)
    over_far(1)
    over_far(2)
    from_z(1, 1)
    from_far(1, 0)
    over_far(3)
    from_far(1, 1)
    for n in (0, 1):
        for m in range(4):
            for o in (0, 1):
                gg = base[o] + hop[m] + 1 - 2 * c
                for k in (0, 1):
                    ref = piece(n, gg, k)
                    remote(ref, ref, b_s.at[n, m, o, k], b_r.at[n, m, o, k], sibling).wait_recv()
    for keep in keeps:
        keep.wait()

    def block(b, k):
        return sg_ref[b, k].reshape(256, 256)

    eye = iota((256, 256), 1) == iota((256, 256), 0)
    for j in range(4):
        rows = slice(j * 256, j * 256 + 256)
        low = slice(R + j * 256, R + j * 256 + 256)
        b = WHERE[(j, j)]
        ir, ii = recip(
            jnp.sum(jnp.where(eye, block(b, 0), 0.0), axis=1, keepdims=True),
            jnp.sum(jnp.where(eye, block(b, 1), 0.0), axis=1, keepdims=True),
        )
        d0_ref[0:1, rows] = jnp.sum(jnp.where(eye, ir, 0.0), axis=0, keepdims=True)
        d0_ref[1:2, rows] = jnp.sum(jnp.where(eye, ii, 0.0), axis=0, keepdims=True)
        for other in range(4):
            cols = slice(other * 256, other * 256 + 256)
            if (j, other) in WHERE:
                b = WHERE[(j, other)]
                re, im = block(b, 0), block(b, 1)
            else:
                b = WHERE[(other, j)]
                re, im = block(b, 0).T, block(b, 1).T
            er, ei = rotate(re, im, -ir, -ii)
            for where, value in ((rows, er), (low, ei)):
                if j == other:
                    value = jnp.where(eye, 0.0, value)
                high, rest = split(value)
                shl_ref[0, where, cols] = high
                shl_ref[1, where, cols] = rest
    times(lhs, shl_ref, u_ref, w_ref[0], w_ref[1], R)
    u_ref[0, 0:64, :] += w_ref[0]
    u_ref[1, 0:64, :] += w_ref[1]
    for j in range(4):
        at = pl.multiple_of(j * 256 + g * 16, 16)
        low = pl.multiple_of(j * 256 + g * 16 + R, 16)
        on = iota((16, R), 1) == iota((16, R), 0) + at
        rows = slice(64 + j * 16, 80 + j * 16)
        er = shl_ref[0, pl.ds(at, 16), :].astype(F32) + shl_ref[1, pl.ds(at, 16), :].astype(F32)
        ei = shl_ref[0, pl.ds(low, 16), :].astype(F32) + shl_ref[1, pl.ds(low, 16), :].astype(F32)
        u_ref[0, rows, :] = jnp.where(on, 1.0, er)
        u_ref[1, rows, :] = ei
    times(lhs, shl_ref, t_ref, u_ref[0], u_ref[1], R)
    times(lhs, shl_ref, t_ref, t_ref[0], t_ref[1], R)
    yr, yi = rotate(u_ref[0] + t_ref[0], u_ref[1] + t_ref[1], d0_ref[0:1, :], d0_ref[1:2, :])
    gw_ref[...] = wr * yr[64:128] - wi * yi[64:128]
    yr, yi = yr[0:64], yi[0:64]
    weighted = -(wr * yr - wi * yi)
    for j in range(4):
        cols = slice(j * 256, j * 256 + 256)
        m = jnp.where(iota((64, 1), 0) < 32, pattern_at(j, 0), pattern_at(j, 1))
        side = weighted[:, cols] * m
        fw_ref[:, cols] = side
        turned = side.T.reshape(16, 2, 8, 64)
        ft_ref[j] = jnp.concatenate([turned[:, 0], turned[:, 1]], axis=2)

    for d, gg in enumerate(grids):
        go(remote(ft_ref.at[:, gg], ea_ref.at[g], a_s.at[d], a_r.at[d], (p, gg)))
    keep = pltpu.make_async_copy(ft_ref.at[:, g], ea_ref.at[g], keep_sem)
    keep.start()
    sent = []

    def send_or_keep(src, dst, ss, rs, target, here):
        away = remote(src, dst, ss, rs, target)
        stay = pltpu.make_async_copy(src, dst, ss)

        @pl.when(jnp.logical_not(here))
        def _():
            away.start()

        @pl.when(here)
        def _():
            stay.start()

        sent.append((here, away, stay))

    def child_rows(src, dst, ss, rs):
        for jj in (0, 1):
            for cc in (0, 1):
                here = jnp.logical_and(p == 2 * c + jj, c == cc)
                rows = pl.ds(jj * 32 + cc * 16, 16)
                send_or_keep(src.at[rows, :], dst.at[p], ss.at[jj, cc], rs.at[p], (2 * c + jj, 2 * q + cc), here)

    for j in range(4):
        send_or_keep(gw_ref.at[pl.ds(j * 16, 16), :], rf_ref.at[p], sg_s.at[j], sf_r.at[p], (4 + j, g), p == 4 + j)
    child_rows(fw_ref, rf_ref, sf_s, sf_r)

    rh, rl = split(yr)
    ih, il = split(yi)
    for at, (re, im) in enumerate(((rh, ih), (rl, il))):
        lhs[at * 128 : at * 128 + 64, 0:R] = re
        lhs[at * 128 + 64 : at * 128 + 128, 0:R] = im
        lhs[at * 128 : at * 128 + 64, R : 2 * R] = -im
        lhs[at * 128 + 64 : at * 128 + 128, R : 2 * R] = re
    wide = dot(lhs[0:256, 0:R], bhl_ref[0, :, 0:C]) + dot(lhs[0:256, R : 2 * R], bhl_ref[0, :, C : 2 * C])
    narrow = dot(lhs[0:128, 0:R], bhl_ref[1, :, 0:C]) + dot(lhs[0:128, R : 2 * R], bhl_ref[1, :, C : 2 * C])
    pr, pi = fold(wide, narrow, 64)

    keep.wait()
    for d in range(15):
        gg = lax.rem(g + 15 - d, 16)
        remote(ea_ref.at[gg], ea_ref.at[gg], a_s.at[d], a_r.at[d], (p, grids[0])).wait_recv()
    for j in range(4):
        send_or_keep(ea_ref.at[:, j], re_ref.at[p], se_s.at[j], se_r.at[p], (4 + j, g), p == 4 + j)

    times(lhs, ehl_ref, k_ref, pr, pi, C)
    ku_ref[0] = k_ref[0] + pr
    ku_ref[1] = k_ref[1] + pi
    times(lhs, ehl_ref, k_ref, ku_ref[0], ku_ref[1], C)
    times(lhs, ehl_ref, k_ref, k_ref[0], k_ref[1], C)
    zr, zi = rotate(ku_ref[0] + k_ref[0], ku_ref[1] + k_ref[1], dinv_ref[0:1, :], dinv_ref[1:2, :])
    dw_ref[...] = wr * (xc_ref[0] + zr) - wi * (xc_ref[1] + zi)
    child_rows(dw_ref, rd_ref, sd_s, sd_r)

    for here, away, stay in sent:

        @pl.when(jnp.logical_not(here))
        def _():
            away.wait_send()

        @pl.when(here)
        def _():
            stay.wait()

    lead = p >= 4
    same = jnp.logical_or(lead, c == half(p))
    for d in range(8):
        pp = poles[d]

        @pl.when(jnp.logical_or(jnp.logical_not(same), d > 0))
        def _():
            remote(rf_ref.at[pp], rf_ref.at[pp], sf_s.at[0, 0], sf_r.at[pp], partner).wait_recv()

        @pl.when(jnp.logical_and(jnp.logical_not(lead), jnp.logical_or(jnp.logical_not(same), d > 0)))
        def _():
            remote(rd_ref.at[pp], rd_ref.at[pp], sd_s.at[0, 0], sd_r.at[pp], partner).wait_recv()

    def total(ref):
        value = ref[0]
        for n in range(1, 8):
            value = value + ref[n]
        return value

    right_ref[...] = total(rf_ref)

    @pl.when(lead)
    def _():
        for d in range(1, 8):
            pp = poles[d]
            remote(re_ref.at[pp], re_ref.at[pp], se_s.at[0], se_r.at[pp], partner).wait_recv()
        side = total(re_ref)
        for k in (0, 1):
            for jj in (0, 1):
                at = k * 512 + jj * 256
                for top_half in (0, 1):
                    lane = top_half * 64 + jj * 32
                    cols = [side[2 * qq + k][:, lane : lane + 32] for qq in range(8)]
                    left_ref[top_half * 8 : top_half * 8 + 8, at : at + 256] = jnp.concatenate(cols, axis=1)

    @pl.when(jnp.logical_not(lead))
    def _():
        diag = total(rd_ref)
        upper = p < 2
        left_ref[:, 0:C] = jnp.where(upper, diag, 0.0)
        left_ref[:, C : 2 * C] = jnp.where(upper, 0.0, diag)

    for copy in pending:
        copy.wait_send()

    for when, here, away in gifts:

        @pl.when(when)
        def _():
            for copy in away:
                copy.wait_send()

    @pl.when(root)
    def _():
        for copy in top_y + top_x + top_x2:
            copy.wait_send()


GROUPS_DS = tuple(pl.ds(blocks.start, blocks.stop - blocks.start) for blocks in GROUPS)


def local(hamiltonian, margin, pattern, shift_real, shift_imag, residue):
    dma = pltpu.SemaphoreType.DMA
    vm = pltpu.VMEM
    left, right = pl.pallas_call(
        kernel,
        name="selected_inversion",
        out_shape=(jax.ShapeDtypeStruct((16, R), F32), jax.ShapeDtypeStruct((16, R), F32)),
        in_specs=[VM, VM, SM, SM, SM, SM],
        out_specs=(VM, VM),
        scratch_shapes=[
            vm((2, 16, 2 * R), F32), vm((2, 1536, 512), F32), vm((2, 64, 1024), F32), vm((2, 1024, C), BF16), vm((2, R, 2 * C), BF16),
            vm((8, C), F32), vm((768, 2 * R), BF16), vm((2, 192, C), F32), vm((2, 192, C), F32),
            vm((2, 64, C), F32), vm((2, 64, R), F32), vm((2, NB, 2, 16, 256), F32),
            vm((NB, 2, 16, 256), F32), vm((NB, 2, 16, 256), F32), vm((NB, 2, 16, 16, 256), F32),
            vm((2, 2 * R, R), BF16), vm((8, R), F32), vm((2, 128, R), F32), vm((2, 128, R), F32),
            vm((2, 64, C), F32), vm((2, 64, C), F32), vm((64, R), F32), vm((4, 16, 8, 128), F32),
            vm((64, R), F32), vm((64, C), F32),
            vm((8, 16, R), F32), vm((8, 16, C), F32), vm((8, 16, 8, 128), F32), vm((16, 4, 8, 128), F32),
            dma((5,)), dma((4, 2)), dma((3, 2)),
            dma((2, 3)), dma((2, 3)), dma((3, 2)), dma((3, 2)),
            dma((2, 3, 4)), dma((2, 3, 4)), dma((3, 4, 2)), dma((3, 4, 2)),
            dma((2,)), dma((2,)), dma((3, 2, 2)), dma((2, 2, 2)),
            dma((2,)), dma((2,)), dma((2,)), dma((2,)), dma((2,)), dma((4, 2)), dma((4, 2)),
            dma((2, 2, 2)), dma((2, 2, 2)), dma((2, 2, 2)), dma((2, 2, 2)),
            dma((2, 4, 2, 2)), dma((2, 4, 2, 2)),
            dma, dma((15,)), dma((15,)), dma((2, 2)), dma((8,)), dma((2, 2)), dma((8,)),
            dma((4,)), dma((4,)), dma((8,)),
        ],
        compiler_params=pltpu.CompilerParams(
            collective_id=0, has_side_effects=True, vmem_limit_bytes=56 << 20
        ),
        cost_estimate=pl.CostEstimate(flops=12 << 30, bytes_accessed=1 << 20, transcendentals=0),
    )(hamiltonian, margin, pattern, shift_real, shift_imag, residue)
    return jnp.concatenate([left, right], axis=1)


def solution(mesh):
    return jax.shard_map(
        local,
        mesh=mesh,
        in_specs=(
            P(("pole", "grid"), None),
            P(("pole", "grid"), None),
            P(),
            P("pole"),
            P("pole"),
            P("pole", None),
        ),
        out_specs=P(("pole", "grid"), None),
        check_vma=False,
    )
```

```python
import jax
import jax.numpy as jnp
from jax import lax
from jax.experimental import pallas as pl
from jax.experimental.pallas import tpu as pltpu
from jax.sharding import PartitionSpec as P

C = 512
R = 1024
F32 = jnp.float32
BF16 = jnp.bfloat16
MESH = pl.DeviceIdType.MESH
ANY = pl.BlockSpec(memory_space=pl.ANY)
VM = pl.BlockSpec(memory_space=pltpu.VMEM)
SM = pl.BlockSpec(memory_space=pltpu.SMEM)
BLOCKS = ((0, 0), (3, 0), (0, 1), (1, 1), (0, 2), (1, 2), (2, 2), (1, 3), (2, 3), (3, 3))
WHERE = {pair: b for b, pair in enumerate(BLOCKS)}
NB = len(BLOCKS)
GROUPS = (slice(0, 4), slice(4, 10))


def mod4(v):
    return lax.rem(v + 4, 4)


def half(v):
    return lax.div(v, 2)


def place():
    p = lax.axis_index("pole")
    g = lax.axis_index("grid")
    x, yl = half(p), lax.rem(p, 2)
    z, q, c = lax.div(g, 4), half(g), lax.rem(g, 2)
    return p, g, x, yl, z, lax.rem(q, 2), q, c


def spot(x, y, z, c):
    return (2 * x + lax.rem(y, 2), 4 * z + 2 * half(y) + c)


def greet(devices):
    barrier = pltpu.get_barrier_semaphore()
    for device in devices:
        pl.semaphore_signal(barrier, inc=1, device_id=device, device_id_type=MESH)
    pl.semaphore_wait(barrier, len(devices))


def remote(src, dst, send, recv, device):
    return pltpu.make_async_remote_copy(
        src_ref=src, dst_ref=dst, send_sem=send, recv_sem=recv, device_id=device, device_id_type=MESH
    )


def split(v):
    high = v.astype(BF16)
    return high, (v - high.astype(F32)).astype(BF16)


def put_pair(lhs_ref, vr, vi, start=0):
    m, k = vr.shape
    rh, rl = split(vr)
    ih, il = split(vi)
    for at, (re, im) in enumerate(((rh, ih), (rl, il))):
        base = start + at * 2 * m
        lhs_ref[base : base + m, 0:k] = re
        lhs_ref[base : base + m, k : 2 * k] = -im
        lhs_ref[base + m : base + 2 * m, 0:k] = im
        lhs_ref[base + m : base + 2 * m, k : 2 * k] = re


def fold(wide, narrow, m):
    total = wide[0 : 2 * m] + wide[2 * m : 4 * m] + narrow
    return total[0:m], total[m : 2 * m]


def dot(a, b):
    return jnp.dot(a, b, preferred_element_type=F32)


def dot_t(a, b):
    return lax.dot_general(a, b, (((1,), (1,)), ((), ())), preferred_element_type=F32)


def times(lhs_ref, rhs_ref, out_ref, vr, vi, width):
    m, k = vr.shape
    put_pair(lhs_ref, vr, vi)
    for n in range(width // 256):
        cols = slice(n * 256, n * 256 + 256)
        wide = dot(lhs_ref[0 : 4 * m, 0 : 2 * k], rhs_ref[0, :, cols])
        narrow = dot(lhs_ref[0 : 2 * m, 0 : 2 * k], rhs_ref[1, :, cols])
        re, im = fold(wide, narrow, m)
        out_ref[0, 0:m, cols] = re
        out_ref[1, 0:m, cols] = im


def rotate(vr, vi, dr, di):
    return vr * dr - vi * di, vr * di + vi * dr


def recip(dr, di):
    den = dr * dr + di * di
    return dr / den, -di / den


def iota(shape, dim):
    return lax.broadcasted_iota(jnp.int32, shape, dim)


def kernel(
    h_ref, s_ref, pat_ref, sr_ref, si_ref, res_ref, left_ref, right_ref,
    hs_ref, ab_ref, a0_ref, ehl_ref, bhl_ref, dinv_ref, lhs, cu_ref, ct_ref, xc_ref, w_ref, tb_ref,
    tin_ref, own_ref, sg_ref, shl_ref, d0_ref, u_ref, t_ref,
    k_ref, ku_ref, fw_ref, ft_ref, gw_ref, dw_ref, rf_ref, rd_ref, re_ref, ea_ref, pre_ref, pin_ref,
    loc_sem, x_s, x_r, f_s, f_r, fo_s, fo_r, g_s, g_r, go_s, go_r,
    y0_s, y0_r, x0_s, x0_r,
    tt_s, tt_r, own_sem, y_s, y_r, yo_s, yo_r, z_s, z_r, o_s, o_r, b_s, b_r,
    pre_s, pre_r, keep_sem, a_s, a_r, sf_s, sf_r, sd_s, sd_r, sg_s, se_s, se_r,
):
    p, g, x, yl, z, yh, q, c = place()
    y = 2 * yh + yl
    sr, si = sr_ref[0], si_ref[0]
    wr, wi = res_ref[0, 0], res_ref[0, 1]
    sib = g + 1 - 2 * c
    sibling = (p, sib)
    partner = (p + 1 - 2 * yl, g)
    over = (p, g + 2 - 4 * yh)
    xs = [spot(mod4(x + d), y, z, c) for d in (1, 2, 3)]
    ys = [spot(x, mod4(y + d), z, c) for d in (1, -1)]
    zs = [spot(x, y, mod4(z + d), c) for d in (1, -1)]
    poles = [lax.rem(p + d, 8) for d in range(8)]
    grids = [lax.rem(g + d, 16) for d in range(1, 16)]
    peers = [[spot(mod4(x + d), y, z, cc) for cc in (c, 1 - c)] for d in range(4)]
    loads = [pltpu.make_async_copy(ref, hs_ref.at[k], loc_sem.at[k]) for k, ref in enumerate((h_ref, s_ref))]
    for copy in loads:
        copy.start()
    greet([peers[d][e] for d in range(4) for e in (0, 1) if d + e > 0] + ys + zs)

    for copy in loads:
        copy.wait()
    pending = []

    def go(copy):
        copy.start()
        pending.append(copy)

    first = c == 0

    def pick(a, b):
        return tuple(jnp.where(first, u, v) for u, v in zip(a, b))

    fs = [pick(ys[i], zs[i]) for i in (0, 1)]
    gs = [pick(zs[i], ys[i]) for i in (0, 1)]
    f0 = jnp.where(first, y, z)
    g0 = jnp.where(first, z, y)

    def row(slot, f, s):
        yy, zz = jnp.where(first, f, s), jnp.where(first, s, f)
        return pl.multiple_of(slot * 512 + lax.rem(yy, 2) * 256 + (2 * zz + half(yy)) * 32, 32)

    def slab(slot, f, s):
        return ab_ref.at[:, pl.ds(row(slot, f, s), 32), :]

    def part(slot, f, s, k):
        return ab_ref.at[k, pl.ds(row(slot, f, s), 32), :]

    root = x >= 2

    def land(slot, cc):
        return ab_ref.at[:, pl.ds(pl.multiple_of(slot * 512 + yl * 256 + q * 32 + cc * 16, 16), 16), :]

    def child_cols(k):
        return hs_ref.at[:, :, pl.ds(pl.multiple_of(k * 512, 128), 512)]

    def stay_put(slot):
        return pltpu.make_async_copy(child_cols(c), land(slot, c), loc_sem.at[slot])

    def give(slot, d, e):
        return remote(
            child_cols(c if e == 0 else 1 - c), land(slot, c), x_s.at[d, e], x_r.at[slot, e], peers[d][e]
        )

    def givers(slot):
        if slot > 0:
            away = [give(slot, d, e) for d, e in ((0, 1), (1, 0), (3, 0), (1, 1), (3, 1))]
            return [(x == slot + 1, [stay_put(slot)], away, [give(slot, 2, e) for e in (0, 1)])]
        return [
            (jnp.logical_and(x < 2, x == c), [stay_put(0)], [give(0, d, 0) for d in (1, 3)], [give(0, 2, 0)]),
            (jnp.logical_and(x < 2, x != c), [], [give(0, d, 1) for d in (0, 1, 3)], [give(0, 2, 1)]),
        ]

    gifts = givers(0) + givers(1) + givers(2)
    for when, here, away, opposite in gifts:

        @pl.when(when)
        def _():
            for copy in away + here:
                copy.start()

    def give_opposite():
        for when, here, away, opposite in gifts:

            @pl.when(when)
            def _():
                for copy in opposite:
                    copy.start()

    def taken(slot):
        source = jnp.where(slot == 0, c, slot + 1)
        remote(land(slot, 1 - c), land(slot, 1 - c), x_s.at[1, 1], x_r.at[slot, 1], peers[1][1]).wait_recv()

        @pl.when(x != source)
        def _():
            remote(land(slot, c), land(slot, c), x_s.at[1, 0], x_r.at[slot, 0], peers[1][0]).wait_recv()

        @pl.when(x == source)
        def _():
            stay_put(slot).wait()

    sx = jnp.maximum(x - 2, 0)
    j0 = 2 * sx + yl
    j1 = 2 * sx + 1 - yl

    def top(k, j):
        return a0_ref.at[k, pl.ds(pl.multiple_of(j * 16, 16), 16), :]

    top_src = [hs_ref.at[k, :, pl.ds(1024, 1024)] for k in (0, 1)]
    top_own = [pltpu.make_async_copy(top_src[k], top(k, j0), loc_sem.at[3 + k]) for k in (0, 1)]
    top_y = [remote(top_src[k], top(k, j0), y0_s.at[k], y0_r.at[k], partner) for k in (0, 1)]
    top_y_in = [remote(top_src[k], top(k, j1), y0_s.at[k], y0_r.at[k], partner) for k in (0, 1)]
    top_x = [
        remote(top_src[k], top(k, j0), x0_s.at[n, 0, k], x0_r.at[sx, 0, k], xs[n]) for n in range(3) for k in (0, 1)
    ]
    top_x2 = [
        remote(top(k, j1), top(k, j1), x0_s.at[n, 1, k], x0_r.at[sx, 1, k], xs[n]) for n in range(3) for k in (0, 1)
    ]

    f_at = (f0, mod4(f0 - 1), mod4(f0 + 1), mod4(f0 + 2))
    g_at = (mod4(g0 - 1), mod4(g0 + 1), mod4(g0 + 2))

    def spread(slot, n):
        ref = slab(slot, f_at[n], g0)
        for d in (0, 1):
            go(remote(ref, ref, g_s.at[d, slot, n], g_r.at[d, slot, n], gs[d]))

    def open_slot(slot):
        taken(slot)
        for d in (0, 1):
            ref = slab(slot, f0, g0)
            go(remote(ref, ref, f_s.at[d, slot], f_r.at[d, slot], fs[d]))
        spread(slot, 0)

    def near(slot):
        for d in (0, 1):
            ref = slab(slot, f_at[1 + d], g0)
            remote(ref, ref, f_s.at[d, slot], f_r.at[d, slot], fs[d]).wait_recv()
            ref = part(slot, f_at[1 + d], g0, d)
            go(remote(ref, ref, fo_s.at[slot, d], fo_r.at[slot, d], fs[d]))
            spread(slot, 1 + d)

    def far(slot):
        for d in (0, 1):
            ref = part(slot, f_at[3], g0, d)
            remote(ref, ref, fo_s.at[slot, d], fo_r.at[slot, d], fs[d]).wait_recv()
        spread(slot, 3)

    def relay(slot, n):
        for d in (0, 1):
            ref = slab(slot, f_at[n], g_at[d])
            remote(ref, ref, g_s.at[d, slot, n], g_r.at[d, slot, n], gs[d]).wait_recv()
            ref = part(slot, f_at[n], g_at[d], d)
            go(remote(ref, ref, go_s.at[slot, n, d], go_r.at[slot, n, d], gs[d]))

    def close_slot(slot):
        for n in range(4):
            for d in (0, 1):
                ref = part(slot, f_at[n], g_at[2], d)
                remote(ref, ref, go_s.at[slot, n, d], go_r.at[slot, n, d], gs[d]).wait_recv()

    def top_start():
        @pl.when(root)
        def _():
            for copy in top_y + top_own + top_x:
                copy.start()

    def top_more():
        @pl.when(root)
        def _():
            for k in (0, 1):
                top_y_in[k].wait_recv()
            for copy in top_x2:
                copy.start()

    dinv_ref[...] = jnp.zeros_like(dinv_ref)

    def scale_rows(n):
        rows = slice(n * 64, n * 64 + 64)
        low = slice(n * 64 + C, n * 64 + C + 64)
        s = ab_ref[1, rows, :]
        re = ab_ref[0, rows, :] - sr * s
        im = -si * s
        eye = iota((64, C), 1) == iota((64, C), 0) + n * 64
        ir, ii = recip(
            jnp.sum(jnp.where(eye, re, 0.0), axis=1, keepdims=True),
            jnp.sum(jnp.where(eye, im, 0.0), axis=1, keepdims=True),
        )
        dinv_ref[0:1, :] += jnp.sum(jnp.where(eye, ir, 0.0), axis=0, keepdims=True)
        dinv_ref[1:2, :] += jnp.sum(jnp.where(eye, ii, 0.0), axis=0, keepdims=True)
        er, ei = rotate(re, im, -ir, -ii)
        for where, value in ((rows, er), (low, ei)):
            high, rest = split(jnp.where(eye, 0.0, value))
            ehl_ref[0, where, :] = high
            ehl_ref[1, where, :] = rest

    def pattern_at(j, half_at):
        return jnp.where(first, pat_ref[j, half_at], pat_ref[j, 2 + half_at]).astype(F32)

    def couple(h, s, j):
        m = jnp.where(iota((1, C), 1) < 256, pattern_at(j, 0), pattern_at(j, 1))
        s = s * m
        return h * m - sr * s, -si * s

    def split_rows(n):
        rows = slice(C + n * 64, C + n * 64 + 64)
        re, im = couple(ab_ref[0, rows, :], ab_ref[1, rows, :], n // 4)
        rows = slice(n * 64, n * 64 + 64)
        for at, value in ((0, re), (C, im)):
            high, rest = split(value)
            bhl_ref[0, rows, at : at + C] = high
            bhl_ref[1, rows, at : at + C] = rest

    def chain_start():
        for j in range(4):
            rows = pl.ds(pl.multiple_of(C + j * 256 + q * 32, 32), 32)
            re, im = couple(ab_ref[0, rows, :], ab_ref[1, rows, :], j)
            ct_ref[0, j * 32 : j * 32 + 32, :] = re
            ct_ref[1, j * 32 : j * 32 + 32, :] = im
        times(lhs, ehl_ref, cu_ref, ct_ref[0, 0:128, :], ct_ref[1, 0:128, :], C)
        cu_ref[0, 0:128, :] += ct_ref[0, 0:128, :]
        cu_ref[1, 0:128, :] += ct_ref[1, 0:128, :]
        for jj in range(2):
            at = pl.multiple_of(jj * 256 + q * 32, 32)
            low = pl.multiple_of(jj * 256 + q * 32 + C, 32)
            eye = iota((32, C), 1) == iota((32, C), 0) + at
            rows = slice(128 + jj * 32, 160 + jj * 32)
            er = ehl_ref[0, pl.ds(at, 32), :].astype(F32) + ehl_ref[1, pl.ds(at, 32), :].astype(F32)
            ei = ehl_ref[0, pl.ds(low, 32), :].astype(F32) + ehl_ref[1, pl.ds(low, 32), :].astype(F32)
            cu_ref[0, rows, :] = jnp.where(eye, 1.0, er)
            cu_ref[1, rows, :] = ei

    def chain_two():
        times(lhs, ehl_ref, ct_ref, cu_ref[0], cu_ref[1], C)

    def chain_three():
        times(lhs, ehl_ref, ct_ref, ct_ref[0], ct_ref[1], C)
        lr, li = rotate(cu_ref[0] + ct_ref[0], cu_ref[1] + ct_ref[1], dinv_ref[0:1, :], dinv_ref[1:2, :])
        xc_ref[0] = lr[128:192]
        xc_ref[1] = li[128:192]
        put_pair(lhs, lr[0:128], li[0:128])
        put_pair(lhs, lr[128:192], li[128:192], 512)

    def product(n):
        rows = slice(n * 256, n * 256 + 256)
        wide = dot_t(lhs[0:512, 0 : 2 * C], bhl_ref[0, rows, :])
        narrow = dot_t(lhs[0:256, 0 : 2 * C], bhl_ref[1, rows, :])
        pair = fold(wide, narrow, 128)
        for k in (0, 1):
            for b, (j, other) in enumerate(BLOCKS):
                if other == n:
                    for cc in (0, 1):
                        tb_ref[cc, b, k] = pair[k][j * 32 + cc * 16 : j * 32 + cc * 16 + 16]

    def product_w(n):
        rows = slice(n * 256, n * 256 + 256)
        wide = dot_t(lhs[512:768, 0 : 2 * C], bhl_ref[0, rows, :])
        narrow = dot_t(lhs[512:640, 0 : 2 * C], bhl_ref[1, rows, :])
        w_ref[0, :, rows], w_ref[1, :, rows] = fold(wide, narrow, 64)

    order = (jnp.maximum(x - 1, 0), jnp.where(x < 2, 1, 0), jnp.where(x == 3, 1, 2))

    def turn(stage, o, *more):
        return lambda: stage(order[o], *more)

    steps = [
        turn(open_slot, 0), give_opposite, turn(near, 0), turn(relay, 0, 0), turn(far, 0),
        turn(open_slot, 1), turn(open_slot, 2), top_start,
        turn(relay, 0, 1), turn(relay, 0, 2), turn(near, 1), turn(relay, 0, 3), turn(relay, 1, 0),
        turn(near, 2), turn(far, 1), turn(relay, 2, 0), turn(relay, 1, 1), turn(relay, 1, 2), top_more,
        turn(far, 2), turn(relay, 1, 3), turn(close_slot, 0), turn(close_slot, 1),
        lambda: scale_rows(0), lambda: scale_rows(1), turn(relay, 2, 1),
        lambda: scale_rows(2), lambda: scale_rows(3), turn(relay, 2, 2),
        lambda: scale_rows(4), lambda: scale_rows(5), lambda: scale_rows(6), turn(relay, 2, 3),
        lambda: scale_rows(7), chain_start, chain_two, chain_three, turn(close_slot, 2),
    ] + [lambda n=n: split_rows(n) for n in range(16)]
    for step in steps:
        step()

    for sx_in in (0, 1):
        jx = (2 * sx_in + yl, 2 * sx_in + 1 - yl)

        @pl.when(x != 2 + sx_in)
        def _():
            for o in (0, 1):
                for k in (0, 1):
                    ref = top(k, jx[o])
                    remote(ref, ref, x0_s.at[0, o, k], x0_r.at[sx_in, o, k], xs[0]).wait_recv()

    @pl.when(root)
    def _():
        for copy in top_own:
            copy.wait()

    swaps = [
        remote(tb_ref.at[1 - c, blocks], tin_ref.at[blocks], tt_s.at[n], tt_r.at[n], sibling)
        for n, blocks in enumerate(GROUPS_DS)
    ]
    def finish(n):
        for b in range(GROUPS[n].start, GROUPS[n].stop):
            j, other = BLOCKS[b]
            s = a0_ref[1, j * 16 : j * 16 + 16, other * 256 : other * 256 + 256]
            h = a0_ref[0, j * 16 : j * 16 + 16, other * 256 : other * 256 + 256]
            own_ref[b, 0] = h - sr * s - tb_ref[c, b, 0]
            own_ref[b, 1] = -si * s - tb_ref[c, b, 1]
        swaps[n].wait_recv()
        rows = GROUPS[n]
        own_ref[rows] = own_ref[rows] - tin_ref[rows]

    def whole(n, gg):
        return sg_ref.at[GROUPS_DS[n], :, gg]

    def piece(n, gg, k):
        return sg_ref.at[GROUPS_DS[n], k, gg]

    base = (g, g + 2 - 4 * yh)
    hop = [0] + [4 * (mod4(z + d) - z) for d in (-1, 1, 2)]

    def hand(n, m, o, ref_of):
        for k in (0, 1):
            ref = piece(n, base[o] + hop[m], k)
            go(remote(ref_of(k), ref, b_s.at[n, m, o, k], b_r.at[n, m, o, k], sibling))

    def along_z(n, o, src):
        dst = whole(n, base[o])
        for d in (0, 1):
            go(remote(dst if src is None else src, dst, z_s.at[d, n, o], z_r.at[d, n, o], zs[d]))

    keeps = []

    def launch(n):
        finish(n)
        src = own_ref.at[GROUPS_DS[n]]
        if n == 0:
            along_z(n, 0, src)
        go(remote(src, whole(n, g), y_s.at[n], y_r.at[n], over))
        if n == 1:
            along_z(n, 0, src)
        keep = pltpu.make_async_copy(src, whole(n, g), own_sem.at[n])
        keep.start()
        keeps.append(keep)
        hand(n, 0, 0, lambda k: own_ref.at[GROUPS_DS[n], k])

    def from_over(n):
        ref = whole(n, base[1])
        remote(ref, ref, y_s.at[n], y_r.at[n], over).wait_recv()
        hand(n, 0, 1, lambda k: piece(n, base[1], k))

    def from_z(n, o):
        for d in (0, 1):
            gg = base[o] + hop[1 + d]
            ref = whole(n, gg)
            remote(ref, ref, z_s.at[d, n, o], z_r.at[d, n, o], zs[d]).wait_recv()
            ref = piece(n, gg, d)
            go(remote(ref, ref, o_s.at[n, o, d], o_r.at[n, o, d], zs[d]))
            if n == 0:
                for k in (0, 1):
                    ref = piece(n, gg, k)
                    go(remote(ref, ref, yo_s.at[1 + d, k], yo_r.at[1 + d, k], over))
            hand(n, 1 + d, o, lambda k, gg=gg: piece(n, gg, k))

    def from_far(n, o):
        gg = base[o] + hop[3]
        for k in (0, 1):
            ref = piece(n, gg, k)
            remote(ref, ref, o_s.at[n, o, k], o_r.at[n, o, k], zs[k]).wait_recv()
            if n == 0:
                go(remote(ref, ref, yo_s.at[3, k], yo_r.at[3, k], over))
            go(remote(ref, ref, b_s.at[n, 3, o, k], b_r.at[n, 3, o, k], sibling))

    def over_far(m):
        gg = base[1] + hop[m]
        for k in (0, 1):
            ref = piece(0, gg, k)
            remote(ref, ref, yo_s.at[m, k], yo_r.at[m, k], over).wait_recv()
            go(remote(ref, ref, b_s.at[0, m, 1, k], b_r.at[0, m, 1, k], sibling))

    product(0)
    product(1)
    go(swaps[0])
    product(2)
    launch(0)
    product(3)
    go(swaps[1])
    product_w(0)
    launch(1)
    from_z(0, 0)
    product_w(1)
    from_over(1)
    along_z(1, 1, None)
    from_over(0)
    product_w(2)
    product_w(3)
    from_far(0, 0)
    from_z(1, 0)
    over_far(1)
    over_far(2)
    from_z(1, 1)
    from_far(1, 0)
    over_far(3)
    from_far(1, 1)

    def arrived(n):
        for m in range(4):
            for o in (0, 1):
                gg = base[o] + hop[m] + 1 - 2 * c
                for k in (0, 1):
                    ref = piece(n, gg, k)
                    remote(ref, ref, b_s.at[n, m, o, k], b_r.at[n, m, o, k], sibling).wait_recv()
        keeps[n].wait()

    def block(b, k):
        return sg_ref[b, k].reshape(256, 256)

    eye = iota((256, 256), 1) == iota((256, 256), 0)
    inverse = {}

    def diagonal(j):
        b = WHERE[(j, j)]
        ir, ii = recip(
            jnp.sum(jnp.where(eye, block(b, 0), 0.0), axis=1, keepdims=True),
            jnp.sum(jnp.where(eye, block(b, 1), 0.0), axis=1, keepdims=True),
        )
        cols = slice(j * 256, j * 256 + 256)
        d0_ref[0:1, cols] = jnp.sum(jnp.where(eye, ir, 0.0), axis=0, keepdims=True)
        d0_ref[1:2, cols] = jnp.sum(jnp.where(eye, ii, 0.0), axis=0, keepdims=True)
        inverse[j] = ir, ii

    def scale_block(j, other):
        rows = slice(j * 256, j * 256 + 256)
        low = slice(R + j * 256, R + j * 256 + 256)
        cols = slice(other * 256, other * 256 + 256)
        if (j, other) in WHERE:
            b = WHERE[(j, other)]
            re, im = block(b, 0), block(b, 1)
        else:
            b = WHERE[(other, j)]
            re, im = block(b, 0).T, block(b, 1).T
        ir, ii = inverse[j]
        er, ei = rotate(re, im, -ir, -ii)
        for where, value in ((rows, er), (low, ei)):
            if j == other:
                value = jnp.where(eye, 0.0, value)
            high, rest = split(value)
            shl_ref[0, where, cols] = high
            shl_ref[1, where, cols] = rest

    early = ((0, 0), (0, 1), (0, 3), (1, 0), (1, 1))
    arrived(0)
    diagonal(0)
    diagonal(1)
    for pair in early:
        scale_block(*pair)
    arrived(1)
    diagonal(2)
    diagonal(3)
    for j in range(4):
        for other in range(4):
            if (j, other) not in early:
                scale_block(j, other)
    times(lhs, shl_ref, u_ref, w_ref[0], w_ref[1], R)
    u_ref[0, 0:64, :] += w_ref[0]
    u_ref[1, 0:64, :] += w_ref[1]
    for j in range(4):
        at = pl.multiple_of(j * 256 + g * 16, 16)
        low = pl.multiple_of(j * 256 + g * 16 + R, 16)
        on = iota((16, R), 1) == iota((16, R), 0) + at
        rows = slice(64 + j * 16, 80 + j * 16)
        er = shl_ref[0, pl.ds(at, 16), :].astype(F32) + shl_ref[1, pl.ds(at, 16), :].astype(F32)
        ei = shl_ref[0, pl.ds(low, 16), :].astype(F32) + shl_ref[1, pl.ds(low, 16), :].astype(F32)
        u_ref[0, rows, :] = jnp.where(on, 1.0, er)
        u_ref[1, rows, :] = ei
    times(lhs, shl_ref, t_ref, u_ref[0], u_ref[1], R)
    times(lhs, shl_ref, t_ref, t_ref[0], t_ref[1], R)
    yr, yi = rotate(u_ref[0] + t_ref[0], u_ref[1] + t_ref[1], d0_ref[0:1, :], d0_ref[1:2, :])
    gw_ref[...] = wr * yr[64:128] - wi * yi[64:128]
    yr, yi = yr[0:64], yi[0:64]
    weighted = -(wr * yr - wi * yi)
    for j in range(4):
        cols = slice(j * 256, j * 256 + 256)
        m = jnp.where(iota((64, 1), 0) < 32, pattern_at(j, 0), pattern_at(j, 1))
        side = weighted[:, cols] * m
        fw_ref[:, cols] = side
        turned = side.T.reshape(16, 2, 8, 64)
        ft_ref[j] = jnp.concatenate([turned[:, 0], turned[:, 1]], axis=2)

    for d, gg in enumerate(grids):
        go(remote(ft_ref.at[:, gg], ea_ref.at[g], a_s.at[d], a_r.at[d], (p, gg)))
    keep = pltpu.make_async_copy(ft_ref.at[:, g], ea_ref.at[g], keep_sem)
    keep.start()
    sent = []

    def send_or_keep(src, dst, ss, rs, target, here):
        away = remote(src, dst, ss, rs, target)
        stay = pltpu.make_async_copy(src, dst, ss)

        @pl.when(jnp.logical_not(here))
        def _():
            away.start()

        @pl.when(here)
        def _():
            stay.start()

        sent.append((here, away, stay))

    def child_rows():
        for jj in (0, 1):
            for cc in (0, 1):
                here = jnp.logical_and(p == 2 * c + jj, c == cc)
                rows = pl.ds(jj * 32 + cc * 16, 16)
                send_or_keep(
                    dw_ref.at[rows, :], rd_ref.at[p], sd_s.at[jj, cc], sd_r.at[p], (2 * c + jj, 2 * q + cc), here
                )

    for j in range(4):
        xx = 2 + j // 2
        send_or_keep(
            gw_ref.at[pl.ds(j * 16, 16), :], rf_ref.at[x, j % 2], sg_s.at[j], sf_r.at[x, j % 2], (2 * xx + yl, g), x == xx
        )
    for jj in (0, 1):
        for cc in (0, 1):
            send_or_keep(
                fw_ref.at[pl.ds(jj * 32 + cc * 16, 16), :], rf_ref.at[x, jj], sf_s.at[jj, cc], sf_r.at[x, jj],
                (2 * c + yl, 2 * q + cc), jnp.logical_and(x == c, c == cc),
            )

    rh, rl = split(yr)
    ih, il = split(yi)
    for at, (re, im) in enumerate(((rh, ih), (rl, il))):
        lhs[at * 128 : at * 128 + 64, 0:R] = re
        lhs[at * 128 + 64 : at * 128 + 128, 0:R] = im
        lhs[at * 128 : at * 128 + 64, R : 2 * R] = -im
        lhs[at * 128 + 64 : at * 128 + 128, R : 2 * R] = re
    wide = dot(lhs[0:256, 0:R], bhl_ref[0, :, 0:C]) + dot(lhs[0:256, R : 2 * R], bhl_ref[0, :, C : 2 * C])
    narrow = dot(lhs[0:128, 0:R], bhl_ref[1, :, 0:C]) + dot(lhs[0:128, R : 2 * R], bhl_ref[1, :, C : 2 * C])
    pr, pi = fold(wide, narrow, 64)

    keep.wait()
    for d in range(15):
        gg = lax.rem(g + 15 - d, 16)
        remote(ea_ref.at[gg], ea_ref.at[gg], a_s.at[d], a_r.at[d], (p, grids[0])).wait_recv()
    for j in range(4):
        send_or_keep(ea_ref.at[:, j], re_ref.at[p], se_s.at[j], se_r.at[p], (4 + j, g), p == 4 + j)

    times(lhs, ehl_ref, k_ref, pr, pi, C)
    ku_ref[0] = k_ref[0] + pr
    ku_ref[1] = k_ref[1] + pi
    times(lhs, ehl_ref, k_ref, ku_ref[0], ku_ref[1], C)
    times(lhs, ehl_ref, k_ref, k_ref[0], k_ref[1], C)
    zr, zi = rotate(ku_ref[0] + k_ref[0], ku_ref[1] + k_ref[1], dinv_ref[0:1, :], dinv_ref[1:2, :])
    dw_ref[...] = wr * (xc_ref[0] + zr) - wi * (xc_ref[1] + zi)
    child_rows()

    for here, away, stay in sent:

        @pl.when(here)
        def _():
            stay.wait()

    lead = p >= 4
    same = jnp.logical_or(lead, c == half(p))
    for d in range(4):
        xx = mod4(x + d)

        @pl.when(jnp.logical_or(jnp.logical_not(same), d > 0))
        def _():
            for n in (0, 1):
                remote(rf_ref.at[xx, n], rf_ref.at[xx, n], sf_s.at[0, 0], sf_r.at[xx, n], partner).wait_recv()

    pre_ref[...] = rf_ref[0, 1 - yl] + rf_ref[1, 1 - yl] + rf_ref[2, 1 - yl] + rf_ref[3, 1 - yl]
    cross = remote(pre_ref, pin_ref, pre_s, pre_r, partner)
    go(cross)
    for d in range(8):
        pp = poles[d]

        @pl.when(jnp.logical_and(jnp.logical_not(lead), jnp.logical_or(jnp.logical_not(same), d > 0)))
        def _():
            remote(rd_ref.at[pp], rd_ref.at[pp], sd_s.at[0, 0], sd_r.at[pp], partner).wait_recv()

    def total(ref):
        value = ref[0]
        for n in range(1, 8):
            value = value + ref[n]
        return value

    @pl.when(lead)
    def _():
        for d in range(1, 8):
            pp = poles[d]
            remote(re_ref.at[pp], re_ref.at[pp], se_s.at[0], se_r.at[pp], partner).wait_recv()
        side = total(re_ref)
        for k in (0, 1):
            for jj in (0, 1):
                at = k * 512 + jj * 256
                for top_half in (0, 1):
                    lane = top_half * 64 + jj * 32
                    cols = [side[2 * qq + k][:, lane : lane + 32] for qq in range(8)]
                    left_ref[top_half * 8 : top_half * 8 + 8, at : at + 256] = jnp.concatenate(cols, axis=1)

    @pl.when(jnp.logical_not(lead))
    def _():
        diag = total(rd_ref)
        upper = p < 2
        left_ref[:, 0:C] = jnp.where(upper, diag, 0.0)
        left_ref[:, C : 2 * C] = jnp.where(upper, 0.0, diag)

    main = rf_ref[0, yl] + rf_ref[1, yl] + rf_ref[2, yl] + rf_ref[3, yl]
    cross.wait_recv()
    right_ref[...] = main + pin_ref[...]

    for here, away, stay in sent:

        @pl.when(jnp.logical_not(here))
        def _():
            away.wait_send()

    for copy in pending:
        copy.wait_send()

    for when, here, away, opposite in gifts:

        @pl.when(when)
        def _():
            for copy in away + opposite:
                copy.wait_send()

    @pl.when(root)
    def _():
        for copy in top_y + top_x + top_x2:
            copy.wait_send()


GROUPS_DS = tuple(pl.ds(blocks.start, blocks.stop - blocks.start) for blocks in GROUPS)


def local(hamiltonian, margin, pattern, shift_real, shift_imag, residue):
    dma = pltpu.SemaphoreType.DMA
    vm = pltpu.VMEM
    left, right = pl.pallas_call(
        kernel,
        name="selected_inversion",
        out_shape=(jax.ShapeDtypeStruct((16, R), F32), jax.ShapeDtypeStruct((16, R), F32)),
        in_specs=[ANY, ANY, SM, SM, SM, SM],
        out_specs=(VM, VM),
        scratch_shapes=[
            vm((2, 16, 2 * R), F32), vm((2, 1536, 512), F32), vm((2, 64, 1024), F32), vm((2, 1024, C), BF16), vm((2, R, 2 * C), BF16),
            vm((8, C), F32), vm((768, 2 * R), BF16), vm((2, 192, C), F32), vm((2, 192, C), F32),
            vm((2, 64, C), F32), vm((2, 64, R), F32), vm((2, NB, 2, 16, 256), F32),
            vm((NB, 2, 16, 256), F32), vm((NB, 2, 16, 256), F32), vm((NB, 2, 16, 16, 256), F32),
            vm((2, 2 * R, R), BF16), vm((8, R), F32), vm((2, 128, R), F32), vm((2, 128, R), F32),
            vm((2, 64, C), F32), vm((2, 64, C), F32), vm((64, R), F32), vm((4, 16, 8, 128), F32),
            vm((64, R), F32), vm((64, C), F32),
            vm((4, 2, 16, R), F32), vm((8, 16, C), F32), vm((8, 16, 8, 128), F32), vm((16, 4, 8, 128), F32),
            vm((16, R), F32), vm((16, R), F32),
            dma((5,)), dma((4, 2)), dma((3, 2)),
            dma((2, 3)), dma((2, 3)), dma((3, 2)), dma((3, 2)),
            dma((2, 3, 4)), dma((2, 3, 4)), dma((3, 4, 2)), dma((3, 4, 2)),
            dma((2,)), dma((2,)), dma((3, 2, 2)), dma((2, 2, 2)),
            dma((2,)), dma((2,)), dma((2,)), dma((2,)), dma((2,)), dma((4, 2)), dma((4, 2)),
            dma((2, 2, 2)), dma((2, 2, 2)), dma((2, 2, 2)), dma((2, 2, 2)),
            dma((2, 4, 2, 2)), dma((2, 4, 2, 2)),
            dma, dma, dma, dma((15,)), dma((15,)), dma((2, 2)), dma((4, 2)), dma((2, 2)), dma((8,)),
            dma((4,)), dma((4,)), dma((8,)),
        ],
        compiler_params=pltpu.CompilerParams(
            collective_id=0, has_side_effects=True, vmem_limit_bytes=56 << 20
        ),
        cost_estimate=pl.CostEstimate(flops=12 << 30, bytes_accessed=1 << 20, transcendentals=0),
    )(hamiltonian, margin, pattern, shift_real, shift_imag, residue)
    return jnp.concatenate([left, right], axis=1)


def solution(mesh):
    return jax.shard_map(
        local,
        mesh=mesh,
        in_specs=(
            P(("pole", "grid"), None),
            P(("pole", "grid"), None),
            P(),
            P("pole"),
            P("pole"),
            P("pole", None),
        ),
        out_specs=P(("pole", "grid"), None),
        check_vma=False,
    )
```

```python
import jax
import jax.numpy as jnp
from jax import lax
from jax.experimental import pallas as pl
from jax.experimental.pallas import tpu as pltpu
from jax.sharding import PartitionSpec as P

C = 512
R = 1024
F32 = jnp.float32
BF16 = jnp.bfloat16
MESH = pl.DeviceIdType.MESH
ANY = pl.BlockSpec(memory_space=pl.ANY)
VM = pl.BlockSpec(memory_space=pltpu.VMEM)
SM = pl.BlockSpec(memory_space=pltpu.SMEM)
BLOCKS = ((0, 0), (3, 0), (0, 1), (1, 1), (0, 2), (1, 2), (2, 2), (1, 3), (2, 3), (3, 3))
WHERE = {pair: b for b, pair in enumerate(BLOCKS)}
NB = len(BLOCKS)
GROUPS = (slice(0, 4), slice(4, 10))


def mod4(v):
    return lax.rem(v + 4, 4)


def half(v):
    return lax.div(v, 2)


def place():
    p = lax.axis_index("pole")
    g = lax.axis_index("grid")
    x, yl = half(p), lax.rem(p, 2)
    z, q, c = lax.div(g, 4), half(g), lax.rem(g, 2)
    return p, g, x, yl, z, lax.rem(q, 2), q, c


def spot(x, y, z, c):
    return (2 * x + lax.rem(y, 2), 4 * z + 2 * half(y) + c)


def greet(devices):
    barrier = pltpu.get_barrier_semaphore()
    for device in devices:
        pl.semaphore_signal(barrier, inc=1, device_id=device, device_id_type=MESH)
    pl.semaphore_wait(barrier, len(devices))


def remote(src, dst, send, recv, device):
    return pltpu.make_async_remote_copy(
        src_ref=src, dst_ref=dst, send_sem=send, recv_sem=recv, device_id=device, device_id_type=MESH
    )


def split(v):
    high = v.astype(BF16)
    return high, (v - high.astype(F32)).astype(BF16)


def put_pair(lhs_ref, vr, vi, start=0):
    m, k = vr.shape
    rh, rl = split(vr)
    ih, il = split(vi)
    for at, (re, im) in enumerate(((rh, ih), (rl, il))):
        base = start + at * 2 * m
        lhs_ref[base : base + m, 0:k] = re
        lhs_ref[base : base + m, k : 2 * k] = -im
        lhs_ref[base + m : base + 2 * m, 0:k] = im
        lhs_ref[base + m : base + 2 * m, k : 2 * k] = re


def fold(wide, narrow, m):
    total = wide[0 : 2 * m] + wide[2 * m : 4 * m] + narrow
    return total[0:m], total[m : 2 * m]


def dot(a, b):
    return jnp.dot(a, b, preferred_element_type=F32)


def dot_t(a, b):
    return lax.dot_general(a, b, (((1,), (1,)), ((), ())), preferred_element_type=F32)


def times(lhs_ref, rhs_ref, out_ref, vr, vi, width):
    m, k = vr.shape
    put_pair(lhs_ref, vr, vi)
    for n in range(width // 256):
        cols = slice(n * 256, n * 256 + 256)
        wide = dot(lhs_ref[0 : 4 * m, 0 : 2 * k], rhs_ref[0, :, cols])
        narrow = dot(lhs_ref[0 : 2 * m, 0 : 2 * k], rhs_ref[1, :, cols])
        re, im = fold(wide, narrow, m)
        out_ref[0, 0:m, cols] = re
        out_ref[1, 0:m, cols] = im


def rotate(vr, vi, dr, di):
    return vr * dr - vi * di, vr * di + vi * dr


def recip(dr, di):
    den = dr * dr + di * di
    return dr / den, -di / den


def iota(shape, dim):
    return lax.broadcasted_iota(jnp.int32, shape, dim)


def kernel(
    h_ref, s_ref, pat_ref, sr_ref, si_ref, res_ref, left_ref, right_ref,
    hs_ref, ab_ref, a0_ref, ehl_ref, bhl_ref, dinv_ref, lhs, cu_ref, ct_ref, xc_ref, w_ref, tb_ref,
    tin_ref, own_ref, sg_ref, shl_ref, d0_ref, u_ref, t_ref,
    k_ref, ku_ref, fw_ref, ft_ref, gw_ref, dw_ref, rf_ref, rd_ref, re_ref, ea_ref, pre_ref, pin_ref,
    loc_sem, x_s, x_r, f_s, f_r, fo_s, fo_r, g_s, g_r, go_s, go_r,
    y0_s, y0_r, x0_s, x0_r,
    tt_s, tt_r, own_sem, y_s, y_r, yo_s, yo_r, z_s, z_r, o_s, o_r, b_s, b_r,
    pre_s, pre_r, keep_sem, a_s, a_r, sf_s, sf_r, sd_s, sd_r, sg_s, se_s, se_r,
):
    p, g, x, yl, z, yh, q, c = place()
    y = 2 * yh + yl
    sr, si = sr_ref[0], si_ref[0]
    wr, wi = res_ref[0, 0], res_ref[0, 1]
    sib = g + 1 - 2 * c
    sibling = (p, sib)
    partner = (p + 1 - 2 * yl, g)
    over = (p, g + 2 - 4 * yh)
    xs = [spot(mod4(x + d), y, z, c) for d in (1, 2, 3)]
    ys = [spot(x, mod4(y + d), z, c) for d in (1, -1)]
    zs = [spot(x, y, mod4(z + d), c) for d in (1, -1)]
    poles = [lax.rem(p + d, 8) for d in range(8)]
    grids = [lax.rem(g + d, 16) for d in range(1, 16)]
    peers = [[spot(mod4(x + d), y, z, cc) for cc in (c, 1 - c)] for d in range(4)]
    loads = [pltpu.make_async_copy(ref, hs_ref.at[k], loc_sem.at[k]) for k, ref in enumerate((h_ref, s_ref))]
    for copy in loads:
        copy.start()
    greet([peers[d][e] for d in range(4) for e in (0, 1) if d + e > 0] + ys + zs)

    for copy in loads:
        copy.wait()
    pending = []

    def go(copy):
        copy.start()
        pending.append(copy)

    first = c == 0

    def pick(a, b):
        return tuple(jnp.where(first, u, v) for u, v in zip(a, b))

    fs = [pick(ys[i], zs[i]) for i in (0, 1)]
    gs = [pick(zs[i], ys[i]) for i in (0, 1)]
    f0 = jnp.where(first, y, z)
    g0 = jnp.where(first, z, y)

    def row(slot, f, s):
        yy, zz = jnp.where(first, f, s), jnp.where(first, s, f)
        return pl.multiple_of(slot * 512 + lax.rem(yy, 2) * 256 + (2 * zz + half(yy)) * 32, 32)

    def slab(slot, f, s):
        return ab_ref.at[:, pl.ds(row(slot, f, s), 32), :]

    def part(slot, f, s, k):
        return ab_ref.at[k, pl.ds(row(slot, f, s), 32), :]

    root = x >= 2

    def land(slot, cc):
        return ab_ref.at[:, pl.ds(pl.multiple_of(slot * 512 + yl * 256 + q * 32 + cc * 16, 16), 16), :]

    def child_cols(k):
        return hs_ref.at[:, :, pl.ds(pl.multiple_of(k * 512, 128), 512)]

    def stay_put(slot):
        return pltpu.make_async_copy(child_cols(c), land(slot, c), loc_sem.at[slot])

    def give(slot, d, e):
        return remote(
            child_cols(c if e == 0 else 1 - c), land(slot, c), x_s.at[d, e], x_r.at[slot, e], peers[d][e]
        )

    def givers(slot):
        if slot > 0:
            away = [give(slot, d, e) for d, e in ((0, 1), (1, 0), (3, 0), (1, 1), (3, 1))]
            return [(x == slot + 1, [stay_put(slot)], away, [give(slot, 2, e) for e in (0, 1)])]
        return [
            (jnp.logical_and(x < 2, x == c), [stay_put(0)], [give(0, d, 0) for d in (1, 3)], [give(0, 2, 0)]),
            (jnp.logical_and(x < 2, x != c), [], [give(0, d, 1) for d in (0, 1, 3)], [give(0, 2, 1)]),
        ]

    gifts = givers(0) + givers(1) + givers(2)
    for when, here, away, opposite in gifts:

        @pl.when(when)
        def _():
            for copy in away + here:
                copy.start()

    def give_opposite():
        for when, here, away, opposite in gifts:

            @pl.when(when)
            def _():
                for copy in opposite:
                    copy.start()

    def taken(slot):
        source = jnp.where(slot == 0, c, slot + 1)
        remote(land(slot, 1 - c), land(slot, 1 - c), x_s.at[1, 1], x_r.at[slot, 1], peers[1][1]).wait_recv()

        @pl.when(x != source)
        def _():
            remote(land(slot, c), land(slot, c), x_s.at[1, 0], x_r.at[slot, 0], peers[1][0]).wait_recv()

        @pl.when(x == source)
        def _():
            stay_put(slot).wait()

    sx = jnp.maximum(x - 2, 0)
    j0 = 2 * sx + yl
    j1 = 2 * sx + 1 - yl

    def top(k, j):
        return a0_ref.at[k, pl.ds(pl.multiple_of(j * 16, 16), 16), :]

    top_src = [hs_ref.at[k, :, pl.ds(1024, 1024)] for k in (0, 1)]
    top_own = [pltpu.make_async_copy(top_src[k], top(k, j0), loc_sem.at[3 + k]) for k in (0, 1)]
    top_y = [remote(top_src[k], top(k, j0), y0_s.at[k], y0_r.at[k], partner) for k in (0, 1)]
    top_y_in = [remote(top_src[k], top(k, j1), y0_s.at[k], y0_r.at[k], partner) for k in (0, 1)]
    top_x = [
        remote(top_src[k], top(k, j0), x0_s.at[n, 0, k], x0_r.at[sx, 0, k], xs[n]) for n in range(3) for k in (0, 1)
    ]
    top_x2 = [
        remote(top(k, j1), top(k, j1), x0_s.at[n, 1, k], x0_r.at[sx, 1, k], xs[n]) for n in range(3) for k in (0, 1)
    ]

    f_at = (f0, mod4(f0 - 1), mod4(f0 + 1), mod4(f0 + 2))
    g_at = (mod4(g0 - 1), mod4(g0 + 1), mod4(g0 + 2))

    def spread(slot, n):
        ref = slab(slot, f_at[n], g0)
        for d in (0, 1):
            go(remote(ref, ref, g_s.at[d, slot, n], g_r.at[d, slot, n], gs[d]))

    def open_slot(slot):
        taken(slot)
        for d in (0, 1):
            ref = slab(slot, f0, g0)
            go(remote(ref, ref, f_s.at[d, slot], f_r.at[d, slot], fs[d]))
        spread(slot, 0)

    def near(slot):
        for d in (0, 1):
            ref = slab(slot, f_at[1 + d], g0)
            remote(ref, ref, f_s.at[d, slot], f_r.at[d, slot], fs[d]).wait_recv()
            ref = part(slot, f_at[1 + d], g0, d)
            go(remote(ref, ref, fo_s.at[slot, d], fo_r.at[slot, d], fs[d]))
            spread(slot, 1 + d)

    def far(slot):
        for d in (0, 1):
            ref = part(slot, f_at[3], g0, d)
            remote(ref, ref, fo_s.at[slot, d], fo_r.at[slot, d], fs[d]).wait_recv()
        spread(slot, 3)

    def relay(slot, n):
        for d in (0, 1):
            ref = slab(slot, f_at[n], g_at[d])
            remote(ref, ref, g_s.at[d, slot, n], g_r.at[d, slot, n], gs[d]).wait_recv()
            ref = part(slot, f_at[n], g_at[d], d)
            go(remote(ref, ref, go_s.at[slot, n, d], go_r.at[slot, n, d], gs[d]))

    def close_slot(slot):
        for n in range(4):
            for d in (0, 1):
                ref = part(slot, f_at[n], g_at[2], d)
                remote(ref, ref, go_s.at[slot, n, d], go_r.at[slot, n, d], gs[d]).wait_recv()

    def top_start():
        @pl.when(root)
        def _():
            for copy in top_y + top_own + top_x:
                copy.start()

    def top_more():
        @pl.when(root)
        def _():
            for k in (0, 1):
                top_y_in[k].wait_recv()
            for copy in top_x2:
                copy.start()

    dinv_ref[...] = jnp.zeros_like(dinv_ref)

    def scale_rows(n):
        rows = slice(n * 64, n * 64 + 64)
        low = slice(n * 64 + C, n * 64 + C + 64)
        s = ab_ref[1, rows, :]
        re = ab_ref[0, rows, :] - sr * s
        im = -si * s
        eye = iota((64, C), 1) == iota((64, C), 0) + n * 64
        ir, ii = recip(
            jnp.sum(jnp.where(eye, re, 0.0), axis=1, keepdims=True),
            jnp.sum(jnp.where(eye, im, 0.0), axis=1, keepdims=True),
        )
        dinv_ref[0:1, :] += jnp.sum(jnp.where(eye, ir, 0.0), axis=0, keepdims=True)
        dinv_ref[1:2, :] += jnp.sum(jnp.where(eye, ii, 0.0), axis=0, keepdims=True)
        er, ei = rotate(re, im, -ir, -ii)
        for where, value in ((rows, er), (low, ei)):
            high, rest = split(jnp.where(eye, 0.0, value))
            ehl_ref[0, where, :] = high
            ehl_ref[1, where, :] = rest

    def pattern_at(j, half_at):
        return jnp.where(first, pat_ref[j, half_at], pat_ref[j, 2 + half_at]).astype(F32)

    def couple(h, s, j):
        m = jnp.where(iota((1, C), 1) < 256, pattern_at(j, 0), pattern_at(j, 1))
        s = s * m
        return h * m - sr * s, -si * s

    def split_rows(n):
        rows = slice(C + n * 64, C + n * 64 + 64)
        re, im = couple(ab_ref[0, rows, :], ab_ref[1, rows, :], n // 4)
        rows = slice(n * 64, n * 64 + 64)
        for at, value in ((0, re), (C, im)):
            high, rest = split(value)
            bhl_ref[0, rows, at : at + C] = high
            bhl_ref[1, rows, at : at + C] = rest

    def chain_start():
        for j in range(4):
            rows = pl.ds(pl.multiple_of(C + j * 256 + q * 32, 32), 32)
            re, im = couple(ab_ref[0, rows, :], ab_ref[1, rows, :], j)
            ct_ref[0, j * 32 : j * 32 + 32, :] = re
            ct_ref[1, j * 32 : j * 32 + 32, :] = im
        times(lhs, ehl_ref, cu_ref, ct_ref[0, 0:128, :], ct_ref[1, 0:128, :], C)
        cu_ref[0, 0:128, :] += ct_ref[0, 0:128, :]
        cu_ref[1, 0:128, :] += ct_ref[1, 0:128, :]
        for jj in range(2):
            at = pl.multiple_of(jj * 256 + q * 32, 32)
            low = pl.multiple_of(jj * 256 + q * 32 + C, 32)
            eye = iota((32, C), 1) == iota((32, C), 0) + at
            rows = slice(128 + jj * 32, 160 + jj * 32)
            er = ehl_ref[0, pl.ds(at, 32), :].astype(F32) + ehl_ref[1, pl.ds(at, 32), :].astype(F32)
            ei = ehl_ref[0, pl.ds(low, 32), :].astype(F32) + ehl_ref[1, pl.ds(low, 32), :].astype(F32)
            cu_ref[0, rows, :] = jnp.where(eye, 1.0, er)
            cu_ref[1, rows, :] = ei

    def chain_two():
        times(lhs, ehl_ref, ct_ref, cu_ref[0], cu_ref[1], C)

    def chain_three():
        times(lhs, ehl_ref, ct_ref, ct_ref[0], ct_ref[1], C)
        lr, li = rotate(cu_ref[0] + ct_ref[0], cu_ref[1] + ct_ref[1], dinv_ref[0:1, :], dinv_ref[1:2, :])
        xc_ref[0] = lr[128:192]
        xc_ref[1] = li[128:192]
        put_pair(lhs, lr[0:128], li[0:128])
        put_pair(lhs, lr[128:192], li[128:192], 512)

    def product(n):
        rows = slice(n * 256, n * 256 + 256)
        wide = dot_t(lhs[0:512, 0 : 2 * C], bhl_ref[0, rows, :])
        narrow = dot_t(lhs[0:256, 0 : 2 * C], bhl_ref[1, rows, :])
        pair = fold(wide, narrow, 128)
        for k in (0, 1):
            for b, (j, other) in enumerate(BLOCKS):
                if other == n:
                    for cc in (0, 1):
                        tb_ref[cc, b, k] = pair[k][j * 32 + cc * 16 : j * 32 + cc * 16 + 16]

    def product_w(n):
        rows = slice(n * 256, n * 256 + 256)
        wide = dot_t(lhs[512:768, 0 : 2 * C], bhl_ref[0, rows, :])
        narrow = dot_t(lhs[512:640, 0 : 2 * C], bhl_ref[1, rows, :])
        w_ref[0, :, rows], w_ref[1, :, rows] = fold(wide, narrow, 64)

    order = (jnp.maximum(x - 1, 0), jnp.where(x < 2, 1, 0), jnp.where(x == 3, 1, 2))

    def turn(stage, o, *more):
        return lambda: stage(order[o], *more)

    steps = [
        turn(open_slot, 0), give_opposite, turn(near, 0), turn(relay, 0, 0), turn(far, 0),
        turn(open_slot, 1), turn(open_slot, 2), top_start,
        turn(relay, 0, 1), turn(relay, 0, 2), turn(near, 1), turn(relay, 0, 3), turn(relay, 1, 0),
        turn(near, 2), turn(far, 1), turn(relay, 2, 0), turn(relay, 1, 1), turn(relay, 1, 2), top_more,
        turn(far, 2), turn(relay, 1, 3), turn(close_slot, 0), turn(close_slot, 1),
        lambda: scale_rows(0), lambda: scale_rows(1), turn(relay, 2, 1),
        lambda: scale_rows(2), lambda: scale_rows(3), turn(relay, 2, 2),
        lambda: scale_rows(4), lambda: scale_rows(5), lambda: scale_rows(6), turn(relay, 2, 3),
        lambda: scale_rows(7), chain_start, chain_two, chain_three, turn(close_slot, 2),
    ] + [lambda n=n: split_rows(n) for n in range(16)]
    for step in steps:
        step()

    for sx_in in (0, 1):
        jx = (2 * sx_in + yl, 2 * sx_in + 1 - yl)

        @pl.when(x != 2 + sx_in)
        def _():
            for o in (0, 1):
                for k in (0, 1):
                    ref = top(k, jx[o])
                    remote(ref, ref, x0_s.at[0, o, k], x0_r.at[sx_in, o, k], xs[0]).wait_recv()

    @pl.when(root)
    def _():
        for copy in top_own:
            copy.wait()

    swaps = [
        remote(tb_ref.at[1 - c, blocks], tin_ref.at[blocks], tt_s.at[n], tt_r.at[n], sibling)
        for n, blocks in enumerate(GROUPS_DS)
    ]
    def finish(n):
        for b in range(GROUPS[n].start, GROUPS[n].stop):
            j, other = BLOCKS[b]
            s = a0_ref[1, j * 16 : j * 16 + 16, other * 256 : other * 256 + 256]
            h = a0_ref[0, j * 16 : j * 16 + 16, other * 256 : other * 256 + 256]
            own_ref[b, 0] = h - sr * s - tb_ref[c, b, 0]
            own_ref[b, 1] = -si * s - tb_ref[c, b, 1]
        swaps[n].wait_recv()
        rows = GROUPS[n]
        own_ref[rows] = own_ref[rows] - tin_ref[rows]

    def whole(n, gg):
        return sg_ref.at[GROUPS_DS[n], :, gg]

    def piece(n, gg, k):
        return sg_ref.at[GROUPS_DS[n], k, gg]

    base = (g, g + 2 - 4 * yh)
    hop = [0] + [4 * (mod4(z + d) - z) for d in (-1, 1, 2)]

    def hand(n, m, o, ref_of):
        for k in (0, 1):
            ref = piece(n, base[o] + hop[m], k)
            go(remote(ref_of(k), ref, b_s.at[n, m, o, k], b_r.at[n, m, o, k], sibling))

    def along_z(n, o, src):
        dst = whole(n, base[o])
        for d in (0, 1):
            go(remote(dst if src is None else src, dst, z_s.at[d, n, o], z_r.at[d, n, o], zs[d]))

    keeps = []

    def launch(n):
        finish(n)
        src = own_ref.at[GROUPS_DS[n]]
        if n == 0:
            along_z(n, 0, src)
        go(remote(src, whole(n, g), y_s.at[n], y_r.at[n], over))
        if n == 1:
            along_z(n, 0, src)
        keep = pltpu.make_async_copy(src, whole(n, g), own_sem.at[n])
        keep.start()
        keeps.append(keep)
        hand(n, 0, 0, lambda k: own_ref.at[GROUPS_DS[n], k])

    def from_over(n):
        ref = whole(n, base[1])
        remote(ref, ref, y_s.at[n], y_r.at[n], over).wait_recv()
        hand(n, 0, 1, lambda k: piece(n, base[1], k))

    def from_z(n, o):
        for d in (0, 1):
            gg = base[o] + hop[1 + d]
            ref = whole(n, gg)
            remote(ref, ref, z_s.at[d, n, o], z_r.at[d, n, o], zs[d]).wait_recv()
            ref = piece(n, gg, d)
            go(remote(ref, ref, o_s.at[n, o, d], o_r.at[n, o, d], zs[d]))
            if n == 0:
                for k in (0, 1):
                    ref = piece(n, gg, k)
                    go(remote(ref, ref, yo_s.at[1 + d, k], yo_r.at[1 + d, k], over))
            hand(n, 1 + d, o, lambda k, gg=gg: piece(n, gg, k))

    def from_far(n, o):
        gg = base[o] + hop[3]
        for k in (0, 1):
            ref = piece(n, gg, k)
            remote(ref, ref, o_s.at[n, o, k], o_r.at[n, o, k], zs[k]).wait_recv()
            if n == 0:
                go(remote(ref, ref, yo_s.at[3, k], yo_r.at[3, k], over))
            go(remote(ref, ref, b_s.at[n, 3, o, k], b_r.at[n, 3, o, k], sibling))

    def over_far(m):
        gg = base[1] + hop[m]
        for k in (0, 1):
            ref = piece(0, gg, k)
            remote(ref, ref, yo_s.at[m, k], yo_r.at[m, k], over).wait_recv()
            go(remote(ref, ref, b_s.at[0, m, 1, k], b_r.at[0, m, 1, k], sibling))

    product(0)
    product(1)
    go(swaps[0])
    product(2)
    launch(0)
    product(3)
    go(swaps[1])
    product_w(0)
    launch(1)
    from_z(0, 0)
    product_w(1)
    from_over(1)
    along_z(1, 1, None)
    from_over(0)
    product_w(2)
    product_w(3)
    from_far(0, 0)
    from_z(1, 0)
    over_far(1)
    over_far(2)
    from_z(1, 1)
    from_far(1, 0)
    over_far(3)
    from_far(1, 1)

    def arrived(n):
        for m in range(4):
            for o in (0, 1):
                gg = base[o] + hop[m] + 1 - 2 * c
                for k in (0, 1):
                    ref = piece(n, gg, k)
                    remote(ref, ref, b_s.at[n, m, o, k], b_r.at[n, m, o, k], sibling).wait_recv()
        keeps[n].wait()

    def block(b, k):
        return sg_ref[b, k].reshape(256, 256)

    eye = iota((256, 256), 1) == iota((256, 256), 0)
    inverse = {}

    def diagonal(j):
        b = WHERE[(j, j)]
        ir, ii = recip(
            jnp.sum(jnp.where(eye, block(b, 0), 0.0), axis=1, keepdims=True),
            jnp.sum(jnp.where(eye, block(b, 1), 0.0), axis=1, keepdims=True),
        )
        cols = slice(j * 256, j * 256 + 256)
        d0_ref[0:1, cols] = jnp.sum(jnp.where(eye, ir, 0.0), axis=0, keepdims=True)
        d0_ref[1:2, cols] = jnp.sum(jnp.where(eye, ii, 0.0), axis=0, keepdims=True)
        inverse[j] = ir, ii

    def scale_block(j, other):
        rows = slice(j * 256, j * 256 + 256)
        low = slice(R + j * 256, R + j * 256 + 256)
        cols = slice(other * 256, other * 256 + 256)
        if (j, other) in WHERE:
            b = WHERE[(j, other)]
            re, im = block(b, 0), block(b, 1)
        else:
            b = WHERE[(other, j)]
            re, im = block(b, 0).T, block(b, 1).T
        ir, ii = inverse[j]
        er, ei = rotate(re, im, -ir, -ii)
        for where, value in ((rows, er), (low, ei)):
            if j == other:
                value = jnp.where(eye, 0.0, value)
            high, rest = split(value)
            shl_ref[0, where, cols] = high
            shl_ref[1, where, cols] = rest

    early = ((0, 0), (0, 1), (0, 3), (1, 0), (1, 1))
    arrived(0)
    diagonal(0)
    diagonal(1)
    for pair in early:
        scale_block(*pair)
    arrived(1)
    diagonal(2)
    diagonal(3)
    for j in range(4):
        for other in range(4):
            if (j, other) not in early:
                scale_block(j, other)
    times(lhs, shl_ref, u_ref, w_ref[0], w_ref[1], R)
    u_ref[0, 0:64, :] += w_ref[0]
    u_ref[1, 0:64, :] += w_ref[1]
    for j in range(4):
        at = pl.multiple_of(j * 256 + g * 16, 16)
        low = pl.multiple_of(j * 256 + g * 16 + R, 16)
        on = iota((16, R), 1) == iota((16, R), 0) + at
        rows = slice(64 + j * 16, 80 + j * 16)
        er = shl_ref[0, pl.ds(at, 16), :].astype(F32) + shl_ref[1, pl.ds(at, 16), :].astype(F32)
        ei = shl_ref[0, pl.ds(low, 16), :].astype(F32) + shl_ref[1, pl.ds(low, 16), :].astype(F32)
        u_ref[0, rows, :] = jnp.where(on, 1.0, er)
        u_ref[1, rows, :] = ei
    times(lhs, shl_ref, t_ref, u_ref[0], u_ref[1], R)
    times(lhs, shl_ref, t_ref, t_ref[0, 0:64], t_ref[1, 0:64], R)
    yr, yi = rotate(
        u_ref[0, 0:64] + t_ref[0, 0:64], u_ref[1, 0:64] + t_ref[1, 0:64], d0_ref[0:1, :], d0_ref[1:2, :]
    )
    u_ref[0, 0:64, :] = yr
    u_ref[1, 0:64, :] = yi
    weighted = -(wr * yr - wi * yi)
    for j in range(4):
        cols = slice(j * 256, j * 256 + 256)
        m = jnp.where(iota((64, 1), 0) < 32, pattern_at(j, 0), pattern_at(j, 1))
        side = weighted[:, cols] * m
        fw_ref[:, cols] = side
        turned = side.T.reshape(16, 2, 8, 64)
        ft_ref[j] = jnp.concatenate([turned[:, 0], turned[:, 1]], axis=2)

    for d, gg in enumerate(grids):
        go(remote(ft_ref.at[:, gg], ea_ref.at[g], a_s.at[d], a_r.at[d], (p, gg)))
    keep = pltpu.make_async_copy(ft_ref.at[:, g], ea_ref.at[g], keep_sem)
    keep.start()
    sent = []

    def send_or_keep(src, dst, ss, rs, target, here):
        away = remote(src, dst, ss, rs, target)
        stay = pltpu.make_async_copy(src, dst, ss)

        @pl.when(jnp.logical_not(here))
        def _():
            away.start()

        @pl.when(here)
        def _():
            stay.start()

        sent.append((here, away, stay))

    def child_rows():
        for jj in (0, 1):
            for cc in (0, 1):
                here = jnp.logical_and(p == 2 * c + jj, c == cc)
                rows = pl.ds(jj * 32 + cc * 16, 16)
                send_or_keep(
                    dw_ref.at[rows, :], rd_ref.at[p], sd_s.at[jj, cc], sd_r.at[p], (2 * c + jj, 2 * q + cc), here
                )

    for jj in (0, 1):
        for cc in (0, 1):
            send_or_keep(
                fw_ref.at[pl.ds(jj * 32 + cc * 16, 16), :], rf_ref.at[x, jj], sf_s.at[jj, cc], sf_r.at[x, jj],
                (2 * c + yl, 2 * q + cc), jnp.logical_and(x == c, c == cc),
            )

    times(lhs, shl_ref, t_ref, t_ref[0, 64:128], t_ref[1, 64:128], R)
    gr, gi = rotate(
        u_ref[0, 64:128] + t_ref[0, 0:64], u_ref[1, 64:128] + t_ref[1, 0:64], d0_ref[0:1, :], d0_ref[1:2, :]
    )
    gw_ref[...] = wr * gr - wi * gi
    for j in range(4):
        xx = 2 + j // 2
        send_or_keep(
            gw_ref.at[pl.ds(j * 16, 16), :], rf_ref.at[x, j % 2], sg_s.at[j], sf_r.at[x, j % 2], (2 * xx + yl, g), x == xx
        )

    keep.wait()
    for d in range(15):
        gg = lax.rem(g + 15 - d, 16)
        remote(ea_ref.at[gg], ea_ref.at[gg], a_s.at[d], a_r.at[d], (p, grids[0])).wait_recv()
    for j in range(4):
        send_or_keep(ea_ref.at[:, j], re_ref.at[p], se_s.at[j], se_r.at[p], (4 + j, g), p == 4 + j)

    yr, yi = u_ref[0, 0:64, :], u_ref[1, 0:64, :]
    rh, rl = split(yr)
    ih, il = split(yi)
    for at, (re, im) in enumerate(((rh, ih), (rl, il))):
        lhs[at * 128 : at * 128 + 64, 0:R] = re
        lhs[at * 128 + 64 : at * 128 + 128, 0:R] = im
        lhs[at * 128 : at * 128 + 64, R : 2 * R] = -im
        lhs[at * 128 + 64 : at * 128 + 128, R : 2 * R] = re
    wide = dot(lhs[0:256, 0:R], bhl_ref[0, :, 0:C]) + dot(lhs[0:256, R : 2 * R], bhl_ref[0, :, C : 2 * C])
    narrow = dot(lhs[0:128, 0:R], bhl_ref[1, :, 0:C]) + dot(lhs[0:128, R : 2 * R], bhl_ref[1, :, C : 2 * C])
    pr, pi = fold(wide, narrow, 64)

    times(lhs, ehl_ref, k_ref, pr, pi, C)
    ku_ref[0] = k_ref[0] + pr
    ku_ref[1] = k_ref[1] + pi
    times(lhs, ehl_ref, k_ref, ku_ref[0], ku_ref[1], C)
    times(lhs, ehl_ref, k_ref, k_ref[0], k_ref[1], C)
    zr, zi = rotate(ku_ref[0] + k_ref[0], ku_ref[1] + k_ref[1], dinv_ref[0:1, :], dinv_ref[1:2, :])
    dw_ref[...] = wr * (xc_ref[0] + zr) - wi * (xc_ref[1] + zi)
    child_rows()

    for here, away, stay in sent:

        @pl.when(here)
        def _():
            stay.wait()

    lead = p >= 4
    same = jnp.logical_or(lead, c == half(p))
    for d in range(4):
        xx = mod4(x + d)

        @pl.when(jnp.logical_or(jnp.logical_not(same), d > 0))
        def _():
            for n in (0, 1):
                remote(rf_ref.at[xx, n], rf_ref.at[xx, n], sf_s.at[0, 0], sf_r.at[xx, n], partner).wait_recv()

    pre_ref[...] = rf_ref[0, 1 - yl] + rf_ref[1, 1 - yl] + rf_ref[2, 1 - yl] + rf_ref[3, 1 - yl]
    cross = remote(pre_ref, pin_ref, pre_s, pre_r, partner)
    go(cross)
    for d in range(8):
        pp = poles[d]

        @pl.when(jnp.logical_and(jnp.logical_not(lead), jnp.logical_or(jnp.logical_not(same), d > 0)))
        def _():
            remote(rd_ref.at[pp], rd_ref.at[pp], sd_s.at[0, 0], sd_r.at[pp], partner).wait_recv()

    def total(ref):
        value = ref[0]
        for n in range(1, 8):
            value = value + ref[n]
        return value

    @pl.when(lead)
    def _():
        for d in range(1, 8):
            pp = poles[d]
            remote(re_ref.at[pp], re_ref.at[pp], se_s.at[0], se_r.at[pp], partner).wait_recv()
        side = total(re_ref)
        for k in (0, 1):
            for jj in (0, 1):
                at = k * 512 + jj * 256
                for top_half in (0, 1):
                    lane = top_half * 64 + jj * 32
                    cols = [side[2 * qq + k][:, lane : lane + 32] for qq in range(8)]
                    left_ref[top_half * 8 : top_half * 8 + 8, at : at + 256] = jnp.concatenate(cols, axis=1)

    @pl.when(jnp.logical_not(lead))
    def _():
        diag = total(rd_ref)
        upper = p < 2
        left_ref[:, 0:C] = jnp.where(upper, diag, 0.0)
        left_ref[:, C : 2 * C] = jnp.where(upper, 0.0, diag)

    main = rf_ref[0, yl] + rf_ref[1, yl] + rf_ref[2, yl] + rf_ref[3, yl]
    cross.wait_recv()
    right_ref[...] = main + pin_ref[...]

    for here, away, stay in sent:

        @pl.when(jnp.logical_not(here))
        def _():
            away.wait_send()

    for copy in pending:
        copy.wait_send()

    for when, here, away, opposite in gifts:

        @pl.when(when)
        def _():
            for copy in away + opposite:
                copy.wait_send()

    @pl.when(root)
    def _():
        for copy in top_y + top_x + top_x2:
            copy.wait_send()


GROUPS_DS = tuple(pl.ds(blocks.start, blocks.stop - blocks.start) for blocks in GROUPS)


def local(hamiltonian, margin, pattern, shift_real, shift_imag, residue):
    dma = pltpu.SemaphoreType.DMA
    vm = pltpu.VMEM
    left, right = pl.pallas_call(
        kernel,
        name="selected_inversion",
        out_shape=(jax.ShapeDtypeStruct((16, R), F32), jax.ShapeDtypeStruct((16, R), F32)),
        in_specs=[ANY, ANY, SM, SM, SM, SM],
        out_specs=(VM, VM),
        scratch_shapes=[
            vm((2, 16, 2 * R), F32), vm((2, 1536, 512), F32), vm((2, 64, 1024), F32), vm((2, 1024, C), BF16), vm((2, R, 2 * C), BF16),
            vm((8, C), F32), vm((768, 2 * R), BF16), vm((2, 192, C), F32), vm((2, 192, C), F32),
            vm((2, 64, C), F32), vm((2, 64, R), F32), vm((2, NB, 2, 16, 256), F32),
            vm((NB, 2, 16, 256), F32), vm((NB, 2, 16, 256), F32), vm((NB, 2, 16, 16, 256), F32),
            vm((2, 2 * R, R), BF16), vm((8, R), F32), vm((2, 128, R), F32), vm((2, 128, R), F32),
            vm((2, 64, C), F32), vm((2, 64, C), F32), vm((64, R), F32), vm((4, 16, 8, 128), F32),
            vm((64, R), F32), vm((64, C), F32),
            vm((4, 2, 16, R), F32), vm((8, 16, C), F32), vm((8, 16, 8, 128), F32), vm((16, 4, 8, 128), F32),
            vm((16, R), F32), vm((16, R), F32),
            dma((5,)), dma((4, 2)), dma((3, 2)),
            dma((2, 3)), dma((2, 3)), dma((3, 2)), dma((3, 2)),
            dma((2, 3, 4)), dma((2, 3, 4)), dma((3, 4, 2)), dma((3, 4, 2)),
            dma((2,)), dma((2,)), dma((3, 2, 2)), dma((2, 2, 2)),
            dma((2,)), dma((2,)), dma((2,)), dma((2,)), dma((2,)), dma((4, 2)), dma((4, 2)),
            dma((2, 2, 2)), dma((2, 2, 2)), dma((2, 2, 2)), dma((2, 2, 2)),
            dma((2, 4, 2, 2)), dma((2, 4, 2, 2)),
            dma, dma, dma, dma((15,)), dma((15,)), dma((2, 2)), dma((4, 2)), dma((2, 2)), dma((8,)),
            dma((4,)), dma((4,)), dma((8,)),
        ],
        compiler_params=pltpu.CompilerParams(
            collective_id=0, has_side_effects=True, vmem_limit_bytes=56 << 20
        ),
        cost_estimate=pl.CostEstimate(flops=12 << 30, bytes_accessed=1 << 20, transcendentals=0),
    )(hamiltonian, margin, pattern, shift_real, shift_imag, residue)
    return jnp.concatenate([left, right], axis=1)


def solution(mesh):
    return jax.shard_map(
        local,
        mesh=mesh,
        in_specs=(
            P(("pole", "grid"), None),
            P(("pole", "grid"), None),
            P(),
            P("pole"),
            P("pole"),
            P("pole", None),
        ),
        out_specs=P(("pole", "grid"), None),
        check_vma=False,
    )
```

```python
import jax
import jax.numpy as jnp
from jax import lax
from jax.experimental import pallas as pl
from jax.experimental.pallas import tpu as pltpu
from jax.sharding import PartitionSpec as P

C = 512
R = 1024
F32 = jnp.float32
BF16 = jnp.bfloat16
MESH = pl.DeviceIdType.MESH
ANY = pl.BlockSpec(memory_space=pl.ANY)
VM = pl.BlockSpec(memory_space=pltpu.VMEM)
SM = pl.BlockSpec(memory_space=pltpu.SMEM)
BLOCKS = ((0, 0), (3, 0), (0, 1), (1, 1), (0, 2), (1, 2), (2, 2), (1, 3), (2, 3), (3, 3))
WHERE = {pair: b for b, pair in enumerate(BLOCKS)}
NB = len(BLOCKS)
GROUPS = (slice(0, 4), slice(4, 10))


def mod4(v):
    return lax.rem(v + 4, 4)


def half(v):
    return lax.div(v, 2)


def place():
    p = lax.axis_index("pole")
    g = lax.axis_index("grid")
    x, yl = half(p), lax.rem(p, 2)
    z, q, c = lax.div(g, 4), half(g), lax.rem(g, 2)
    return p, g, x, yl, z, lax.rem(q, 2), q, c


def spot(x, y, z, c):
    return (2 * x + lax.rem(y, 2), 4 * z + 2 * half(y) + c)


def greet(devices):
    barrier = pltpu.get_barrier_semaphore()
    for device in devices:
        pl.semaphore_signal(barrier, inc=1, device_id=device, device_id_type=MESH)
    pl.semaphore_wait(barrier, len(devices))


def remote(src, dst, send, recv, device):
    return pltpu.make_async_remote_copy(
        src_ref=src, dst_ref=dst, send_sem=send, recv_sem=recv, device_id=device, device_id_type=MESH
    )


def split(v):
    high = v.astype(BF16)
    return high, (v - high.astype(F32)).astype(BF16)


def put_pair(lhs_ref, vr, vi, start=0):
    m, k = vr.shape
    rh, rl = split(vr)
    ih, il = split(vi)
    for at, (re, im) in enumerate(((rh, ih), (rl, il))):
        base = start + at * 2 * m
        lhs_ref[base : base + m, 0:k] = re
        lhs_ref[base : base + m, k : 2 * k] = -im
        lhs_ref[base + m : base + 2 * m, 0:k] = im
        lhs_ref[base + m : base + 2 * m, k : 2 * k] = re


def fold(wide, narrow, m):
    total = wide[0 : 2 * m] + wide[2 * m : 4 * m] + narrow
    return total[0:m], total[m : 2 * m]


def dot(a, b):
    return jnp.dot(a, b, preferred_element_type=F32)


def dot_t(a, b):
    return lax.dot_general(a, b, (((1,), (1,)), ((), ())), preferred_element_type=F32)


def times(lhs_ref, rhs_ref, out_ref, vr, vi, width):
    m, k = vr.shape
    put_pair(lhs_ref, vr, vi)
    for n in range(width // 256):
        cols = slice(n * 256, n * 256 + 256)
        wide = dot(lhs_ref[0 : 4 * m, 0 : 2 * k], rhs_ref[0, :, cols])
        narrow = dot(lhs_ref[0 : 2 * m, 0 : 2 * k], rhs_ref[1, :, cols])
        re, im = fold(wide, narrow, m)
        out_ref[0, 0:m, cols] = re
        out_ref[1, 0:m, cols] = im


def rotate(vr, vi, dr, di):
    return vr * dr - vi * di, vr * di + vi * dr


def recip(dr, di):
    den = dr * dr + di * di
    return dr / den, -di / den


def iota(shape, dim):
    return lax.broadcasted_iota(jnp.int32, shape, dim)


def kernel(
    h_ref, s_ref, pat_ref, sr_ref, si_ref, res_ref, left_ref, right_ref,
    hs_ref, ab_ref, a0_ref, ehl_ref, bhl_ref, dinv_ref, lhs, cu_ref, ct_ref, xc_ref, w_ref, tb_ref,
    tin_ref, own_ref, sg_ref, shl_ref, d0_ref, u_ref, t_ref,
    k_ref, ku_ref, fw_ref, ft_ref, gw_ref, dw_ref, rf_ref, rd_ref, re_ref, ea_ref, pre_ref, pin_ref,
    loc_sem, x_s, x_r, f_s, f_r, fo_s, fo_r, g_s, g_r, go_s, go_r,
    y0_s, y0_r, x0_s, x0_r,
    tt_s, tt_r, own_sem, y_s, y_r, yo_s, yo_r, z_s, z_r, o_s, o_r, b_s, b_r,
    pre_s, pre_r, keep_sem, a_s, a_r, sf_s, sf_r, sd_s, sd_r, sg_s, se_s, se_r,
):
    p, g, x, yl, z, yh, q, c = place()
    y = 2 * yh + yl
    sr, si = sr_ref[0], si_ref[0]
    wr, wi = res_ref[0, 0], res_ref[0, 1]
    sib = g + 1 - 2 * c
    sibling = (p, sib)
    partner = (p + 1 - 2 * yl, g)
    over = (p, g + 2 - 4 * yh)
    xs = [spot(mod4(x + d), y, z, c) for d in (1, 2, 3)]
    ys = [spot(x, mod4(y + d), z, c) for d in (1, -1)]
    zs = [spot(x, y, mod4(z + d), c) for d in (1, -1)]
    poles = [lax.rem(p + d, 8) for d in range(8)]
    grids = [lax.rem(g + d, 16) for d in range(1, 16)]
    peers = [[spot(mod4(x + d), y, z, cc) for cc in (c, 1 - c)] for d in range(4)]
    loads = [pltpu.make_async_copy(ref, hs_ref.at[k], loc_sem.at[k]) for k, ref in enumerate((h_ref, s_ref))]
    for copy in loads:
        copy.start()
    greet([peers[d][e] for d in range(4) for e in (0, 1) if d + e > 0] + ys + zs)

    for copy in loads:
        copy.wait()
    pending = []

    def go(copy):
        copy.start()
        pending.append(copy)

    first = c == 0

    def pick(a, b):
        return tuple(jnp.where(first, u, v) for u, v in zip(a, b))

    fs = [pick(ys[i], zs[i]) for i in (0, 1)]
    gs = [pick(zs[i], ys[i]) for i in (0, 1)]
    f0 = jnp.where(first, y, z)
    g0 = jnp.where(first, z, y)

    def row(slot, f, s):
        yy, zz = jnp.where(first, f, s), jnp.where(first, s, f)
        return pl.multiple_of(slot * 512 + lax.rem(yy, 2) * 256 + (2 * zz + half(yy)) * 32, 32)

    def slab(slot, f, s):
        return ab_ref.at[:, pl.ds(row(slot, f, s), 32), :]

    def part(slot, f, s, k):
        return ab_ref.at[k, pl.ds(row(slot, f, s), 32), :]

    root = x >= 2

    def land(slot, cc):
        return ab_ref.at[:, pl.ds(pl.multiple_of(slot * 512 + yl * 256 + q * 32 + cc * 16, 16), 16), :]

    def child_cols(k):
        return hs_ref.at[:, :, pl.ds(pl.multiple_of(k * 512, 128), 512)]

    def stay_put(slot):
        return pltpu.make_async_copy(child_cols(c), land(slot, c), loc_sem.at[slot])

    def give(slot, d, e):
        return remote(
            child_cols(c if e == 0 else 1 - c), land(slot, c), x_s.at[d, e], x_r.at[slot, e], peers[d][e]
        )

    def givers(slot):
        if slot > 0:
            away = [give(slot, d, e) for d, e in ((0, 1), (1, 0), (3, 0), (1, 1), (3, 1))]
            return [(x == slot + 1, [stay_put(slot)], away, [give(slot, 2, e) for e in (0, 1)])]
        return [
            (jnp.logical_and(x < 2, x == c), [stay_put(0)], [give(0, d, 0) for d in (1, 3)], [give(0, 2, 0)]),
            (jnp.logical_and(x < 2, x != c), [], [give(0, d, 1) for d in (0, 1, 3)], [give(0, 2, 1)]),
        ]

    gifts = givers(0) + givers(1) + givers(2)
    for when, here, away, opposite in gifts:

        @pl.when(when)
        def _():
            for copy in away + here:
                copy.start()

    def give_opposite():
        for when, here, away, opposite in gifts:

            @pl.when(when)
            def _():
                for copy in opposite:
                    copy.start()

    def taken(slot):
        source = jnp.where(slot == 0, c, slot + 1)
        remote(land(slot, 1 - c), land(slot, 1 - c), x_s.at[1, 1], x_r.at[slot, 1], peers[1][1]).wait_recv()

        @pl.when(x != source)
        def _():
            remote(land(slot, c), land(slot, c), x_s.at[1, 0], x_r.at[slot, 0], peers[1][0]).wait_recv()

        @pl.when(x == source)
        def _():
            stay_put(slot).wait()

    sx = jnp.maximum(x - 2, 0)
    j0 = 2 * sx + yl
    j1 = 2 * sx + 1 - yl

    def top(k, j):
        return a0_ref.at[k, pl.ds(pl.multiple_of(j * 16, 16), 16), :]

    top_src = [hs_ref.at[k, :, pl.ds(1024, 1024)] for k in (0, 1)]
    top_own = [pltpu.make_async_copy(top_src[k], top(k, j0), loc_sem.at[3 + k]) for k in (0, 1)]
    top_y = [remote(top_src[k], top(k, j0), y0_s.at[k], y0_r.at[k], partner) for k in (0, 1)]
    top_y_in = [remote(top_src[k], top(k, j1), y0_s.at[k], y0_r.at[k], partner) for k in (0, 1)]
    top_x = [
        remote(top_src[k], top(k, j0), x0_s.at[n, 0, k], x0_r.at[sx, 0, k], xs[n]) for n in range(3) for k in (0, 1)
    ]
    top_x2 = [
        remote(top(k, j1), top(k, j1), x0_s.at[n, 1, k], x0_r.at[sx, 1, k], xs[n]) for n in range(3) for k in (0, 1)
    ]

    f_at = (f0, mod4(f0 - 1), mod4(f0 + 1), mod4(f0 + 2))
    g_at = (mod4(g0 - 1), mod4(g0 + 1), mod4(g0 + 2))

    def spread(slot, n):
        ref = slab(slot, f_at[n], g0)
        for d in (0, 1):
            go(remote(ref, ref, g_s.at[d, slot, n], g_r.at[d, slot, n], gs[d]))

    def open_slot(slot):
        taken(slot)
        for d in (0, 1):
            ref = slab(slot, f0, g0)
            go(remote(ref, ref, f_s.at[d, slot], f_r.at[d, slot], fs[d]))
        spread(slot, 0)

    def near(slot):
        for d in (0, 1):
            ref = slab(slot, f_at[1 + d], g0)
            remote(ref, ref, f_s.at[d, slot], f_r.at[d, slot], fs[d]).wait_recv()
            ref = part(slot, f_at[1 + d], g0, d)
            go(remote(ref, ref, fo_s.at[slot, d], fo_r.at[slot, d], fs[d]))
            spread(slot, 1 + d)

    def far(slot):
        for d in (0, 1):
            ref = part(slot, f_at[3], g0, d)
            remote(ref, ref, fo_s.at[slot, d], fo_r.at[slot, d], fs[d]).wait_recv()
        spread(slot, 3)

    def relay(slot, n):
        for d in (0, 1):
            ref = slab(slot, f_at[n], g_at[d])
            remote(ref, ref, g_s.at[d, slot, n], g_r.at[d, slot, n], gs[d]).wait_recv()
            ref = part(slot, f_at[n], g_at[d], d)
            go(remote(ref, ref, go_s.at[slot, n, d], go_r.at[slot, n, d], gs[d]))

    def close_slot(slot):
        for n in range(4):
            for d in (0, 1):
                ref = part(slot, f_at[n], g_at[2], d)
                remote(ref, ref, go_s.at[slot, n, d], go_r.at[slot, n, d], gs[d]).wait_recv()

    def top_start():
        @pl.when(root)
        def _():
            for copy in top_y + top_own + top_x:
                copy.start()

    def top_more():
        @pl.when(root)
        def _():
            for k in (0, 1):
                top_y_in[k].wait_recv()
            for copy in top_x2:
                copy.start()

    dinv_ref[...] = jnp.zeros_like(dinv_ref)

    def scale_rows(n):
        rows = slice(n * 64, n * 64 + 64)
        low = slice(n * 64 + C, n * 64 + C + 64)
        s = ab_ref[1, rows, :]
        re = ab_ref[0, rows, :] - sr * s
        im = -si * s
        eye = iota((64, C), 1) == iota((64, C), 0) + n * 64
        ir, ii = recip(
            jnp.sum(jnp.where(eye, re, 0.0), axis=1, keepdims=True),
            jnp.sum(jnp.where(eye, im, 0.0), axis=1, keepdims=True),
        )
        dinv_ref[0:1, :] += jnp.sum(jnp.where(eye, ir, 0.0), axis=0, keepdims=True)
        dinv_ref[1:2, :] += jnp.sum(jnp.where(eye, ii, 0.0), axis=0, keepdims=True)
        er, ei = rotate(re, im, -ir, -ii)
        for where, value in ((rows, er), (low, ei)):
            high, rest = split(jnp.where(eye, 0.0, value))
            ehl_ref[0, where, :] = high
            ehl_ref[1, where, :] = rest

    def pattern_at(j, half_at):
        return jnp.where(first, pat_ref[j, half_at], pat_ref[j, 2 + half_at]).astype(F32)

    def couple(h, s, j):
        m = jnp.where(iota((1, C), 1) < 256, pattern_at(j, 0), pattern_at(j, 1))
        s = s * m
        return h * m - sr * s, -si * s

    def split_rows(n):
        rows = slice(C + n * 64, C + n * 64 + 64)
        re, im = couple(ab_ref[0, rows, :], ab_ref[1, rows, :], n // 4)
        rows = slice(n * 64, n * 64 + 64)
        for at, value in ((0, re), (C, im)):
            high, rest = split(value)
            bhl_ref[0, rows, at : at + C] = high
            bhl_ref[1, rows, at : at + C] = rest

    def chain_start():
        for j in range(4):
            rows = pl.ds(pl.multiple_of(C + j * 256 + q * 32, 32), 32)
            re, im = couple(ab_ref[0, rows, :], ab_ref[1, rows, :], j)
            ct_ref[0, j * 32 : j * 32 + 32, :] = re
            ct_ref[1, j * 32 : j * 32 + 32, :] = im
        times(lhs, ehl_ref, cu_ref, ct_ref[0, 0:128, :], ct_ref[1, 0:128, :], C)
        cu_ref[0, 0:128, :] += ct_ref[0, 0:128, :]
        cu_ref[1, 0:128, :] += ct_ref[1, 0:128, :]
        for jj in range(2):
            at = pl.multiple_of(jj * 256 + q * 32, 32)
            low = pl.multiple_of(jj * 256 + q * 32 + C, 32)
            eye = iota((32, C), 1) == iota((32, C), 0) + at
            rows = slice(128 + jj * 32, 160 + jj * 32)
            er = ehl_ref[0, pl.ds(at, 32), :].astype(F32) + ehl_ref[1, pl.ds(at, 32), :].astype(F32)
            ei = ehl_ref[0, pl.ds(low, 32), :].astype(F32) + ehl_ref[1, pl.ds(low, 32), :].astype(F32)
            cu_ref[0, rows, :] = jnp.where(eye, 1.0, er)
            cu_ref[1, rows, :] = ei

    def chain_two():
        times(lhs, ehl_ref, ct_ref, cu_ref[0], cu_ref[1], C)

    def chain_three():
        times(lhs, ehl_ref, ct_ref, ct_ref[0], ct_ref[1], C)
        lr, li = rotate(cu_ref[0] + ct_ref[0], cu_ref[1] + ct_ref[1], dinv_ref[0:1, :], dinv_ref[1:2, :])
        xc_ref[0] = lr[128:192]
        xc_ref[1] = li[128:192]
        put_pair(lhs, lr[0:128], li[0:128])
        put_pair(lhs, lr[128:192], li[128:192], 512)

    def product(n):
        rows = slice(n * 256, n * 256 + 256)
        wide = dot_t(lhs[0:512, 0 : 2 * C], bhl_ref[0, rows, :])
        narrow = dot_t(lhs[0:256, 0 : 2 * C], bhl_ref[1, rows, :])
        pair = fold(wide, narrow, 128)
        for k in (0, 1):
            for b, (j, other) in enumerate(BLOCKS):
                if other == n:
                    for cc in (0, 1):
                        tb_ref[cc, b, k] = pair[k][j * 32 + cc * 16 : j * 32 + cc * 16 + 16]

    def product_w(n):
        rows = slice(n * 256, n * 256 + 256)
        wide = dot_t(lhs[512:768, 0 : 2 * C], bhl_ref[0, rows, :])
        narrow = dot_t(lhs[512:640, 0 : 2 * C], bhl_ref[1, rows, :])
        w_ref[0, :, rows], w_ref[1, :, rows] = fold(wide, narrow, 64)

    order = (jnp.maximum(x - 1, 0), jnp.where(x < 2, 1, 0), jnp.where(x == 3, 1, 2))

    def turn(stage, o, *more):
        return lambda: stage(order[o], *more)

    steps = [
        turn(open_slot, 0), give_opposite, turn(near, 0), turn(relay, 0, 0), turn(far, 0),
        turn(open_slot, 1), turn(open_slot, 2), top_start,
        turn(relay, 0, 1), turn(relay, 0, 2), turn(near, 1), turn(relay, 0, 3), turn(relay, 1, 0),
        turn(near, 2), turn(far, 1), turn(relay, 2, 0), turn(relay, 1, 1), turn(relay, 1, 2), top_more,
        turn(far, 2), turn(relay, 1, 3), turn(close_slot, 0), turn(close_slot, 1),
        lambda: scale_rows(0), lambda: scale_rows(1), turn(relay, 2, 1),
        lambda: scale_rows(2), lambda: scale_rows(3), turn(relay, 2, 2),
        lambda: scale_rows(4), lambda: scale_rows(5), lambda: scale_rows(6), turn(relay, 2, 3),
        lambda: scale_rows(7), chain_start, chain_two, chain_three, turn(close_slot, 2),
    ] + [lambda n=n: split_rows(n) for n in range(16)]
    for step in steps:
        step()

    for sx_in in (0, 1):
        jx = (2 * sx_in + yl, 2 * sx_in + 1 - yl)

        @pl.when(x != 2 + sx_in)
        def _():
            for o in (0, 1):
                for k in (0, 1):
                    ref = top(k, jx[o])
                    remote(ref, ref, x0_s.at[0, o, k], x0_r.at[sx_in, o, k], xs[0]).wait_recv()

    @pl.when(root)
    def _():
        for copy in top_own:
            copy.wait()

    swaps = [
        remote(tb_ref.at[1 - c, blocks], tin_ref.at[blocks], tt_s.at[n], tt_r.at[n], sibling)
        for n, blocks in enumerate(GROUPS_DS)
    ]
    def finish(n):
        for b in range(GROUPS[n].start, GROUPS[n].stop):
            j, other = BLOCKS[b]
            s = a0_ref[1, j * 16 : j * 16 + 16, other * 256 : other * 256 + 256]
            h = a0_ref[0, j * 16 : j * 16 + 16, other * 256 : other * 256 + 256]
            own_ref[b, 0] = h - sr * s - tb_ref[c, b, 0]
            own_ref[b, 1] = -si * s - tb_ref[c, b, 1]
        swaps[n].wait_recv()
        rows = GROUPS[n]
        own_ref[rows] = own_ref[rows] - tin_ref[rows]

    def whole(n, gg):
        return sg_ref.at[GROUPS_DS[n], :, gg]

    def piece(n, gg, k):
        return sg_ref.at[GROUPS_DS[n], k, gg]

    base = (g, g + 2 - 4 * yh)
    hop = [0] + [4 * (mod4(z + d) - z) for d in (-1, 1, 2)]

    def hand(n, m, o, src=None):
        dst = whole(n, base[o] + hop[m])
        go(remote(dst if src is None else src, dst, b_s.at[n, m, o, 0], b_r.at[n, m, o, 0], sibling))

    def along_z(n, o, src):
        dst = whole(n, base[o])
        for d in (0, 1):
            go(remote(dst if src is None else src, dst, z_s.at[d, n, o], z_r.at[d, n, o], zs[d]))

    keeps = []

    def launch(n):
        finish(n)
        src = own_ref.at[GROUPS_DS[n]]
        if n == 0:
            along_z(n, 0, src)
        go(remote(src, whole(n, g), y_s.at[n], y_r.at[n], over))
        if n == 1:
            along_z(n, 0, src)
        keep = pltpu.make_async_copy(src, whole(n, g), own_sem.at[n])
        keep.start()
        keeps.append(keep)
        hand(n, 0, 0, src)

    def from_over(n):
        ref = whole(n, base[1])
        remote(ref, ref, y_s.at[n], y_r.at[n], over).wait_recv()
        hand(n, 0, 1)

    def from_z(n, o):
        for d in (0, 1):
            gg = base[o] + hop[1 + d]
            ref = whole(n, gg)
            remote(ref, ref, z_s.at[d, n, o], z_r.at[d, n, o], zs[d]).wait_recv()
            ref = piece(n, gg, d)
            go(remote(ref, ref, o_s.at[n, o, d], o_r.at[n, o, d], zs[d]))
            if n == 0:
                ref = whole(n, gg)
                go(remote(ref, ref, yo_s.at[1 + d, 0], yo_r.at[1 + d, 0], over))
            hand(n, 1 + d, o)

    def from_far(n, o):
        gg = base[o] + hop[3]
        for k in (0, 1):
            ref = piece(n, gg, k)
            remote(ref, ref, o_s.at[n, o, k], o_r.at[n, o, k], zs[k]).wait_recv()
            if n == 0:
                go(remote(ref, ref, yo_s.at[3, k], yo_r.at[3, k], over))
            go(remote(ref, ref, b_s.at[n, 3, o, k], b_r.at[n, 3, o, k], sibling))

    def over_far(m):
        gg = base[1] + hop[m]
        if m < 3:
            ref = whole(0, gg)
            remote(ref, ref, yo_s.at[m, 0], yo_r.at[m, 0], over).wait_recv()
            hand(0, m, 1)
            return
        for k in (0, 1):
            ref = piece(0, gg, k)
            remote(ref, ref, yo_s.at[m, k], yo_r.at[m, k], over).wait_recv()
            go(remote(ref, ref, b_s.at[0, m, 1, k], b_r.at[0, m, 1, k], sibling))

    product(0)
    product(1)
    go(swaps[0])
    product(2)
    launch(0)
    product(3)
    go(swaps[1])
    product_w(0)
    launch(1)
    from_z(0, 0)
    product_w(1)
    from_over(1)
    along_z(1, 1, None)
    from_over(0)
    product_w(2)
    product_w(3)
    from_far(0, 0)
    from_z(1, 0)
    over_far(1)
    over_far(2)
    from_z(1, 1)
    from_far(1, 0)
    over_far(3)
    from_far(1, 1)

    def arrived(n):
        for m in range(4):
            for o in (0, 1):
                gg = base[o] + hop[m] + 1 - 2 * c
                for k in (0, 1) if m == 3 else (0,):
                    ref = piece(n, gg, k) if m == 3 else whole(n, gg)
                    remote(ref, ref, b_s.at[n, m, o, k], b_r.at[n, m, o, k], sibling).wait_recv()
        keeps[n].wait()

    def block(b, k):
        return sg_ref[b, k].reshape(256, 256)

    eye = iota((256, 256), 1) == iota((256, 256), 0)
    inverse = {}

    def diagonal(j):
        b = WHERE[(j, j)]
        ir, ii = recip(
            jnp.sum(jnp.where(eye, block(b, 0), 0.0), axis=1, keepdims=True),
            jnp.sum(jnp.where(eye, block(b, 1), 0.0), axis=1, keepdims=True),
        )
        cols = slice(j * 256, j * 256 + 256)
        d0_ref[0:1, cols] = jnp.sum(jnp.where(eye, ir, 0.0), axis=0, keepdims=True)
        d0_ref[1:2, cols] = jnp.sum(jnp.where(eye, ii, 0.0), axis=0, keepdims=True)
        inverse[j] = ir, ii

    def scale_block(j, other):
        rows = slice(j * 256, j * 256 + 256)
        low = slice(R + j * 256, R + j * 256 + 256)
        cols = slice(other * 256, other * 256 + 256)
        if (j, other) in WHERE:
            b = WHERE[(j, other)]
            re, im = block(b, 0), block(b, 1)
        else:
            b = WHERE[(other, j)]
            re, im = block(b, 0).T, block(b, 1).T
        ir, ii = inverse[j]
        er, ei = rotate(re, im, -ir, -ii)
        for where, value in ((rows, er), (low, ei)):
            if j == other:
                value = jnp.where(eye, 0.0, value)
            high, rest = split(value)
            shl_ref[0, where, cols] = high
            shl_ref[1, where, cols] = rest

    early = ((0, 0), (0, 1), (0, 3), (1, 0), (1, 1))
    arrived(0)
    diagonal(0)
    diagonal(1)
    for pair in early:
        scale_block(*pair)
    arrived(1)
    diagonal(2)
    diagonal(3)
    for j in range(4):
        for other in range(4):
            if (j, other) not in early:
                scale_block(j, other)
    times(lhs, shl_ref, u_ref, w_ref[0], w_ref[1], R)
    u_ref[0, 0:64, :] += w_ref[0]
    u_ref[1, 0:64, :] += w_ref[1]
    for j in range(4):
        at = pl.multiple_of(j * 256 + g * 16, 16)
        low = pl.multiple_of(j * 256 + g * 16 + R, 16)
        on = iota((16, R), 1) == iota((16, R), 0) + at
        rows = slice(64 + j * 16, 80 + j * 16)
        er = shl_ref[0, pl.ds(at, 16), :].astype(F32) + shl_ref[1, pl.ds(at, 16), :].astype(F32)
        ei = shl_ref[0, pl.ds(low, 16), :].astype(F32) + shl_ref[1, pl.ds(low, 16), :].astype(F32)
        u_ref[0, rows, :] = jnp.where(on, 1.0, er)
        u_ref[1, rows, :] = ei
    times(lhs, shl_ref, t_ref, u_ref[0], u_ref[1], R)
    times(lhs, shl_ref, t_ref, t_ref[0, 0:64], t_ref[1, 0:64], R)
    yr, yi = rotate(
        u_ref[0, 0:64] + t_ref[0, 0:64], u_ref[1, 0:64] + t_ref[1, 0:64], d0_ref[0:1, :], d0_ref[1:2, :]
    )
    u_ref[0, 0:64, :] = yr
    u_ref[1, 0:64, :] = yi
    weighted = -(wr * yr - wi * yi)
    for j in range(4):
        cols = slice(j * 256, j * 256 + 256)
        m = jnp.where(iota((64, 1), 0) < 32, pattern_at(j, 0), pattern_at(j, 1))
        side = weighted[:, cols] * m
        fw_ref[:, cols] = side
        turned = side.T.reshape(16, 2, 8, 64)
        ft_ref[j] = jnp.concatenate([turned[:, 0], turned[:, 1]], axis=2)

    for d, gg in enumerate(grids):
        go(remote(ft_ref.at[:, gg], ea_ref.at[g], a_s.at[d], a_r.at[d], (p, gg)))
    keep = pltpu.make_async_copy(ft_ref.at[:, g], ea_ref.at[g], keep_sem)
    keep.start()
    sent = []

    def send_or_keep(src, dst, ss, rs, target, here):
        away = remote(src, dst, ss, rs, target)
        stay = pltpu.make_async_copy(src, dst, ss)

        @pl.when(jnp.logical_not(here))
        def _():
            away.start()

        @pl.when(here)
        def _():
            stay.start()

        sent.append((here, away, stay))

    def child_rows():
        for jj in (0, 1):
            for cc in (0, 1):
                here = jnp.logical_and(p == 2 * c + jj, c == cc)
                rows = pl.ds(jj * 32 + cc * 16, 16)
                send_or_keep(
                    dw_ref.at[rows, :], rd_ref.at[p], sd_s.at[jj, cc], sd_r.at[p], (2 * c + jj, 2 * q + cc), here
                )

    for jj in (0, 1):
        for cc in (0, 1):
            send_or_keep(
                fw_ref.at[pl.ds(jj * 32 + cc * 16, 16), :], rf_ref.at[x, jj], sf_s.at[jj, cc], sf_r.at[x, jj],
                (2 * c + yl, 2 * q + cc), jnp.logical_and(x == c, c == cc),
            )

    times(lhs, shl_ref, t_ref, t_ref[0, 64:128], t_ref[1, 64:128], R)
    gr, gi = rotate(
        u_ref[0, 64:128] + t_ref[0, 0:64], u_ref[1, 64:128] + t_ref[1, 0:64], d0_ref[0:1, :], d0_ref[1:2, :]
    )
    gw_ref[...] = wr * gr - wi * gi
    for j in range(4):
        xx = 2 + j // 2
        send_or_keep(
            gw_ref.at[pl.ds(j * 16, 16), :], rf_ref.at[x, j % 2], sg_s.at[j], sf_r.at[x, j % 2], (2 * xx + yl, g), x == xx
        )

    keep.wait()
    for d in range(15):
        gg = lax.rem(g + 15 - d, 16)
        remote(ea_ref.at[gg], ea_ref.at[gg], a_s.at[d], a_r.at[d], (p, grids[0])).wait_recv()
    for j in range(4):
        send_or_keep(ea_ref.at[:, j], re_ref.at[p], se_s.at[j], se_r.at[p], (4 + j, g), p == 4 + j)

    yr, yi = u_ref[0, 0:64, :], u_ref[1, 0:64, :]
    rh, rl = split(yr)
    ih, il = split(yi)
    for at, (re, im) in enumerate(((rh, ih), (rl, il))):
        lhs[at * 128 : at * 128 + 64, 0:R] = re
        lhs[at * 128 + 64 : at * 128 + 128, 0:R] = im
        lhs[at * 128 : at * 128 + 64, R : 2 * R] = -im
        lhs[at * 128 + 64 : at * 128 + 128, R : 2 * R] = re
    wide = dot(lhs[0:256, 0:R], bhl_ref[0, :, 0:C]) + dot(lhs[0:256, R : 2 * R], bhl_ref[0, :, C : 2 * C])
    narrow = dot(lhs[0:128, 0:R], bhl_ref[1, :, 0:C]) + dot(lhs[0:128, R : 2 * R], bhl_ref[1, :, C : 2 * C])
    pr, pi = fold(wide, narrow, 64)

    times(lhs, ehl_ref, k_ref, pr, pi, C)
    ku_ref[0] = k_ref[0] + pr
    ku_ref[1] = k_ref[1] + pi
    times(lhs, ehl_ref, k_ref, ku_ref[0], ku_ref[1], C)
    times(lhs, ehl_ref, k_ref, k_ref[0], k_ref[1], C)
    zr, zi = rotate(ku_ref[0] + k_ref[0], ku_ref[1] + k_ref[1], dinv_ref[0:1, :], dinv_ref[1:2, :])
    dw_ref[...] = wr * (xc_ref[0] + zr) - wi * (xc_ref[1] + zi)
    child_rows()

    for here, away, stay in sent:

        @pl.when(here)
        def _():
            stay.wait()

    lead = p >= 4
    same = jnp.logical_or(lead, c == half(p))
    for d in range(4):
        xx = mod4(x + d)

        @pl.when(jnp.logical_or(jnp.logical_not(same), d > 0))
        def _():
            for n in (0, 1):
                remote(rf_ref.at[xx, n], rf_ref.at[xx, n], sf_s.at[0, 0], sf_r.at[xx, n], partner).wait_recv()

    pre_ref[...] = rf_ref[0, 1 - yl] + rf_ref[1, 1 - yl] + rf_ref[2, 1 - yl] + rf_ref[3, 1 - yl]
    cross = remote(pre_ref, pin_ref, pre_s, pre_r, partner)
    go(cross)
    for d in range(8):
        pp = poles[d]

        @pl.when(jnp.logical_and(jnp.logical_not(lead), jnp.logical_or(jnp.logical_not(same), d > 0)))
        def _():
            remote(rd_ref.at[pp], rd_ref.at[pp], sd_s.at[0, 0], sd_r.at[pp], partner).wait_recv()

    def total(ref):
        value = ref[0]
        for n in range(1, 8):
            value = value + ref[n]
        return value

    @pl.when(lead)
    def _():
        for d in range(1, 8):
            pp = poles[d]
            remote(re_ref.at[pp], re_ref.at[pp], se_s.at[0], se_r.at[pp], partner).wait_recv()
        side = total(re_ref)
        for k in (0, 1):
            for jj in (0, 1):
                at = k * 512 + jj * 256
                for top_half in (0, 1):
                    lane = top_half * 64 + jj * 32
                    cols = [side[2 * qq + k][:, lane : lane + 32] for qq in range(8)]
                    left_ref[top_half * 8 : top_half * 8 + 8, at : at + 256] = jnp.concatenate(cols, axis=1)

    @pl.when(jnp.logical_not(lead))
    def _():
        diag = total(rd_ref)
        upper = p < 2
        left_ref[:, 0:C] = jnp.where(upper, diag, 0.0)
        left_ref[:, C : 2 * C] = jnp.where(upper, 0.0, diag)

    main = rf_ref[0, yl] + rf_ref[1, yl] + rf_ref[2, yl] + rf_ref[3, yl]
    cross.wait_recv()
    right_ref[...] = main + pin_ref[...]

    for here, away, stay in sent:

        @pl.when(jnp.logical_not(here))
        def _():
            away.wait_send()

    for copy in pending:
        copy.wait_send()

    for when, here, away, opposite in gifts:

        @pl.when(when)
        def _():
            for copy in away + opposite:
                copy.wait_send()

    @pl.when(root)
    def _():
        for copy in top_y + top_x + top_x2:
            copy.wait_send()


GROUPS_DS = tuple(pl.ds(blocks.start, blocks.stop - blocks.start) for blocks in GROUPS)


def local(hamiltonian, margin, pattern, shift_real, shift_imag, residue):
    dma = pltpu.SemaphoreType.DMA
    vm = pltpu.VMEM
    left, right = pl.pallas_call(
        kernel,
        name="selected_inversion",
        out_shape=(jax.ShapeDtypeStruct((16, R), F32), jax.ShapeDtypeStruct((16, R), F32)),
        in_specs=[ANY, ANY, SM, SM, SM, SM],
        out_specs=(VM, VM),
        scratch_shapes=[
            vm((2, 16, 2 * R), F32), vm((2, 1536, 512), F32), vm((2, 64, 1024), F32), vm((2, 1024, C), BF16), vm((2, R, 2 * C), BF16),
            vm((8, C), F32), vm((768, 2 * R), BF16), vm((2, 192, C), F32), vm((2, 192, C), F32),
            vm((2, 64, C), F32), vm((2, 64, R), F32), vm((2, NB, 2, 16, 256), F32),
            vm((NB, 2, 16, 256), F32), vm((NB, 2, 16, 256), F32), vm((NB, 2, 16, 16, 256), F32),
            vm((2, 2 * R, R), BF16), vm((8, R), F32), vm((2, 128, R), F32), vm((2, 128, R), F32),
            vm((2, 64, C), F32), vm((2, 64, C), F32), vm((64, R), F32), vm((4, 16, 8, 128), F32),
            vm((64, R), F32), vm((64, C), F32),
            vm((4, 2, 16, R), F32), vm((8, 16, C), F32), vm((8, 16, 8, 128), F32), vm((16, 4, 8, 128), F32),
            vm((16, R), F32), vm((16, R), F32),
            dma((5,)), dma((4, 2)), dma((3, 2)),
            dma((2, 3)), dma((2, 3)), dma((3, 2)), dma((3, 2)),
            dma((2, 3, 4)), dma((2, 3, 4)), dma((3, 4, 2)), dma((3, 4, 2)),
            dma((2,)), dma((2,)), dma((3, 2, 2)), dma((2, 2, 2)),
            dma((2,)), dma((2,)), dma((2,)), dma((2,)), dma((2,)), dma((4, 2)), dma((4, 2)),
            dma((2, 2, 2)), dma((2, 2, 2)), dma((2, 2, 2)), dma((2, 2, 2)),
            dma((2, 4, 2, 2)), dma((2, 4, 2, 2)),
            dma, dma, dma, dma((15,)), dma((15,)), dma((2, 2)), dma((4, 2)), dma((2, 2)), dma((8,)),
            dma((4,)), dma((4,)), dma((8,)),
        ],
        compiler_params=pltpu.CompilerParams(
            collective_id=0, has_side_effects=True, vmem_limit_bytes=56 << 20
        ),
        cost_estimate=pl.CostEstimate(flops=12 << 30, bytes_accessed=1 << 20, transcendentals=0),
    )(hamiltonian, margin, pattern, shift_real, shift_imag, residue)
    return jnp.concatenate([left, right], axis=1)


def solution(mesh):
    return jax.shard_map(
        local,
        mesh=mesh,
        in_specs=(
            P(("pole", "grid"), None),
            P(("pole", "grid"), None),
            P(),
            P("pole"),
            P("pole"),
            P("pole", None),
        ),
        out_specs=P(("pole", "grid"), None),
        check_vma=False,
    )
```
